32 devices in a mesh: item: 4 (over y, x), seq: 8 (over z, core).
Axes of the slice: x: 2, y: 2, z: 4, core: 2. Of those that a mesh axis runs over, the one named last changes fastest.
Arguments:
- tokens: bfloat16 [4, 1024, 768], P('item', 'seq'), may hold values from -6 to 6
- rand_blocks: int32 [16, 4, 12, 3], P(None, 'item'), may hold values from 0 to 15, all different within a row; in each aligned block of 12 rows (0 to 11, 12 to 23, ..., all dimensions but the last counted through in order) at most 3 rows name the same one
- w_query: bfloat16 [768, 768], replicated, may hold values from -0.21875 to 0.21875
- w_key: bfloat16 [768, 768], replicated, may hold values from -0.21875 to 0.21875
- w_value: bfloat16 [768, 768], replicated, may hold values from -0.21875 to 0.21875
- w_out: bfloat16 [768, 768], replicated, may hold values from -0.875 to 0.875
- w_up: bfloat16 [768, 3072], replicated, may hold values from -0.21875 to 0.21875
- w_down: bfloat16 [3072, 768], replicated, may hold values from -0.109375 to 0.109375
- bias_query: float32 [768], replicated, may hold values from -3 to 3
- bias_value: float32 [768], replicated, may hold values from -3 to 3
- bias_out: float32 [768], replicated, may hold values from -3 to 3
- bias_up: float32 [3072], replicated, may hold values from -3 to 3
- bias_down: float32 [768], replicated, may hold values from -3 to 3
- attn_gain: float32 [768], replicated, may hold values from 0.5 to 1.5
- attn_shift: float32 [768], replicated, may hold values from -2 to 2
- ffn_gain: float32 [768], replicated, may hold values from 0.5 to 1.5
- ffn_shift: float32 [768], replicated, may hold values from -2 to 2
- cotangent: bfloat16 [4, 1024, 768], P('item', 'seq'), may hold values from -6 to 6
Outputs:
- layer_out: bfloat16 [4, 1024, 768], P('item', 'seq')
- grad_tokens: bfloat16 [4, 1024, 768], P('item', 'seq')
- grad_w_query: float32 [768, 768], replicated
- grad_w_key: float32 [768, 768], replicated
- grad_w_value: float32 [768, 768], replicated
- grad_w_out: float32 [768, 768], replicated
- grad_w_up: float32 [768, 3072], replicated
- grad_w_down: float32 [3072, 768], replicated
- grad_bias_query: float32 [768], replicated
- grad_bias_value: float32 [768], replicated
- grad_bias_out: float32 [768], replicated
- grad_bias_up: float32 [3072], replicated
- grad_bias_down: float32 [768], replicated
- grad_attn_gain: float32 [768], replicated
- grad_attn_shift: float32 [768], replicated
- grad_ffn_gain: float32 [768], replicated
- grad_ffn_shift: float32 [768], replicated
The draws below stay inside these ranges and needn't reach their ends.
Inputs may be any that keep to these rules, and one draw needn't show every extreme that they name: Each row rand_blocks[j, t, h, :] names 3 different key blocks. Among the rows of one query block of the 1 sequence of one index of item (all heads together), no key block is named more than 3 times, and in some such group one key block is named exactly 3 times.
All inputs are finite; a program needn't handle non-finite values.
Results may differ from the reference program's by a relative error of at most 0.015.
Values may be sent and summed in bfloat16 or wider, within the bound.
No kernel may reach another device: no remote copies, remote signals or barrier semaphores. Data moves between devices by JAX's collectives and lax.ppermute only.
A program may use at most 448 MiB of HBM per device.

```python
import math
import jax
import jax.numpy as jnp
import numpy as np
from jax import lax

D = 768
HEADS = 12
HD = 64
FF = 3072
BLOCK = 64
RAND = 3
NBLK = 16
LEN = 1024
SEQS = 1
SEQTOT = 4
MOST = 3


def level_of(stream_key, shape, shards, least, high):
    level = 1.0
    for position, shards_of in shards:
        draws = jax.random.uniform(jax.random.fold_in(jax.random.fold_in(stream_key, 6), position), (shards_of,), jnp.float32, least / len(shards), high / len(shards))
        level = level * jnp.repeat(jnp.exp(draws), shape[position] // shards_of).reshape((-1,) + (1,) * (len(shape) - 1 - position))
    return level


def routed_block(own_key, own, number, rows, count, top, most, lean):
    sequence = jax.random.permutation(own_key, count)
    heavy_load, ordinary = shares(count, rows * top, most, lean, True), shares(count, rows * top, most, lean, False)
    places = jnp.arange(count)

    def named(tallies, turn):
        used = int((tallies > 0).sum())
        fixed = max(1, used // 4)
        passed = fixed + (places - fixed + turn * (used - fixed)) % max(1, count - fixed)
        return jnp.zeros((count,), jnp.int32).at[sequence[jnp.where(places < fixed, places, passed)]].set(jnp.asarray(tallies, jnp.int32))

    tallies = jnp.where(number % 4 == 0, named(heavy_load, number // 4), named(ordinary, number - number // 4 - 1))
    mixed = jax.random.permutation(jax.random.fold_in(own, 3), count)
    donor, receiver = mixed[0:count // 2 * 2:2], mixed[1:count // 2 * 2:2]
    margin = jnp.minimum(tallies[donor] - 1, most - tallies[receiver]) // 2
    margin = jnp.where((donor == sequence[0]) | (receiver == sequence[0]) | (tallies[receiver] == 0), 0, jnp.maximum(margin, 0))
    passed = jax.random.randint(jax.random.fold_in(own, 4), (count // 2,), 0, 1 << 20) % (margin + 1)
    tallies = tallies.at[donor].add(-passed).at[receiver].add(passed)
    labels = jnp.searchsorted(jnp.cumsum(tallies), jnp.arange(rows * top), side="right").astype(jnp.int32)
    listing = labels.reshape(top, rows).T
    listing = listing[jax.random.permutation(jax.random.fold_in(own, 1), rows)]
    turn = jax.random.randint(jax.random.fold_in(own, 2), (rows, 1), 0, top)
    return jnp.take_along_axis(listing, (jnp.arange(top)[None, :] + turn) % top, axis=1)


def shares(amount, total, reach, lean, full):
    portions = [(1 << 20) // math.isqrt(rank ** lean) + 1 for rank in range(1, amount + 1)]
    largest = reach if full else min(reach, max(-(-total // amount), total * portions[0] // sum(portions)))
    least = 1 if total - largest >= amount - 1 else 0
    holding, spare = [largest] + [least] * (amount - 1), total - largest - least * (amount - 1)
    while spare > 0:
        free = [i for i in range(1, amount) if holding[i] < largest] or [i for i in range(1, amount) if holding[i] < reach]
        mass, remaining = sum([portions[i] for i in free]), spare
        for i in free:
            addition = min(reach - holding[i], max(1, remaining * portions[i] // mass), spare)
            holding[i] = holding[i] + addition
            spare = spare - addition
    return np.array(holding)


def centred(rng, dims, width, limit, cuts=(), kind=jnp.bfloat16):
    array = jax.random.normal(rng, dims, jnp.float32) * width
    if len(cuts) > 0:
        array = level_of(rng, dims, cuts, -0.22, 0.18) * array
    return jnp.clip(array, min=-limit, max=limit).astype(kind)


def setup_inputs(seed: int = 0) -> dict:
    seeds = jax.random.split(jax.random.key(seed), 19)
    tokens = centred(seeds[0], (SEQTOT, LEN, D), 1.0, 6.0, ((0, 4), (1, 8)))
    rand_blocks_keys = jax.random.split(jax.random.fold_in(seeds[1], 1), NBLK * SEQTOT * HEADS // (SEQS * HEADS))
    rand_blocks_turns = jax.random.permutation(jax.random.fold_in(seeds[1], 3), NBLK * SEQTOT * HEADS // (SEQS * HEADS))
    rand_blocks = jax.vmap(lambda own, number: routed_block(jax.random.fold_in(seeds[1], 2), own, number, SEQS * HEADS, NBLK, RAND, MOST, 2))(rand_blocks_keys, rand_blocks_turns).reshape((NBLK, SEQTOT, HEADS, RAND))
    w_query = centred(seeds[2], (D, D), D ** -0.5, 0.21875)
    w_key = centred(seeds[3], (D, D), D ** -0.5, 0.21875)
    w_value = centred(seeds[4], (D, D), D ** -0.5, 0.21875)
    w_out = centred(seeds[5], (D, D), (D // 16) ** -0.5, 0.875)
    w_up = centred(seeds[6], (D, FF), D ** -0.5, 0.21875)
    w_down = centred(seeds[7], (FF, D), FF ** -0.5, 0.109375)
    bias_query = centred(seeds[8], (D,), 0.5, 3.0, (), jnp.float32)
    bias_value = centred(seeds[9], (D,), 0.5, 3.0, (), jnp.float32)
    bias_out = centred(seeds[10], (D,), 0.5, 3.0, (), jnp.float32)
    bias_up = centred(seeds[11], (FF,), 0.5, 3.0, (), jnp.float32)
    bias_down = centred(seeds[12], (D,), 0.5, 3.0, (), jnp.float32)
    attn_gain = jnp.clip(1.0 + 0.1 * jax.random.normal(seeds[13], (D,), jnp.float32), 0.5, 1.5)
    attn_shift = centred(seeds[14], (D,), 0.3, 2.0, (), jnp.float32)
    ffn_gain = jnp.clip(1.0 + 0.1 * jax.random.normal(seeds[15], (D,), jnp.float32), 0.5, 1.5)
    ffn_shift = centred(seeds[16], (D,), 0.3, 2.0, (), jnp.float32)
    cotangent = centred(seeds[17], (SEQTOT, LEN, D), 1.0, 6.0, ((0, 4), (1, 8)))
    return dict(tokens=tokens, rand_blocks=rand_blocks, w_query=w_query, w_key=w_key, w_value=w_value, w_out=w_out, w_up=w_up, w_down=w_down, bias_query=bias_query, bias_value=bias_value, bias_out=bias_out, bias_up=bias_up, bias_down=bias_down, attn_gain=attn_gain, attn_shift=attn_shift, ffn_gain=ffn_gain, ffn_shift=ffn_shift, cotangent=cotangent)


@jax.custom_vjp
def low(v):
    return lax.optimization_barrier(v.astype(jnp.bfloat16)).astype(jnp.float32)

@jax.custom_vjp
def low_back(v):
    return v

def low_keep(v):
    return (low(v), None)

def low_pass(kept, grad):
    return (grad,)

def back_keep(v):
    return (v, None)

def back_low(kept, grad):
    return (low(grad),)
low.defvjp(low_keep, low_pass)
low_back.defvjp(back_keep, back_low)
epsilon = 1e-05

def matmul(left, right):
    return jnp.dot(left, right, precision=lax.Precision.HIGHEST)

def product(form, left, right):
    return jnp.einsum(form, left, right, precision=lax.Precision.HIGHEST)

def layer_norm(values, norm_gain, norm_bias):
    center = values - lax.optimization_barrier(jnp.mean(values, axis=-1, keepdims=True))
    spread = lax.optimization_barrier(jnp.mean(center * center, axis=-1, keepdims=True))
    return center * lax.rsqrt(spread + epsilon) * norm_gain + norm_bias

def head_attention(operands):
    queries, key_blocks, values, chosen = operands
    score_scale = HD ** (-0.5)
    inner_ids = jnp.arange(1, NBLK - 1, dtype=jnp.int32)
    fixed_blocks = jnp.stack([inner_ids - 1, inner_ids, inner_ids + 1, jnp.zeros_like(inner_ids), jnp.full_like(inner_ids, NBLK - 1)], axis=1)
    picked = jnp.concatenate([fixed_blocks, chosen[1:NBLK - 1].astype(jnp.int32)], axis=1)
    near_keys = key_blocks[picked].reshape(NBLK - 2, (5 + RAND) * BLOCK, HD)
    near_values = values[picked].reshape(NBLK - 2, (5 + RAND) * BLOCK, HD)
    scores = low_back(product('nqd,nkd->nqk', queries[1:NBLK - 1], near_keys) * score_scale)
    row_peak = lax.optimization_barrier(jnp.max(scores, axis=-1, keepdims=True))
    weights = jnp.exp(scores - row_peak)
    row_total = lax.optimization_barrier(jnp.sum(weights, axis=-1, keepdims=True))
    middle = product('nqk,nkd->nqd', low(weights), near_values) / row_total
    global_queries = jnp.stack([queries[0], queries[NBLK - 1]])
    global_scores = low_back(product('gqd,nkd->gqnk', global_queries, key_blocks) * score_scale)
    block_peak = lax.optimization_barrier(jnp.max(global_scores, axis=-1, keepdims=True))
    global_weights = jnp.exp(global_scores - block_peak)
    top_peak = lax.optimization_barrier(jnp.max(block_peak, axis=2, keepdims=True))
    factor = jnp.exp(block_peak - top_peak)
    global_total = lax.optimization_barrier(jnp.sum(factor * lax.optimization_barrier(jnp.sum(global_weights, axis=-1, keepdims=True)), axis=2))
    global_sum = lax.optimization_barrier(jnp.sum(factor * product('gqnk,nkd->gqnd', low(global_weights), values), axis=2))
    global_out = global_sum / global_total
    return jnp.concatenate([global_out[0:1], middle, global_out[1:2]], axis=0)

def to_heads(values):
    return values.reshape(NBLK, BLOCK, HEADS, HD).transpose(2, 0, 1, 3)

def layer_forward(inputs, params, chosen):
    w_query, w_key, w_value, w_out, w_up, w_down, bias_query, bias_value, bias_out, bias_up, bias_down, attn_gain, attn_shift, ffn_gain, ffn_shift = params
    normed = low(layer_norm(inputs, attn_gain, attn_shift))
    queries = low(low_back(matmul(normed, w_query) + bias_query))
    key_rows = low(low_back(matmul(normed, w_key)))
    value_rows = low(low_back(matmul(normed, w_value) + bias_value))
    context = lax.map(jax.checkpoint(head_attention), (to_heads(queries), to_heads(key_rows), to_heads(value_rows), chosen.transpose(1, 0, 2)))
    context = low(low_back(context.transpose(1, 2, 0, 3).reshape(LEN, D)))
    middle = inputs + low_back(matmul(context, w_out) + bias_out)
    normed_two = low(layer_norm(middle, ffn_gain, ffn_shift))
    hidden = low_back(matmul(normed_two, w_up) + bias_up)
    active = low(jax.nn.gelu(hidden, approximate=False))
    return middle + matmul(active, w_down) + bias_down

def reference(tokens, rand_blocks, w_query, w_key, w_value, w_out, w_up, w_down, bias_query, bias_value, bias_out, bias_up, bias_down, attn_gain, attn_shift, ffn_gain, ffn_shift, cotangent):
    raw_params = (w_query, w_key, w_value, w_out, w_up, w_down, bias_query, bias_value, bias_out, bias_up, bias_down, attn_gain, attn_shift, ffn_gain, ffn_shift)
    params = tuple((member.astype(jnp.float32) for member in raw_params))
    seq_blocks_all = rand_blocks.transpose(1, 0, 2, 3)

    def one_sequence(summed, pieces):
        seq_tokens, seq_blocks, seq_cot = pieces

        def forward(seq_inputs, seq_params):
            return layer_forward(seq_inputs, seq_params, seq_blocks)
        seq_out, pullback = jax.vjp(forward, seq_tokens.astype(jnp.float32), params)
        grad_inputs, grad_params = pullback(seq_cot.astype(jnp.float32))
        summed = jax.tree.map(jnp.add, summed, grad_params)
        return (summed, (seq_out.astype(jnp.bfloat16), grad_inputs.astype(jnp.bfloat16)))
    initial = jax.tree.map(jnp.zeros_like, params)
    summed, (outputs, grad_tokens) = lax.scan(one_sequence, initial, (tokens, seq_blocks_all, cotangent))
    return (outputs, grad_tokens, summed[0], summed[1], summed[2], summed[3], summed[4], summed[5], summed[6], summed[7], summed[8], summed[9], summed[10], summed[11], summed[12], summed[13], summed[14])
```

```python
import functools

import jax
import jax.numpy as jnp
from jax import lax
from jax.experimental import pallas as pl
from jax.experimental.pallas import tpu as pltpu
from jax.sharding import PartitionSpec as P

HEADS = 12
HD = 64
BLOCK = 64
RAND = 3


epsilon = 1e-05


def from_root(shard, axis, root):
    mine = lax.axis_index(axis) == root
    return lax.psum(jnp.where(mine, shard, jnp.zeros_like(shard)), axis)


def extended(block, sides, width):
    for axis, dim in sides:
        count = lax.axis_size(axis)
        forward = [(i, i + 1) for i in range(count - 1)]
        backward = [(target, source) for source, target in forward]
        low = lax.ppermute(
            lax.slice_in_dim(block, block.shape[dim] - width, None, axis=dim), axis, forward
        )
        high = lax.ppermute(lax.slice_in_dim(block, 0, width, axis=dim), axis, backward)
        block = jnp.concatenate([low, block, high], axis=dim)
    return block


def joined(shard, axis, join):
    gathered = jax.tree.map(
        lambda a, kind: lax.all_gather(a.astype(kind), axis),
        shard,
        (jnp.bfloat16, jnp.bfloat16, jnp.bfloat16),
    )

    def take(source):
        return jax.tree.map(
            lambda a, own: lax.dynamic_index_in_dim(a, source, 0, False).astype(own.dtype),
            gathered,
            shard,
        )

    return lax.fori_loop(
        1, lax.axis_size(axis), lambda source, state: join(state, take(source)), take(0)
    )


def entering(shard, axis, combine, identity, reverse):
    count, position = (lax.axis_size(axis), lax.axis_index(axis))
    everything = jax.tree.map(
        lambda part, kind: lax.all_gather(part.astype(kind), axis),
        shard,
        jax.tree.map(lambda a: jnp.bfloat16 if a.dtype == jnp.float32 else a.dtype, shard),
    )
    start = jax.tree.map(
        lambda part, zero: jnp.broadcast_to(jnp.asarray(zero, part.dtype), part.shape),
        shard,
        identity,
    )

    def step(k, before):
        at = count - 1 - k if reverse else k
        reached = at > position if reverse else at < position
        new = combine(
            before, jax.tree.map(lambda part, own: part[at].astype(own.dtype), everything, shard)
        )
        return jax.tree.map(lambda a, b: jnp.where(reached, a, b), new, before)

    return lax.fori_loop(0, count, step, start)


def layer_norm(values, norm_gain, norm_bias):
    center = values - jnp.mean(values, axis=-1, keepdims=True)
    spread = jnp.mean(center * center, axis=-1, keepdims=True)
    return center * lax.rsqrt(spread + epsilon) * norm_gain + norm_bias


def gelu_exact(values):
    return jax.nn.gelu(values, approximate=False)


def dense_rows(left, right):
    return jnp.dot(left, right, preferred_element_type=jnp.float32)


def dense_left(left, right):
    return lax.dot_general(
        left, right, (((0,), (0,)), ((), ())), preferred_element_type=jnp.float32
    )


def dense_back(left, right):
    return lax.dot_general(
        left, right, (((1,), (1,)), ((), ())), preferred_element_type=jnp.float32
    )


def mixed_sum(form, left, right):
    return jnp.einsum(form, left, right, preferred_element_type=jnp.float32)


def exact_sum(form, left, right):
    return jnp.einsum(
        form, left, right, precision=lax.Precision.HIGHEST, preferred_element_type=jnp.float32
    )


def from_ends(first_part, last_part):
    head_part = from_root(first_part, "seq", 0)
    tail_part = from_root(last_part, "seq", lax.axis_size("seq") - 1)
    return (head_part, tail_part)


def merge_rows(left_part, right_part):
    left_peak, left_total, left_sum = left_part
    right_peak, right_total, right_sum = right_part
    new_peak = jnp.maximum(left_peak, right_peak)
    left_scale = jnp.exp(left_peak - new_peak)
    right_scale = jnp.exp(right_peak - new_peak)
    return (
        new_peak,
        left_total * left_scale + right_total * right_scale,
        left_sum * left_scale[..., None] + right_sum * right_scale[..., None],
    )


def add_pair(earlier_sum, later_sum):
    return (earlier_sum[0] + later_sum[0], earlier_sum[1] + later_sum[1])


def general_device(
    tokens,
    rand_blocks,
    w_query,
    w_key,
    w_value,
    w_out,
    w_up,
    w_down,
    bias_query,
    bias_value,
    bias_out,
    bias_up,
    bias_down,
    attn_gain,
    attn_shift,
    ffn_gain,
    ffn_shift,
    cotangent,
):
    seq_here, local_len, model_width = tokens.shape
    blocks_all = rand_blocks.shape[0]
    devices = lax.axis_size("seq")
    position = lax.axis_index("seq")
    per_dev = blocks_all // devices
    slot_cap = max(2, seq_here * HEADS * RAND * 4 // (3 * blocks_all))
    pair_width = 2 * HD
    lane_count = seq_here * HEADS * RAND
    slot_size = BLOCK * pair_width
    rows_here = seq_here * local_len
    score_scale = HD ** (-0.5)

    def to_heads(values):
        return values.reshape(seq_here, per_dev, BLOCK, HEADS, -1).transpose(0, 1, 3, 2, 4)

    def from_heads(values):
        return values.transpose(0, 1, 3, 2, 4).reshape(rows_here, -1)

    inputs = tokens.reshape(rows_here, model_width).astype(jnp.float32)
    normed = layer_norm(inputs, attn_gain, attn_shift).astype(jnp.bfloat16)
    queries = (dense_rows(normed, w_query) + bias_query).astype(jnp.bfloat16)
    key_rows = dense_rows(normed, w_key).astype(jnp.bfloat16)
    value_rows = (dense_rows(normed, w_value) + bias_value).astype(jnp.bfloat16)
    kv_tokens = jnp.stack(
        [
            key_rows.reshape(seq_here, local_len, HEADS, HD),
            value_rows.reshape(seq_here, local_len, HEADS, HD),
        ],
        axis=3,
    ).reshape(seq_here, local_len, 2 * model_width)
    padded = extended(kv_tokens, (("seq", 1),), BLOCK)
    pad_blocks = padded.reshape(seq_here, per_dev + 2, BLOCK, HEADS, pair_width)
    window = jnp.stack(
        [pad_blocks[:, 0:per_dev], pad_blocks[:, 1 : per_dev + 1], pad_blocks[:, 2 : per_dev + 2]],
        axis=2,
    )
    window = window.transpose(0, 1, 4, 2, 3, 5).reshape(
        seq_here, per_dev, HEADS, 3 * BLOCK, pair_width
    )
    packed = jnp.concatenate([queries.reshape(seq_here, local_len, model_width), kv_tokens], axis=2)
    head_pack, tail_pack = from_ends(packed[:, :BLOCK], packed[:, local_len - BLOCK :])
    global_pack = jnp.stack([head_pack, tail_pack], axis=1)
    global_query = (
        global_pack[..., :model_width]
        .reshape(seq_here, 2, BLOCK, HEADS, HD)
        .transpose(0, 3, 1, 2, 4)
        .reshape(seq_here, HEADS, 2 * BLOCK, HD)
    )
    global_kv = (
        global_pack[..., model_width:]
        .reshape(seq_here, 2, BLOCK, HEADS, pair_width)
        .transpose(0, 3, 1, 2, 4)
        .reshape(seq_here, HEADS, 2 * BLOCK, pair_width)
    )
    flat_req = rand_blocks.reshape(blocks_all, lane_count)
    block_ids = jnp.arange(blocks_all, dtype=jnp.int32)
    live_rows = (block_ids != 0) & (block_ids != blocks_all - 1)
    own_blocks = position * per_dev + jnp.arange(per_dev, dtype=jnp.int32)
    matches = (
        (flat_req[:, :, None] == own_blocks[None, None, :]) & live_rows[:, None, None]
    ).astype(jnp.int32)
    order_rank = jnp.cumsum(matches, axis=1) - matches
    slot_ids = jnp.arange(slot_cap, dtype=jnp.int32)
    chosen = matches[..., None] * (order_rank[..., None] == slot_ids).astype(jnp.int32)
    lane_ids = jnp.arange(lane_count, dtype=jnp.int32)
    source_rows = lane_ids // (HEADS * RAND) * (per_dev * HEADS) + lane_ids // RAND % HEADS
    slot_live = jnp.sum(chosen, axis=1)
    slot_rows = (
        jnp.sum(chosen * source_rows[None, :, None, None], axis=1)
        + (jnp.arange(per_dev, dtype=jnp.int32) * HEADS)[None, :, None]
    )
    kv_heads = (
        kv_tokens.reshape(seq_here, per_dev, BLOCK, HEADS, pair_width)
        .transpose(0, 1, 3, 2, 4)
        .reshape(seq_here * per_dev * HEADS, slot_size)
    )
    served = jnp.take(kv_heads, slot_rows.reshape(-1), axis=0) * slot_live.reshape(-1, 1).astype(
        jnp.bfloat16
    )
    served = served.reshape(devices, per_dev, per_dev, slot_cap, slot_size)
    replies = lax.all_to_all(served, "seq", split_axis=0, concat_axis=0, tiled=True)
    fetched = replies.transpose(1, 0, 2, 3, 4).reshape(per_dev * blocks_all * slot_cap, slot_size)
    my_blocks = lax.dynamic_slice_in_dim(flat_req, position * per_dev, per_dev, 0)
    same_key = (my_blocks[:, :, None] == my_blocks[:, None, :]) & (
        lane_ids[None, None, :] < lane_ids[None, :, None]
    )
    my_ranks = jnp.sum(same_key.astype(jnp.int32), axis=2)
    pick_rows = (
        jnp.arange(per_dev, dtype=jnp.int32)[:, None] * blocks_all + my_blocks
    ) * slot_cap + my_ranks
    rand_kv = jnp.take(fetched, pick_rows.reshape(-1), axis=0).reshape(
        per_dev, seq_here, HEADS, RAND, BLOCK, pair_width
    )
    rand_kv = rand_kv.transpose(1, 0, 2, 3, 4, 5).reshape(
        seq_here, per_dev, HEADS, RAND * BLOCK, pair_width
    )
    global_kv_all = jnp.broadcast_to(
        global_kv[:, None], (seq_here, per_dev, HEADS, 2 * BLOCK, pair_width)
    )
    keys_all = jnp.concatenate([window, global_kv_all, rand_kv], axis=3)
    list_keys = keys_all[..., :HD]
    list_values = keys_all[..., HD:]
    query_heads = to_heads(queries)
    scores = mixed_sum("sjhqd,sjhkd->sjhqk", query_heads, list_keys) * score_scale
    row_peak = jnp.max(scores, axis=-1, keepdims=True)
    weights = jnp.exp(scores - row_peak)
    row_total = jnp.sum(weights, axis=-1, keepdims=True)
    near_out = (
        mixed_sum("sjhqk,sjhkd->sjhqd", weights.astype(jnp.bfloat16), list_values) / row_total
    )
    local_heads = kv_tokens.reshape(seq_here, per_dev, BLOCK, HEADS, pair_width).transpose(
        0, 3, 1, 2, 4
    )
    local_keys = local_heads[..., :HD]
    local_values = local_heads[..., HD:]
    global_scores = mixed_sum("shqd,shjkd->shqjk", global_query, local_keys) * score_scale
    block_peak = jnp.max(global_scores, axis=-1, keepdims=True)
    global_weights = jnp.exp(global_scores - block_peak)
    local_top = jnp.max(block_peak, axis=3, keepdims=True)
    factor = jnp.exp(block_peak - local_top)
    local_total = jnp.sum(factor * jnp.sum(global_weights, axis=-1, keepdims=True), axis=(3, 4))
    local_sum = jnp.sum(
        factor * mixed_sum("shqjk,shjkd->shqjd", global_weights.astype(jnp.bfloat16), local_values),
        axis=3,
    )
    global_top, global_total, global_sum = joined(
        (local_top[..., 0, 0], local_total, local_sum), "seq", merge_rows
    )
    global_ctx = global_sum / global_total[..., None]
    global_lse = global_top + jnp.log(global_total)
    block_here = jnp.arange(per_dev, dtype=jnp.int32)
    head_mask = ((position == 0) & (block_here == 0))[None, :, None, None, None]
    tail_mask = ((position == devices - 1) & (block_here == per_dev - 1))[None, :, None, None, None]
    context = jnp.where(head_mask, global_ctx[:, None, :, :BLOCK], near_out)
    context = jnp.where(tail_mask, global_ctx[:, None, :, BLOCK:], context)
    context_rows = from_heads(context).astype(jnp.bfloat16)
    middle = inputs + (dense_rows(context_rows, w_out) + bias_out)
    normed_two = layer_norm(middle, ffn_gain, ffn_shift).astype(jnp.bfloat16)
    hidden = dense_rows(normed_two, w_up) + bias_up
    active = gelu_exact(hidden).astype(jnp.bfloat16)
    layer_out = (
        (middle + dense_rows(active, w_down) + bias_down)
        .astype(jnp.bfloat16)
        .reshape(seq_here, local_len, model_width)
    )
    cot_rows = cotangent.reshape(rows_here, model_width)
    cot_float = cot_rows.astype(jnp.float32)
    grad_w_down = dense_left(active, cot_rows)
    grad_bias_down = jnp.sum(cot_float, axis=0)
    d_active = dense_back(cot_rows, w_down)
    gelu_pull = jax.vjp(gelu_exact, hidden)[1]
    d_hidden = gelu_pull(d_active)[0].astype(jnp.bfloat16)
    grad_w_up = dense_left(normed_two, d_hidden)
    grad_bias_up = jnp.sum(d_hidden.astype(jnp.float32), axis=0)
    norm_pull_two = jax.vjp(layer_norm, middle, ffn_gain, ffn_shift)[1]
    d_middle_norm, grad_ffn_gain, grad_ffn_shift = norm_pull_two(dense_back(d_hidden, w_up))
    d_middle = cot_float + d_middle_norm
    d_attended = d_middle.astype(jnp.bfloat16)
    grad_w_out = dense_left(context_rows, d_attended)
    grad_bias_out = jnp.sum(d_attended.astype(jnp.float32), axis=0)
    d_context = dense_back(d_attended, w_out).astype(jnp.bfloat16)
    d_tokens = d_context.reshape(seq_here, local_len, model_width)
    head_grad, tail_grad = from_ends(d_tokens[:, :BLOCK], d_tokens[:, local_len - BLOCK :])
    d_heads = jnp.where(head_mask | tail_mask, jnp.zeros((), jnp.bfloat16), to_heads(d_context))
    d_float = d_heads.astype(jnp.float32)
    row_delta = jnp.sum(d_float * near_out, axis=-1, keepdims=True)
    scores = mixed_sum("sjhqd,sjhkd->sjhqk", query_heads, list_keys) * score_scale
    weights = jnp.exp(scores - row_peak)
    d_weights = mixed_sum("sjhqd,sjhkd->sjhqk", d_heads, list_values)
    d_scores = (weights / row_total * (d_weights - row_delta)).astype(jnp.bfloat16)
    d_query = mixed_sum("sjhqk,sjhkd->sjhqd", d_scores, list_keys) * score_scale
    d_list_keys = mixed_sum("sjhqk,sjhqd->sjhkd", d_scores, query_heads) * score_scale
    d_list_values = exact_sum(
        "sjhqk,sjhqd->sjhkd", weights.astype(jnp.bfloat16).astype(jnp.float32), d_float / row_total
    )
    d_kv = jnp.concatenate([d_list_keys, d_list_values], axis=-1)
    d_window = d_kv[:, :, :, : 3 * BLOCK].reshape(seq_here, per_dev, HEADS, 3, BLOCK, pair_width)
    keep_dims = ((0, 0), (0, 0), (0, 0))
    spread_sum = jnp.pad(d_window[:, :, :, 0], ((0, 0), (0, 2)) + keep_dims)
    spread_sum = spread_sum + jnp.pad(d_window[:, :, :, 1], ((0, 0), (1, 1)) + keep_dims)
    spread_sum = spread_sum + jnp.pad(d_window[:, :, :, 2], ((0, 0), (2, 0)) + keep_dims)
    own_grad = spread_sum[:, 1 : per_dev + 1]
    rim_grad = jnp.concatenate(
        [spread_sum[:, 0:1], spread_sum[:, per_dev + 1 : per_dev + 2]], axis=1
    )
    rim_grad = rim_grad.transpose(0, 1, 3, 2, 4).reshape(seq_here, 2 * BLOCK, 2 * model_width)
    back_rim = extended(rim_grad.astype(jnp.bfloat16), (("seq", 1),), BLOCK).astype(rim_grad.dtype)
    from_left = (
        back_rim[:, :BLOCK].reshape(seq_here, BLOCK, HEADS, pair_width).transpose(0, 2, 1, 3)
    )
    from_right = (
        back_rim[:, 3 * BLOCK :].reshape(seq_here, BLOCK, HEADS, pair_width).transpose(0, 2, 1, 3)
    )
    own_grad = own_grad.at[:, 0].add(from_left).at[:, per_dev - 1].add(from_right)
    global_part = jnp.sum(d_kv[:, :, :, 3 * BLOCK : 5 * BLOCK], axis=1)
    rand_part = d_kv[:, :, :, 5 * BLOCK :].reshape(seq_here, per_dev, HEADS, RAND, slot_size)
    rand_part = rand_part.transpose(1, 0, 2, 3, 4).reshape(per_dev * lane_count, slot_size)
    slot_grads = (
        jnp.zeros((per_dev * blocks_all * slot_cap, slot_size), jnp.float32)
        .at[pick_rows.reshape(-1)]
        .add(rand_part)
    )
    slot_grads = slot_grads.reshape(per_dev, devices, per_dev, slot_cap, slot_size).transpose(
        1, 0, 2, 3, 4
    )
    returned = lax.all_to_all(
        slot_grads.astype(jnp.bfloat16), "seq", split_axis=0, concat_axis=0, tiled=True
    ).astype(slot_grads.dtype)
    dump_row = seq_here * per_dev * HEADS
    targets = jnp.where(slot_live > 0, slot_rows, dump_row).reshape(-1)
    collected = (
        jnp.zeros((dump_row + 1, slot_size), jnp.float32)
        .at[targets]
        .add(returned.reshape(-1, slot_size))
    )
    own_grad = own_grad + collected[:dump_row].reshape(seq_here, per_dev, HEADS, BLOCK, pair_width)
    global_grad = (
        jnp.stack([head_grad, tail_grad], axis=1)
        .reshape(seq_here, 2, BLOCK, HEADS, HD)
        .transpose(0, 3, 1, 2, 4)
        .reshape(seq_here, HEADS, 2 * BLOCK, HD)
    )
    global_float = global_grad.astype(jnp.float32)
    global_delta = jnp.sum(global_float * global_ctx, axis=-1)
    global_scores = mixed_sum("shqd,shjkd->shqjk", global_query, local_keys) * score_scale
    global_weights = jnp.exp(global_scores - block_peak)
    coefficient = jnp.exp(block_peak - global_lse[..., None, None])
    global_probs = global_weights * coefficient
    global_dweights = mixed_sum("shqd,shjkd->shqjk", global_grad, local_values)
    global_dscores = (global_probs * (global_dweights - global_delta[..., None, None])).astype(
        jnp.bfloat16
    )
    d_global_query = mixed_sum("shqjk,shjkd->shqd", global_dscores, local_keys) * score_scale
    d_local_keys = mixed_sum("shqjk,shqd->shjkd", global_dscores, global_query) * score_scale
    d_local_values = exact_sum(
        "shqjk,shqd->shjkd",
        global_weights.astype(jnp.bfloat16).astype(jnp.float32) * coefficient,
        global_float,
    )
    own_grad = own_grad + jnp.concatenate([d_local_keys, d_local_values], axis=-1).transpose(
        0, 2, 1, 3, 4
    )
    head_terms = (d_global_query[:, :, :BLOCK], global_part[:, :, :BLOCK])
    tail_terms = (d_global_query[:, :, BLOCK:], global_part[:, :, BLOCK:])
    zero_terms = (jnp.zeros_like(head_terms[0]), jnp.zeros_like(head_terms[1]))
    head_rest = entering(head_terms, "seq", add_pair, zero_terms, True)
    tail_rest = entering(tail_terms, "seq", add_pair, zero_terms, False)
    head_full = add_pair(head_rest, head_terms)
    tail_full = add_pair(tail_rest, tail_terms)
    d_query = (
        d_query
        + jnp.where(head_mask, head_full[0][:, None], 0.0)
        + jnp.where(tail_mask, tail_full[0][:, None], 0.0)
    )
    own_grad = (
        own_grad
        + jnp.where(head_mask, head_full[1][:, None], 0.0)
        + jnp.where(tail_mask, tail_full[1][:, None], 0.0)
    )
    d_query_rows = from_heads(d_query).astype(jnp.bfloat16)
    kv_grad = own_grad.transpose(0, 1, 3, 2, 4).reshape(rows_here, HEADS, pair_width)
    d_key_rows = kv_grad[..., :HD].reshape(rows_here, model_width).astype(jnp.bfloat16)
    d_value_rows = kv_grad[..., HD:].reshape(rows_here, model_width).astype(jnp.bfloat16)
    grad_w_query = dense_left(normed, d_query_rows)
    grad_bias_query = jnp.sum(d_query_rows.astype(jnp.float32), axis=0)
    grad_w_key = dense_left(normed, d_key_rows)
    grad_w_value = dense_left(normed, d_value_rows)
    grad_bias_value = jnp.sum(d_value_rows.astype(jnp.float32), axis=0)
    d_normed = (
        dense_back(d_query_rows, w_query)
        + dense_back(d_key_rows, w_key)
        + dense_back(d_value_rows, w_value)
    )
    norm_pull_one = jax.vjp(layer_norm, inputs, attn_gain, attn_shift)[1]
    d_inputs_norm, grad_attn_gain, grad_attn_shift = norm_pull_one(d_normed)
    grad_tokens = (
        (d_middle + d_inputs_norm).astype(jnp.bfloat16).reshape(seq_here, local_len, model_width)
    )
    grad_list = [
        grad_w_query,
        grad_w_key,
        grad_w_value,
        grad_w_out,
        grad_w_up,
        grad_w_down,
        grad_bias_query,
        grad_bias_value,
        grad_bias_out,
        grad_bias_up,
        grad_bias_down,
        grad_attn_gain,
        grad_attn_shift,
        grad_ffn_gain,
        grad_ffn_shift,
    ]
    flattened = jnp.concatenate([member.reshape(-1) for member in grad_list])
    item_count = lax.axis_size("item")
    length_all = flattened.shape[0]
    stride_all = 128 * item_count * devices
    padded_len = (length_all + stride_all - 1) // stride_all * stride_all
    lead_pad = padded_len - length_all
    grad_grid = jnp.pad(flattened, (lead_pad, 0)).reshape(-1, 128)
    shared_rows = lax.psum_scatter(grad_grid, ("item", "seq"), scatter_dimension=0, tiled=True)
    summed = (
        lax.all_gather(shared_rows.astype(jnp.bfloat16), ("item", "seq"), axis=0, tiled=True)
        .astype(shared_rows.dtype)
        .reshape(-1)
    )
    results = []
    offset = lead_pad
    for member in grad_list:
        results.append(summed[offset : offset + member.size].reshape(member.shape))
        offset = offset + member.size
    return (
        layer_out,
        grad_tokens,
        results[0],
        results[1],
        results[2],
        results[3],
        results[4],
        results[5],
        results[6],
        results[7],
        results[8],
        results[9],
        results[10],
        results[11],
        results[12],
        results[13],
        results[14],
    )


LANES = 128
GROUP = 4
FAR = -1e30
BF = jnp.bfloat16
F32 = jnp.float32
VMEM_ASK = 56 * 1024 * 1024


def over_z(value, step):
    count = lax.axis_size("seq")
    return lax.ppermute(value, "seq", [(i, i ^ (2 * step)) for i in range(count)])


def over_core(value):
    count = lax.axis_size("seq")
    return lax.ppermute(value, "seq", [(i, i ^ 1) for i in range(count)])


def over_item(value, step):
    count = lax.axis_size("item")
    return lax.ppermute(value, "item", [(i, i ^ step) for i in range(count)])


def in_order(parts, place):
    low = (place & 1) == 1
    high = (place & 2) == 2
    p0, p1, p2, p3 = parts
    p0, p1, p2, p3 = (
        jnp.where(low, p1, p0),
        jnp.where(low, p0, p1),
        jnp.where(low, p3, p2),
        jnp.where(low, p2, p3),
    )
    return [
        jnp.where(high, p2, p0),
        jnp.where(high, p3, p1),
        jnp.where(high, p0, p2),
        jnp.where(high, p1, p3),
    ]


def params(**more):
    return pltpu.CompilerParams(vmem_limit_bytes=VMEM_ASK, **more)


def vmem(count):
    return [pl.BlockSpec(memory_space=pltpu.VMEM)] * count


def cost(flops, moved, special=0):
    return pl.CostEstimate(flops=flops, bytes_accessed=moved, transcendentals=special)


def dot_nn(left, right):
    return lax.dot_general(left, right, (((1,), (0,)), ((), ())), preferred_element_type=F32)


def dot_tn(left, right):
    return lax.dot_general(left, right, (((0,), (0,)), ((), ())), preferred_element_type=F32)


def dot_nt(left, right):
    return lax.dot_general(left, right, (((1,), (1,)), ((), ())), preferred_element_type=F32)


def attend_kernel(heads, *refs):
    own, other, mult_ref = refs[:4], refs[4:8], refs[8]
    ctx_refs, out_ref, lse_ref = refs[9:13], refs[13], refs[14]
    width = heads * HD
    for h in range(heads):
        low = h * HD
        query = jnp.concatenate([r[low : low + HD, :] for r in own], axis=1)
        key = jnp.concatenate(
            [r[width + low : width + low + HD, :] for r in own]
            + [r[low : low + HD, :] for r in other],
            axis=1,
        )
        value = jnp.concatenate(
            [r[2 * width + low : 2 * width + low + HD, :] for r in own]
            + [r[width + low : width + low + HD, :] for r in other],
            axis=1,
        )
        rows, lanes = key.shape[1], query.shape[1]
        scores = dot_tn(key, query) * (HD**-0.5)
        scores = scores.reshape(rows // BLOCK, BLOCK, lanes)
        mult = mult_ref[h][:, None, :]
        scores = jnp.where(mult > 0.0, scores, FAR)
        peak = jnp.max(jnp.max(scores, axis=0), axis=0, keepdims=True)
        weights = jnp.exp(scores - peak[None]) * mult
        total = jnp.sum(jnp.sum(weights, axis=0), axis=0, keepdims=True)
        packed = weights.astype(BF).reshape(rows, lanes)
        out = dot_nn(value, packed) / total
        out_ref[low : low + HD, :] = out
        lse_ref[h] = peak + jnp.log(total)
        rounded = out.astype(BF)
        for k in range(4):
            ctx_refs[k][low : low + HD, :] = rounded[:, k * LANES : (k + 1) * LANES]


def attend_back_kernel(heads, *refs):
    own, other, mult_ref, out_ref, lse_ref = refs[:4], refs[4:8], refs[8], refs[9], refs[10]
    grad_refs = refs[11:15]
    dq_ref, dkv_ref, far_ref = refs[15:18]
    width = heads * HD
    for h in range(heads):
        low = h * HD
        query = jnp.concatenate([r[low : low + HD, :] for r in own], axis=1)
        key = jnp.concatenate(
            [r[width + low : width + low + HD, :] for r in own]
            + [r[low : low + HD, :] for r in other],
            axis=1,
        )
        value = jnp.concatenate(
            [r[2 * width + low : 2 * width + low + HD, :] for r in own]
            + [r[width + low : width + low + HD, :] for r in other],
            axis=1,
        )
        grad = jnp.concatenate([r[low : low + HD, :] for r in grad_refs], axis=1)
        rows, lanes = key.shape[1], query.shape[1]
        scale = HD**-0.5
        scores = dot_tn(key, query) * scale
        scores = scores.reshape(rows // BLOCK, BLOCK, lanes)
        mult = mult_ref[h][:, None, :]
        scores = jnp.where(mult > 0.0, scores, FAR)
        probs = jnp.exp(scores - lse_ref[h][None]) * mult
        delta = jnp.sum(grad.astype(F32) * out_ref[low : low + HD, :], axis=0, keepdims=True)
        d_probs = dot_tn(value, grad).reshape(rows // BLOCK, BLOCK, lanes)
        d_scores = (probs * (d_probs - delta[None])).astype(BF).reshape(rows, lanes)
        packed = probs.astype(BF).reshape(rows, lanes)
        dq_ref[low : low + HD, :] = (dot_nn(key, d_scores) * scale).astype(BF)
        d_key = dot_nt(query, d_scores) * scale
        d_value = dot_nt(grad, packed)
        half = rows // 2
        dkv_ref[low : low + HD, :] = d_key[:, :half]
        dkv_ref[width + low : width + low + HD, :] = d_value[:, :half]
        far_ref[low : low + HD, :] = d_key[:, half:].astype(BF)
        far_ref[width + low : width + low + HD, :] = d_value[:, half:].astype(BF)


def norm_parts(values):
    center = values - jnp.mean(values, axis=-1, keepdims=True)
    rate = lax.rsqrt(jnp.mean(center * center, axis=-1, keepdims=True) + epsilon)
    return center * rate, rate


def middle_kernel(
    place_ref, tokens_ref, ctx0, ctx1, ctx2, ctx3, w_out_ref, b_out_ref, gain_ref, shift_ref,
    w_up_ref, b_up_ref, d_active_ref, cot_ref,
    send0, send1, send2, send3, back0, back1, back2, back3, middle_ref, active_ref, d_middle_ref,
    grad_up_ref, grad_out_ref, grad_gain_ref, grad_shift_ref,
    ctx_full, active_t, d_hidden_f,
):
    chip, item = place_ref[0], place_ref[1]
    rows, width = tokens_ref.shape
    part = width // GROUP
    fan = w_up_ref.shape[1]
    for k, ref in enumerate((ctx0, ctx1, ctx2, ctx3)):
        at = pl.multiple_of((chip ^ k) * part, part)
        ctx_full[pl.ds(at, part), :] = ref[...]
    context = ctx_full[...]
    middle = tokens_ref[...].astype(F32) + (dot_tn(context, w_out_ref[...]) + b_out_ref[...])
    middle_ref[...] = middle
    hat, rate = norm_parts(middle)
    normed = (hat * gain_ref[...] + shift_ref[...]).astype(BF)
    d_norm = jnp.zeros((rows, width), F32)
    chunk = width
    for j in range(fan // chunk):
        cols = slice(j * chunk, (j + 1) * chunk)
        hidden = dot_nn(normed, w_up_ref[:, cols]) + b_up_ref[:, cols]
        bell = 0.5 * (1.0 + lax.erf(hidden * (0.5**0.5)))
        active = (hidden * bell).astype(BF)
        active_ref[:, cols] = active
        active_t[cols, :] = active.T
        slope = bell + hidden * jnp.exp(-0.5 * hidden * hidden) * 0.3989422804014327
        d_hidden = (d_active_ref[:, cols] * slope).astype(BF)
        grad_up_ref[:, cols] = jnp.sum(d_hidden.astype(F32), axis=0, keepdims=True)
        for b in range(chunk // LANES):
            at = j * chunk + b * LANES
            d_hidden_f[at : at + LANES, :] = d_hidden[:, b * LANES : (b + 1) * LANES]
        d_norm = d_norm + dot_nt(d_hidden, w_up_ref[:, cols])
    grad_gain_ref[...] = jnp.sum(d_norm * hat, axis=0, keepdims=True)
    grad_shift_ref[...] = jnp.sum(d_norm, axis=0, keepdims=True)
    scaled = d_norm * gain_ref[...]
    d_middle = cot_ref[...].astype(F32) + rate * (
        scaled
        - jnp.mean(scaled, axis=-1, keepdims=True)
        - hat * jnp.mean(scaled * hat, axis=-1, keepdims=True)
    )
    d_middle_ref[...] = d_middle
    d_attended = d_middle.astype(BF)
    grad_out_ref[...] = jnp.sum(d_attended.astype(F32), axis=0, keepdims=True)
    d_context = dot_nt(w_out_ref[...], d_attended).astype(BF)
    ctx_full_back = d_context
    normed_t = normed.T
    quarter, small = fan // 8, width // 8
    half = 2 * quarter + small
    for k, ref in enumerate((send0, send1, send2, send3)):
        target = item ^ k
        for c in range(2):
            base = c * (half + 2 * width)
            at = pl.multiple_of(c * (fan // 2) + target * quarter, quarter)
            ref[base : base + quarter, :] = active_t[pl.ds(at, quarter), :]
            ref[base + quarter : base + 2 * quarter, :] = d_hidden_f[pl.ds(at, quarter), :]
            at = pl.multiple_of(c * (width // 2) + target * small, small)
            ref[base + 2 * quarter : base + half, :] = ctx_full[pl.ds(at, small), :]
        ref[half : half + width, :] = normed_t
        for b in range(width // LANES):
            at = half + width + b * LANES
            ref[at : at + LANES, :] = d_attended[:, b * LANES : (b + 1) * LANES]
    ctx_full[...] = ctx_full_back
    for k, ref in enumerate((back0, back1, back2, back3)):
        at = pl.multiple_of((chip ^ k) * part, part)
        ref[...] = ctx_full[pl.ds(at, part), :]


def weight_grad_kernel(
    width, fan, place_ref, own0, own1, own2, own3, far0, far1, far2, far3, cot_ref,
    out0, out1, out2, out3,
    up_left, up_right, down_left, out_left, out_right, flat,
):
    chip, core = place_ref[0], place_ref[2]
    quarter, small = fan // 8, width // 8
    half = 2 * quarter + small
    for s, ref in enumerate((own0, own1, own2, own3, far0, far1, far2, far3)):
        if s < 4:
            mine, shared = core * (half + 2 * width), half
        else:
            mine, shared = core * (2 * width), (1 - core) * half

        def rows(start, size, ref=ref):
            if not isinstance(start, int):
                start = pl.multiple_of(start, 32)
            return ref[pl.ds(start, size), :]

        span = slice(s * LANES, (s + 1) * LANES)
        down_left[:, span] = rows(mine, quarter)
        for b in range(quarter // LANES):
            up_right[span, b * LANES : (b + 1) * LANES] = rows(mine + quarter + b * LANES, LANES)
        out_left[:, span] = rows(mine + 2 * quarter, small)
        up_left[:, span] = rows(shared, width)
        for b in range(width // LANES):
            out_right[span, b * LANES : (b + 1) * LANES] = rows(shared + width + b * LANES, LANES)
    blocks = width // LANES
    at = 0
    grad_up = dot_nn(up_left[...], up_right[...]).astype(BF)
    for b in range(quarter // LANES):
        flat[at : at + width, :] = grad_up[:, b * LANES : (b + 1) * LANES]
        at += width
    grad_out = dot_nn(out_left[...], out_right[...]).astype(BF)
    for b in range(blocks // 2):
        flat[at : at + small, :] = grad_out[:, b * LANES : (b + 1) * LANES]
        at += small
    grad_down = dot_nn(down_left[...], cot_ref[...]).astype(BF)
    for b in range(blocks):
        flat[at : at + quarter, :] = grad_down[:, b * LANES : (b + 1) * LANES]
        at += quarter
    for b in range(blocks // 2, blocks):
        flat[at : at + small, :] = grad_out[:, b * LANES : (b + 1) * LANES]
        at += small
    shard = at // GROUP
    for k, ref in enumerate((out0, out1, out2, out3)):
        start = pl.multiple_of((chip ^ k) * shard, 16)
        ref[...] = flat[pl.ds(start, shard), :]


def place_kernel(place_ref, first_ref, second_ref, *refs):
    up_ref, down_ref, out_ref = refs[-3:]
    width = up_ref.shape[0]
    quarter, small = down_ref.shape[0], out_ref.shape[0]
    blocks = width // LANES
    for b in range(quarter // LANES):
        up_ref[:, b * LANES : (b + 1) * LANES] = first_ref[b * width : (b + 1) * width, :].astype(F32)
    for b in range(blocks):
        span = slice(b * LANES, (b + 1) * LANES)
        down_ref[:, span] = second_ref[b * quarter : (b + 1) * quarter, :].astype(F32)
        if b < blocks // 2:
            at = (quarter // LANES) * width + b * small
            out_ref[:, span] = first_ref[at : at + small, :].astype(F32)
        else:
            at = blocks * quarter + (b - blocks // 2) * small
            out_ref[:, span] = second_ref[at : at + small, :].astype(F32)


def put_piece(place, first, second, sofar, width, fan):
    quarter, small = fan // 8, width // 8
    half_rows = first.shape[0]
    shapes = (
        jax.ShapeDtypeStruct((width, fan), F32),
        jax.ShapeDtypeStruct((fan, width), F32),
        jax.ShapeDtypeStruct((width, width), F32),
    )
    filled = () if sofar is None else tuple(sofar)
    return pl.pallas_call(
        place_kernel,
        grid_spec=pltpu.PrefetchScalarGridSpec(
            num_scalar_prefetch=1,
            grid=(1,),
            in_specs=[
                pl.BlockSpec((half_rows, LANES), lambda g, at: (0, 0)),
                pl.BlockSpec((half_rows, LANES), lambda g, at: (0, 0)),
            ]
            + [pl.BlockSpec(memory_space=pl.ANY)] * len(filled),
            out_specs=[
                pl.BlockSpec((width, quarter), lambda g, at: (0, at[0])),
                pl.BlockSpec((quarter, width), lambda g, at: (at[0], 0)),
                pl.BlockSpec((small, width), lambda g, at: (at[0], 0)),
            ],
        ),
        out_shape=shapes,
        input_output_aliases={3 + i: i for i in range(len(filled))},
        compiler_params=params(),
        cost_estimate=cost(0, 6 * 2 * half_rows * LANES),
        name="place_grads",
    )(place, first, second, *filled)


def split_device(
    tokens,
    rand_blocks,
    w_query,
    w_key,
    w_value,
    w_out,
    w_up,
    w_down,
    bias_query,
    bias_value,
    bias_out,
    bias_up,
    bias_down,
    attn_gain,
    attn_shift,
    ffn_gain,
    ffn_shift,
    cotangent,
):
    _, local_len, width = tokens.shape
    fan = w_up.shape[1]
    blocks_all = rand_blocks.shape[0]
    position, item = lax.axis_index("seq"), lax.axis_index("item")
    chip, core = position // 2, position % 2
    heads = HEADS // GROUP
    part = heads * HD
    places = jnp.stack([chip, item, core]).astype(jnp.int32)
    row = lambda v: v.reshape(1, -1)

    steps = jnp.arange(GROUP, dtype=jnp.int32)
    pair = jnp.arange(2, dtype=jnp.int32)
    per_dev = local_len // BLOCK
    chips_in_order = chip ^ steps
    own_ids = ((2 * chips_in_order + core) * per_dev)[:, None] + pair[None]
    other_ids = ((2 * chips_in_order + 1 - core) * per_dev)[:, None] + pair[None]
    own_ids, other_ids = own_ids.reshape(-1), other_ids.reshape(-1)
    key_ids = jnp.concatenate([own_ids, other_ids])[:, None]
    named = lax.dynamic_slice_in_dim(rand_blocks[:, 0], chip * heads, heads, 1)
    named = jnp.take(named, own_ids, axis=0)
    query_ids = own_ids[None, :]
    count = lambda hit: hit.astype(F32)
    fixed = (
        count(key_ids == query_ids - 1)
        + count(key_ids == query_ids)
        + count(key_ids == query_ids + 1)
        + count(key_ids == 0)
        + count(key_ids == blocks_all - 1)
    )
    drawn = sum(
        count(key_ids[None] == named[:, :, n].T[:, None, :]) for n in range(RAND)
    )
    whole = (query_ids == 0) | (query_ids == blocks_all - 1)
    mult = jnp.where(whole[None], 1.0, fixed[None] + drawn)
    mult = jnp.broadcast_to(mult[..., None], mult.shape + (BLOCK,)).reshape(
        heads, 2 * own_ids.shape[0], own_ids.shape[0] * BLOCK
    )

    inputs = tokens[0].astype(F32)
    normed = layer_norm(inputs, attn_gain, attn_shift).astype(BF)
    project = lambda w, b: (dot_nt(w.T, normed) + b).astype(BF)
    q_t = project(w_query, bias_query[:, None]).reshape(GROUP, part, local_len)
    k_t = project(w_key, 0.0).reshape(GROUP, part, local_len)
    v_t = project(w_value, bias_value[:, None]).reshape(GROUP, part, local_len)
    by_chip = jnp.concatenate([q_t, k_t, v_t], axis=1)
    cut = [lax.dynamic_index_in_dim(by_chip, chip ^ k, 0, False) for k in range(GROUP)]
    own = [cut[0]] + [over_z(cut[k], k) for k in range(1, GROUP)]
    other = [over_core(piece[part:]) for piece in own]

    attended = pl.pallas_call(
        functools.partial(attend_kernel, heads),
        in_specs=vmem(9),
        out_specs=vmem(6),
        out_shape=[jax.ShapeDtypeStruct((part, local_len), BF)] * 4
        + [
            jax.ShapeDtypeStruct((part, GROUP * local_len), F32),
            jax.ShapeDtypeStruct((heads, 1, GROUP * local_len), F32),
        ],
        compiler_params=params(),
        cost_estimate=cost(4 * 10**8, 2 * 10**6, 2 * 10**6),
        name="attend",
    )(*own, *other, mult)
    ctx_own, out_t, lse = attended[:4], attended[4], attended[5]
    ctx = [ctx_own[0]] + [over_z(ctx_own[k], k) for k in range(1, GROUP)]

    cot = cotangent[0]
    d_active = dense_back(cot, w_down)
    quarter, small = fan // 8, width // 8
    half = 2 * quarter + small
    sent_rows = 2 * half + 2 * width
    outs = pl.pallas_call(
        middle_kernel,
        in_specs=[pl.BlockSpec(memory_space=pltpu.SMEM)] + vmem(13),
        out_specs=vmem(15),
        out_shape=[jax.ShapeDtypeStruct((sent_rows, LANES), BF)] * 4
        + [jax.ShapeDtypeStruct((part, local_len), BF)] * 4
        + [
            jax.ShapeDtypeStruct((local_len, width), F32),
            jax.ShapeDtypeStruct((local_len, fan), BF),
            jax.ShapeDtypeStruct((local_len, width), F32),
            jax.ShapeDtypeStruct((1, fan), F32),
            jax.ShapeDtypeStruct((1, width), F32),
            jax.ShapeDtypeStruct((1, width), F32),
            jax.ShapeDtypeStruct((1, width), F32),
        ],
        scratch_shapes=[
            pltpu.VMEM((width, local_len), BF),
            pltpu.VMEM((fan, local_len), BF),
            pltpu.VMEM((fan, local_len), BF),
        ],
        compiler_params=params(),
        cost_estimate=cost(2 * 10**9, 12 * 10**6, 10**6),
        name="middle",
    )(
        places, tokens[0], *ctx, w_out, row(bias_out), row(ffn_gain), row(ffn_shift),
        w_up, row(bias_up), d_active, cot,
    )
    sends, backs = outs[:4], outs[4:8]
    middle, active, d_middle, grad_up_b, grad_out_b, grad_fg, grad_fs = outs[8:]
    layer_out = (middle + dense_rows(active, w_down) + bias_down).astype(BF)

    d_ctx = [backs[0]] + [over_z(backs[k], k) for k in range(1, GROUP)]
    d_q, d_kv, d_far = pl.pallas_call(
        functools.partial(attend_back_kernel, heads),
        in_specs=vmem(15),
        out_specs=vmem(3),
        out_shape=[
            jax.ShapeDtypeStruct((part, GROUP * local_len), BF),
            jax.ShapeDtypeStruct((2 * part, GROUP * local_len), F32),
            jax.ShapeDtypeStruct((2 * part, GROUP * local_len), BF),
        ],
        compiler_params=params(),
        cost_estimate=cost(10**9, 3 * 10**6, 2 * 10**6),
        name="attend_back",
    )(*own, *other, mult, out_t, lse, *d_ctx)
    d_kv = (d_kv + over_core(d_far).astype(F32)).astype(BF)
    d_heads = jnp.concatenate([d_q, d_kv], axis=0)

    normed_z = jnp.concatenate([normed] + [over_z(normed, k) for k in range(1, GROUP)], axis=0)
    grad_t = dense_rows(d_heads, normed_z)
    mid = width // 2
    kept = lax.dynamic_slice_in_dim(grad_t, core * mid, mid, 1)
    given = lax.dynamic_slice_in_dim(grad_t, (1 - core) * mid, mid, 1).astype(BF)
    grad_t = (kept + over_core(given).astype(F32)).reshape(GROUP, 3 * part // GROUP, mid)
    rows_of = lambda k: lax.dynamic_index_in_dim(grad_t, item ^ k, 0, False)
    shard = rows_of(0)
    for k in range(1, GROUP):
        shard = shard + over_item(rows_of(k).astype(BF), k).astype(F32)
    shard = shard.astype(BF)
    shard = jnp.stack(in_order([shard] + [over_z(shard, k) for k in range(1, GROUP)], chip))
    shard = jnp.stack(
        in_order([shard] + [over_item(shard, k) for k in range(1, GROUP)], item)
    )
    mirror = over_core(shard)
    low_half = jnp.where(core == 0, shard, mirror)
    high_half = jnp.where(core == 0, mirror, shard)
    full_t = jnp.stack([low_half, high_half])
    full_t = full_t.transpose(2, 1, 3, 0, 4).reshape(GROUP, 3, part, width)
    full_t = full_t.transpose(1, 0, 2, 3).reshape(3, width, width)
    grad_qkv = [full_t[n].T.astype(F32) for n in range(3)]

    d_back = [
        d_heads[:, k * local_len : (k + 1) * local_len] for k in range(GROUP)
    ]
    d_back = [d_back[0]] + [over_z(d_back[k], k) for k in range(1, GROUP)]
    d_back = jnp.stack(in_order(d_back, chip)).reshape(GROUP, 3, part, local_len)
    d_back = [d_back[:, n].reshape(width, local_len) for n in range(3)]
    d_normed = sum(
        lax.dot_general(d, w, (((0,), (1,)), ((), ())), preferred_element_type=F32)
        for d, w in zip(d_back, (w_query, w_key, w_value))
    )
    norm_pull = jax.vjp(layer_norm, inputs, attn_gain, attn_shift)[1]
    d_inputs, grad_ag, grad_as = norm_pull(d_normed)
    grad_tokens = (d_middle + d_inputs).astype(BF)

    cots = jnp.concatenate([cot] + [over_item(cot, k) for k in range(1, GROUP)], axis=0)
    cots = jnp.concatenate([cots, over_core(cots)], axis=0)
    near = [sends[0]] + [over_item(sends[k], k) for k in range(1, GROUP)]
    far = [
        over_core(lax.dynamic_slice_in_dim(piece, (1 - core) * half, half + 2 * width, 0))
        for piece in near
    ]
    flat_rows = 2 * quarter * (width // LANES) + small * (width // LANES)
    shard_rows = flat_rows // GROUP
    shards = pl.pallas_call(
        functools.partial(weight_grad_kernel, width, fan),
        in_specs=[pl.BlockSpec(memory_space=pltpu.SMEM)] + vmem(9),
        out_specs=vmem(4),
        out_shape=[jax.ShapeDtypeStruct((shard_rows, LANES), BF)] * 4,
        scratch_shapes=[
            pltpu.VMEM((width, 8 * LANES), BF),
            pltpu.VMEM((8 * LANES, quarter), BF),
            pltpu.VMEM((quarter, 8 * LANES), BF),
            pltpu.VMEM((small, 8 * LANES), BF),
            pltpu.VMEM((8 * LANES, width), BF),
            pltpu.VMEM((flat_rows, LANES), BF),
        ],
        compiler_params=params(),
        cost_estimate=cost(15 * 10**8, 10**7),
        name="weight_grad",
    )(places, *near, *far, cots)
    total = shards[0].astype(F32)
    for k in range(1, GROUP):
        total = total + over_z(shards[k], k).astype(F32)
    total = total.astype(BF)
    total = jnp.concatenate(
        in_order([total] + [over_z(total, k) for k in range(1, GROUP)], chip), axis=0
    )
    cutting = flat_rows // 2
    first, second = total[:cutting], total[cutting:]
    first_x, second_y = over_item(first, 1), over_item(second, 2)
    first_y, second_x = over_item(first, 2), over_item(second, 1)
    first_d, second_d = over_item(first_x, 2), over_item(second_y, 1)
    pieces = [(first, second), (first_x, second_x), (first_y, second_y), (first_d, second_d)]
    filled = None
    for flip in range(2):
        for k, (one, two) in enumerate(pieces):
            at = ((core ^ flip) * GROUP + (item ^ k)).reshape(1).astype(jnp.int32)
            if flip:
                one, two = over_core(one), over_core(two)
            filled = put_piece(at, one, two, filled, width, fan)
    grad_up, grad_down, grad_out = filled

    flat_small = [
        jnp.sum(cot.astype(F32), axis=0),
        grad_out_b,
        grad_up_b,
        grad_fg,
        grad_fs,
        grad_ag,
        grad_as,
        jnp.sum(d_back[0].astype(F32), axis=1),
        jnp.sum(d_back[2].astype(F32), axis=1),
    ]
    tiny = jnp.concatenate([v.reshape(-1, LANES) for v in flat_small], axis=0)
    tiny = tiny + over_core(tiny)
    tiny = tiny + over_item(tiny, 1)
    tiny = tiny + over_item(tiny, 2)
    tiny = tiny + over_z(tiny, 1)
    tiny = tiny + over_z(tiny, 2)
    tiny = tiny.reshape(-1)
    cuts, at = [], 0
    for v in flat_small:
        cuts.append(tiny[at : at + v.size])
        at += v.size
    g_bd, g_bo, g_bu, g_fg, g_fs, g_ag, g_as, g_bq, g_bv = cuts
    return (
        layer_out[None],
        grad_tokens[None],
        grad_qkv[0],
        grad_qkv[1],
        grad_qkv[2],
        grad_out,
        grad_up,
        grad_down,
        g_bq,
        g_bv,
        g_bo,
        g_bu,
        g_bd,
        g_ag,
        g_as,
        g_fg,
        g_fs,
    )


def per_device(tokens, rand_blocks, *rest):
    seqs, local_len, width = tokens.shape
    fan = rest[4].shape[1]
    fits = (
        seqs == 1
        and local_len == LANES
        and lax.axis_size("item") == GROUP
        and lax.axis_size("seq") == 2 * GROUP
        and HEADS % GROUP == 0
        and width == HEADS * HD
        and fan % (8 * LANES) == 0
        and width % (2 * LANES) == 0
    )
    chosen = split_device if fits else general_device
    return chosen(tokens, rand_blocks, *rest)


def solution(mesh):
    placed = (
        P("item", "seq", None),
        P(None, "item", None, None),
        P(),
        P(),
        P(),
        P(),
        P(),
        P(),
        P(),
        P(),
        P(),
        P(),
        P(),
        P(),
        P(),
        P(),
        P(),
        P("item", "seq", None),
    )
    return jax.shard_map(
        per_device,
        mesh=mesh,
        in_specs=placed,
        out_specs=(
            P("item", "seq", None),
            P("item", "seq", None),
            P(),
            P(),
            P(),
            P(),
            P(),
            P(),
            P(),
            P(),
            P(),
            P(),
            P(),
            P(),
            P(),
            P(),
            P(),
        ),
        check_vma=False,
    )
```

```python
import functools

import jax
import jax.numpy as jnp
from jax import lax
from jax.experimental import pallas as pl
from jax.experimental.pallas import tpu as pltpu
from jax.sharding import PartitionSpec as P

HEADS = 12
HD = 64
BLOCK = 64
RAND = 3


epsilon = 1e-05


def from_root(shard, axis, root):
    mine = lax.axis_index(axis) == root
    return lax.psum(jnp.where(mine, shard, jnp.zeros_like(shard)), axis)


def extended(block, sides, width):
    for axis, dim in sides:
        count = lax.axis_size(axis)
        forward = [(i, i + 1) for i in range(count - 1)]
        backward = [(target, source) for source, target in forward]
        low = lax.ppermute(
            lax.slice_in_dim(block, block.shape[dim] - width, None, axis=dim), axis, forward
        )
        high = lax.ppermute(lax.slice_in_dim(block, 0, width, axis=dim), axis, backward)
        block = jnp.concatenate([low, block, high], axis=dim)
    return block


def joined(shard, axis, join):
    gathered = jax.tree.map(
        lambda a, kind: lax.all_gather(a.astype(kind), axis),
        shard,
        (jnp.bfloat16, jnp.bfloat16, jnp.bfloat16),
    )

    def take(source):
        return jax.tree.map(
            lambda a, own: lax.dynamic_index_in_dim(a, source, 0, False).astype(own.dtype),
            gathered,
            shard,
        )

    return lax.fori_loop(
        1, lax.axis_size(axis), lambda source, state: join(state, take(source)), take(0)
    )


def entering(shard, axis, combine, identity, reverse):
    count, position = (lax.axis_size(axis), lax.axis_index(axis))
    everything = jax.tree.map(
        lambda part, kind: lax.all_gather(part.astype(kind), axis),
        shard,
        jax.tree.map(lambda a: jnp.bfloat16 if a.dtype == jnp.float32 else a.dtype, shard),
    )
    start = jax.tree.map(
        lambda part, zero: jnp.broadcast_to(jnp.asarray(zero, part.dtype), part.shape),
        shard,
        identity,
    )

    def step(k, before):
        at = count - 1 - k if reverse else k
        reached = at > position if reverse else at < position
        new = combine(
            before, jax.tree.map(lambda part, own: part[at].astype(own.dtype), everything, shard)
        )
        return jax.tree.map(lambda a, b: jnp.where(reached, a, b), new, before)

    return lax.fori_loop(0, count, step, start)


def layer_norm(values, norm_gain, norm_bias):
    center = values - jnp.mean(values, axis=-1, keepdims=True)
    spread = jnp.mean(center * center, axis=-1, keepdims=True)
    return center * lax.rsqrt(spread + epsilon) * norm_gain + norm_bias


def gelu_exact(values):
    return jax.nn.gelu(values, approximate=False)


def dense_rows(left, right):
    return jnp.dot(left, right, preferred_element_type=jnp.float32)


def dense_left(left, right):
    return lax.dot_general(
        left, right, (((0,), (0,)), ((), ())), preferred_element_type=jnp.float32
    )


def dense_back(left, right):
    return lax.dot_general(
        left, right, (((1,), (1,)), ((), ())), preferred_element_type=jnp.float32
    )


def mixed_sum(form, left, right):
    return jnp.einsum(form, left, right, preferred_element_type=jnp.float32)


def exact_sum(form, left, right):
    return jnp.einsum(
        form, left, right, precision=lax.Precision.HIGHEST, preferred_element_type=jnp.float32
    )


def from_ends(first_part, last_part):
    head_part = from_root(first_part, "seq", 0)
    tail_part = from_root(last_part, "seq", lax.axis_size("seq") - 1)
    return (head_part, tail_part)


def merge_rows(left_part, right_part):
    left_peak, left_total, left_sum = left_part
    right_peak, right_total, right_sum = right_part
    new_peak = jnp.maximum(left_peak, right_peak)
    left_scale = jnp.exp(left_peak - new_peak)
    right_scale = jnp.exp(right_peak - new_peak)
    return (
        new_peak,
        left_total * left_scale + right_total * right_scale,
        left_sum * left_scale[..., None] + right_sum * right_scale[..., None],
    )


def add_pair(earlier_sum, later_sum):
    return (earlier_sum[0] + later_sum[0], earlier_sum[1] + later_sum[1])


def general_device(
    tokens,
    rand_blocks,
    w_query,
    w_key,
    w_value,
    w_out,
    w_up,
    w_down,
    bias_query,
    bias_value,
    bias_out,
    bias_up,
    bias_down,
    attn_gain,
    attn_shift,
    ffn_gain,
    ffn_shift,
    cotangent,
):
    seq_here, local_len, model_width = tokens.shape
    blocks_all = rand_blocks.shape[0]
    devices = lax.axis_size("seq")
    position = lax.axis_index("seq")
    per_dev = blocks_all // devices
    slot_cap = max(2, seq_here * HEADS * RAND * 4 // (3 * blocks_all))
    pair_width = 2 * HD
    lane_count = seq_here * HEADS * RAND
    slot_size = BLOCK * pair_width
    rows_here = seq_here * local_len
    score_scale = HD ** (-0.5)

    def to_heads(values):
        return values.reshape(seq_here, per_dev, BLOCK, HEADS, -1).transpose(0, 1, 3, 2, 4)

    def from_heads(values):
        return values.transpose(0, 1, 3, 2, 4).reshape(rows_here, -1)

    inputs = tokens.reshape(rows_here, model_width).astype(jnp.float32)
    normed = layer_norm(inputs, attn_gain, attn_shift).astype(jnp.bfloat16)
    queries = (dense_rows(normed, w_query) + bias_query).astype(jnp.bfloat16)
    key_rows = dense_rows(normed, w_key).astype(jnp.bfloat16)
    value_rows = (dense_rows(normed, w_value) + bias_value).astype(jnp.bfloat16)
    kv_tokens = jnp.stack(
        [
            key_rows.reshape(seq_here, local_len, HEADS, HD),
            value_rows.reshape(seq_here, local_len, HEADS, HD),
        ],
        axis=3,
    ).reshape(seq_here, local_len, 2 * model_width)
    padded = extended(kv_tokens, (("seq", 1),), BLOCK)
    pad_blocks = padded.reshape(seq_here, per_dev + 2, BLOCK, HEADS, pair_width)
    window = jnp.stack(
        [pad_blocks[:, 0:per_dev], pad_blocks[:, 1 : per_dev + 1], pad_blocks[:, 2 : per_dev + 2]],
        axis=2,
    )
    window = window.transpose(0, 1, 4, 2, 3, 5).reshape(
        seq_here, per_dev, HEADS, 3 * BLOCK, pair_width
    )
    packed = jnp.concatenate([queries.reshape(seq_here, local_len, model_width), kv_tokens], axis=2)
    head_pack, tail_pack = from_ends(packed[:, :BLOCK], packed[:, local_len - BLOCK :])
    global_pack = jnp.stack([head_pack, tail_pack], axis=1)
    global_query = (
        global_pack[..., :model_width]
        .reshape(seq_here, 2, BLOCK, HEADS, HD)
        .transpose(0, 3, 1, 2, 4)
        .reshape(seq_here, HEADS, 2 * BLOCK, HD)
    )
    global_kv = (
        global_pack[..., model_width:]
        .reshape(seq_here, 2, BLOCK, HEADS, pair_width)
        .transpose(0, 3, 1, 2, 4)
        .reshape(seq_here, HEADS, 2 * BLOCK, pair_width)
    )
    flat_req = rand_blocks.reshape(blocks_all, lane_count)
    block_ids = jnp.arange(blocks_all, dtype=jnp.int32)
    live_rows = (block_ids != 0) & (block_ids != blocks_all - 1)
    own_blocks = position * per_dev + jnp.arange(per_dev, dtype=jnp.int32)
    matches = (
        (flat_req[:, :, None] == own_blocks[None, None, :]) & live_rows[:, None, None]
    ).astype(jnp.int32)
    order_rank = jnp.cumsum(matches, axis=1) - matches
    slot_ids = jnp.arange(slot_cap, dtype=jnp.int32)
    chosen = matches[..., None] * (order_rank[..., None] == slot_ids).astype(jnp.int32)
    lane_ids = jnp.arange(lane_count, dtype=jnp.int32)
    source_rows = lane_ids // (HEADS * RAND) * (per_dev * HEADS) + lane_ids // RAND % HEADS
    slot_live = jnp.sum(chosen, axis=1)
    slot_rows = (
        jnp.sum(chosen * source_rows[None, :, None, None], axis=1)
        + (jnp.arange(per_dev, dtype=jnp.int32) * HEADS)[None, :, None]
    )
    kv_heads = (
        kv_tokens.reshape(seq_here, per_dev, BLOCK, HEADS, pair_width)
        .transpose(0, 1, 3, 2, 4)
        .reshape(seq_here * per_dev * HEADS, slot_size)
    )
    served = jnp.take(kv_heads, slot_rows.reshape(-1), axis=0) * slot_live.reshape(-1, 1).astype(
        jnp.bfloat16
    )
    served = served.reshape(devices, per_dev, per_dev, slot_cap, slot_size)
    replies = lax.all_to_all(served, "seq", split_axis=0, concat_axis=0, tiled=True)
    fetched = replies.transpose(1, 0, 2, 3, 4).reshape(per_dev * blocks_all * slot_cap, slot_size)
    my_blocks = lax.dynamic_slice_in_dim(flat_req, position * per_dev, per_dev, 0)
    same_key = (my_blocks[:, :, None] == my_blocks[:, None, :]) & (
        lane_ids[None, None, :] < lane_ids[None, :, None]
    )
    my_ranks = jnp.sum(same_key.astype(jnp.int32), axis=2)
    pick_rows = (
        jnp.arange(per_dev, dtype=jnp.int32)[:, None] * blocks_all + my_blocks
    ) * slot_cap + my_ranks
    rand_kv = jnp.take(fetched, pick_rows.reshape(-1), axis=0).reshape(
        per_dev, seq_here, HEADS, RAND, BLOCK, pair_width
    )
    rand_kv = rand_kv.transpose(1, 0, 2, 3, 4, 5).reshape(
        seq_here, per_dev, HEADS, RAND * BLOCK, pair_width
    )
    global_kv_all = jnp.broadcast_to(
        global_kv[:, None], (seq_here, per_dev, HEADS, 2 * BLOCK, pair_width)
    )
    keys_all = jnp.concatenate([window, global_kv_all, rand_kv], axis=3)
    list_keys = keys_all[..., :HD]
    list_values = keys_all[..., HD:]
    query_heads = to_heads(queries)
    scores = mixed_sum("sjhqd,sjhkd->sjhqk", query_heads, list_keys) * score_scale
    row_peak = jnp.max(scores, axis=-1, keepdims=True)
    weights = jnp.exp(scores - row_peak)
    row_total = jnp.sum(weights, axis=-1, keepdims=True)
    near_out = (
        mixed_sum("sjhqk,sjhkd->sjhqd", weights.astype(jnp.bfloat16), list_values) / row_total
    )
    local_heads = kv_tokens.reshape(seq_here, per_dev, BLOCK, HEADS, pair_width).transpose(
        0, 3, 1, 2, 4
    )
    local_keys = local_heads[..., :HD]
    local_values = local_heads[..., HD:]
    global_scores = mixed_sum("shqd,shjkd->shqjk", global_query, local_keys) * score_scale
    block_peak = jnp.max(global_scores, axis=-1, keepdims=True)
    global_weights = jnp.exp(global_scores - block_peak)
    local_top = jnp.max(block_peak, axis=3, keepdims=True)
    factor = jnp.exp(block_peak - local_top)
    local_total = jnp.sum(factor * jnp.sum(global_weights, axis=-1, keepdims=True), axis=(3, 4))
    local_sum = jnp.sum(
        factor * mixed_sum("shqjk,shjkd->shqjd", global_weights.astype(jnp.bfloat16), local_values),
        axis=3,
    )
    global_top, global_total, global_sum = joined(
        (local_top[..., 0, 0], local_total, local_sum), "seq", merge_rows
    )
    global_ctx = global_sum / global_total[..., None]
    global_lse = global_top + jnp.log(global_total)
    block_here = jnp.arange(per_dev, dtype=jnp.int32)
    head_mask = ((position == 0) & (block_here == 0))[None, :, None, None, None]
    tail_mask = ((position == devices - 1) & (block_here == per_dev - 1))[None, :, None, None, None]
    context = jnp.where(head_mask, global_ctx[:, None, :, :BLOCK], near_out)
    context = jnp.where(tail_mask, global_ctx[:, None, :, BLOCK:], context)
    context_rows = from_heads(context).astype(jnp.bfloat16)
    middle = inputs + (dense_rows(context_rows, w_out) + bias_out)
    normed_two = layer_norm(middle, ffn_gain, ffn_shift).astype(jnp.bfloat16)
    hidden = dense_rows(normed_two, w_up) + bias_up
    active = gelu_exact(hidden).astype(jnp.bfloat16)
    layer_out = (
        (middle + dense_rows(active, w_down) + bias_down)
        .astype(jnp.bfloat16)
        .reshape(seq_here, local_len, model_width)
    )
    cot_rows = cotangent.reshape(rows_here, model_width)
    cot_float = cot_rows.astype(jnp.float32)
    grad_w_down = dense_left(active, cot_rows)
    grad_bias_down = jnp.sum(cot_float, axis=0)
    d_active = dense_back(cot_rows, w_down)
    gelu_pull = jax.vjp(gelu_exact, hidden)[1]
    d_hidden = gelu_pull(d_active)[0].astype(jnp.bfloat16)
    grad_w_up = dense_left(normed_two, d_hidden)
    grad_bias_up = jnp.sum(d_hidden.astype(jnp.float32), axis=0)
    norm_pull_two = jax.vjp(layer_norm, middle, ffn_gain, ffn_shift)[1]
    d_middle_norm, grad_ffn_gain, grad_ffn_shift = norm_pull_two(dense_back(d_hidden, w_up))
    d_middle = cot_float + d_middle_norm
    d_attended = d_middle.astype(jnp.bfloat16)
    grad_w_out = dense_left(context_rows, d_attended)
    grad_bias_out = jnp.sum(d_attended.astype(jnp.float32), axis=0)
    d_context = dense_back(d_attended, w_out).astype(jnp.bfloat16)
    d_tokens = d_context.reshape(seq_here, local_len, model_width)
    head_grad, tail_grad = from_ends(d_tokens[:, :BLOCK], d_tokens[:, local_len - BLOCK :])
    d_heads = jnp.where(head_mask | tail_mask, jnp.zeros((), jnp.bfloat16), to_heads(d_context))
    d_float = d_heads.astype(jnp.float32)
    row_delta = jnp.sum(d_float * near_out, axis=-1, keepdims=True)
    scores = mixed_sum("sjhqd,sjhkd->sjhqk", query_heads, list_keys) * score_scale
    weights = jnp.exp(scores - row_peak)
    d_weights = mixed_sum("sjhqd,sjhkd->sjhqk", d_heads, list_values)
    d_scores = (weights / row_total * (d_weights - row_delta)).astype(jnp.bfloat16)
    d_query = mixed_sum("sjhqk,sjhkd->sjhqd", d_scores, list_keys) * score_scale
    d_list_keys = mixed_sum("sjhqk,sjhqd->sjhkd", d_scores, query_heads) * score_scale
    d_list_values = exact_sum(
        "sjhqk,sjhqd->sjhkd", weights.astype(jnp.bfloat16).astype(jnp.float32), d_float / row_total
    )
    d_kv = jnp.concatenate([d_list_keys, d_list_values], axis=-1)
    d_window = d_kv[:, :, :, : 3 * BLOCK].reshape(seq_here, per_dev, HEADS, 3, BLOCK, pair_width)
    keep_dims = ((0, 0), (0, 0), (0, 0))
    spread_sum = jnp.pad(d_window[:, :, :, 0], ((0, 0), (0, 2)) + keep_dims)
    spread_sum = spread_sum + jnp.pad(d_window[:, :, :, 1], ((0, 0), (1, 1)) + keep_dims)
    spread_sum = spread_sum + jnp.pad(d_window[:, :, :, 2], ((0, 0), (2, 0)) + keep_dims)
    own_grad = spread_sum[:, 1 : per_dev + 1]
    rim_grad = jnp.concatenate(
        [spread_sum[:, 0:1], spread_sum[:, per_dev + 1 : per_dev + 2]], axis=1
    )
    rim_grad = rim_grad.transpose(0, 1, 3, 2, 4).reshape(seq_here, 2 * BLOCK, 2 * model_width)
    back_rim = extended(rim_grad.astype(jnp.bfloat16), (("seq", 1),), BLOCK).astype(rim_grad.dtype)
    from_left = (
        back_rim[:, :BLOCK].reshape(seq_here, BLOCK, HEADS, pair_width).transpose(0, 2, 1, 3)
    )
    from_right = (
        back_rim[:, 3 * BLOCK :].reshape(seq_here, BLOCK, HEADS, pair_width).transpose(0, 2, 1, 3)
    )
    own_grad = own_grad.at[:, 0].add(from_left).at[:, per_dev - 1].add(from_right)
    global_part = jnp.sum(d_kv[:, :, :, 3 * BLOCK : 5 * BLOCK], axis=1)
    rand_part = d_kv[:, :, :, 5 * BLOCK :].reshape(seq_here, per_dev, HEADS, RAND, slot_size)
    rand_part = rand_part.transpose(1, 0, 2, 3, 4).reshape(per_dev * lane_count, slot_size)
    slot_grads = (
        jnp.zeros((per_dev * blocks_all * slot_cap, slot_size), jnp.float32)
        .at[pick_rows.reshape(-1)]
        .add(rand_part)
    )
    slot_grads = slot_grads.reshape(per_dev, devices, per_dev, slot_cap, slot_size).transpose(
        1, 0, 2, 3, 4
    )
    returned = lax.all_to_all(
        slot_grads.astype(jnp.bfloat16), "seq", split_axis=0, concat_axis=0, tiled=True
    ).astype(slot_grads.dtype)
    dump_row = seq_here * per_dev * HEADS
    targets = jnp.where(slot_live > 0, slot_rows, dump_row).reshape(-1)
    collected = (
        jnp.zeros((dump_row + 1, slot_size), jnp.float32)
        .at[targets]
        .add(returned.reshape(-1, slot_size))
    )
    own_grad = own_grad + collected[:dump_row].reshape(seq_here, per_dev, HEADS, BLOCK, pair_width)
    global_grad = (
        jnp.stack([head_grad, tail_grad], axis=1)
        .reshape(seq_here, 2, BLOCK, HEADS, HD)
        .transpose(0, 3, 1, 2, 4)
        .reshape(seq_here, HEADS, 2 * BLOCK, HD)
    )
    global_float = global_grad.astype(jnp.float32)
    global_delta = jnp.sum(global_float * global_ctx, axis=-1)
    global_scores = mixed_sum("shqd,shjkd->shqjk", global_query, local_keys) * score_scale
    global_weights = jnp.exp(global_scores - block_peak)
    coefficient = jnp.exp(block_peak - global_lse[..., None, None])
    global_probs = global_weights * coefficient
    global_dweights = mixed_sum("shqd,shjkd->shqjk", global_grad, local_values)
    global_dscores = (global_probs * (global_dweights - global_delta[..., None, None])).astype(
        jnp.bfloat16
    )
    d_global_query = mixed_sum("shqjk,shjkd->shqd", global_dscores, local_keys) * score_scale
    d_local_keys = mixed_sum("shqjk,shqd->shjkd", global_dscores, global_query) * score_scale
    d_local_values = exact_sum(
        "shqjk,shqd->shjkd",
        global_weights.astype(jnp.bfloat16).astype(jnp.float32) * coefficient,
        global_float,
    )
    own_grad = own_grad + jnp.concatenate([d_local_keys, d_local_values], axis=-1).transpose(
        0, 2, 1, 3, 4
    )
    head_terms = (d_global_query[:, :, :BLOCK], global_part[:, :, :BLOCK])
    tail_terms = (d_global_query[:, :, BLOCK:], global_part[:, :, BLOCK:])
    zero_terms = (jnp.zeros_like(head_terms[0]), jnp.zeros_like(head_terms[1]))
    head_rest = entering(head_terms, "seq", add_pair, zero_terms, True)
    tail_rest = entering(tail_terms, "seq", add_pair, zero_terms, False)
    head_full = add_pair(head_rest, head_terms)
    tail_full = add_pair(tail_rest, tail_terms)
    d_query = (
        d_query
        + jnp.where(head_mask, head_full[0][:, None], 0.0)
        + jnp.where(tail_mask, tail_full[0][:, None], 0.0)
    )
    own_grad = (
        own_grad
        + jnp.where(head_mask, head_full[1][:, None], 0.0)
        + jnp.where(tail_mask, tail_full[1][:, None], 0.0)
    )
    d_query_rows = from_heads(d_query).astype(jnp.bfloat16)
    kv_grad = own_grad.transpose(0, 1, 3, 2, 4).reshape(rows_here, HEADS, pair_width)
    d_key_rows = kv_grad[..., :HD].reshape(rows_here, model_width).astype(jnp.bfloat16)
    d_value_rows = kv_grad[..., HD:].reshape(rows_here, model_width).astype(jnp.bfloat16)
    grad_w_query = dense_left(normed, d_query_rows)
    grad_bias_query = jnp.sum(d_query_rows.astype(jnp.float32), axis=0)
    grad_w_key = dense_left(normed, d_key_rows)
    grad_w_value = dense_left(normed, d_value_rows)
    grad_bias_value = jnp.sum(d_value_rows.astype(jnp.float32), axis=0)
    d_normed = (
        dense_back(d_query_rows, w_query)
        + dense_back(d_key_rows, w_key)
        + dense_back(d_value_rows, w_value)
    )
    norm_pull_one = jax.vjp(layer_norm, inputs, attn_gain, attn_shift)[1]
    d_inputs_norm, grad_attn_gain, grad_attn_shift = norm_pull_one(d_normed)
    grad_tokens = (
        (d_middle + d_inputs_norm).astype(jnp.bfloat16).reshape(seq_here, local_len, model_width)
    )
    grad_list = [
        grad_w_query,
        grad_w_key,
        grad_w_value,
        grad_w_out,
        grad_w_up,
        grad_w_down,
        grad_bias_query,
        grad_bias_value,
        grad_bias_out,
        grad_bias_up,
        grad_bias_down,
        grad_attn_gain,
        grad_attn_shift,
        grad_ffn_gain,
        grad_ffn_shift,
    ]
    flattened = jnp.concatenate([member.reshape(-1) for member in grad_list])
    item_count = lax.axis_size("item")
    length_all = flattened.shape[0]
    stride_all = 128 * item_count * devices
    padded_len = (length_all + stride_all - 1) // stride_all * stride_all
    lead_pad = padded_len - length_all
    grad_grid = jnp.pad(flattened, (lead_pad, 0)).reshape(-1, 128)
    shared_rows = lax.psum_scatter(grad_grid, ("item", "seq"), scatter_dimension=0, tiled=True)
    summed = (
        lax.all_gather(shared_rows.astype(jnp.bfloat16), ("item", "seq"), axis=0, tiled=True)
        .astype(shared_rows.dtype)
        .reshape(-1)
    )
    results = []
    offset = lead_pad
    for member in grad_list:
        results.append(summed[offset : offset + member.size].reshape(member.shape))
        offset = offset + member.size
    return (
        layer_out,
        grad_tokens,
        results[0],
        results[1],
        results[2],
        results[3],
        results[4],
        results[5],
        results[6],
        results[7],
        results[8],
        results[9],
        results[10],
        results[11],
        results[12],
        results[13],
        results[14],
    )


LANES = 128
GROUP = 4
FAR = -1e30
BF = jnp.bfloat16
F32 = jnp.float32
VMEM_ASK = 56 * 1024 * 1024


def over_z(value, step):
    count = lax.axis_size("seq")
    return lax.ppermute(value, "seq", [(i, i ^ (2 * step)) for i in range(count)])


def over_core(value):
    count = lax.axis_size("seq")
    return lax.ppermute(value, "seq", [(i, i ^ 1) for i in range(count)])


def over_item(value, step):
    count = lax.axis_size("item")
    return lax.ppermute(value, "item", [(i, i ^ step) for i in range(count)])


def in_order(parts, place):
    low = (place & 1) == 1
    high = (place & 2) == 2
    p0, p1, p2, p3 = parts
    p0, p1, p2, p3 = (
        jnp.where(low, p1, p0),
        jnp.where(low, p0, p1),
        jnp.where(low, p3, p2),
        jnp.where(low, p2, p3),
    )
    return [
        jnp.where(high, p2, p0),
        jnp.where(high, p3, p1),
        jnp.where(high, p0, p2),
        jnp.where(high, p1, p3),
    ]


def params(**more):
    return pltpu.CompilerParams(vmem_limit_bytes=VMEM_ASK, **more)


def vmem(count):
    return [pl.BlockSpec(memory_space=pltpu.VMEM)] * count


def cost(flops, moved, special=0):
    return pl.CostEstimate(flops=flops, bytes_accessed=moved, transcendentals=special)


LIGHT = cost(10**6, 10**5)


def dot_nn(left, right):
    return lax.dot_general(left, right, (((1,), (0,)), ((), ())), preferred_element_type=F32)


def dot_tn(left, right):
    return lax.dot_general(left, right, (((0,), (0,)), ((), ())), preferred_element_type=F32)


def dot_nt(left, right):
    return lax.dot_general(left, right, (((1,), (1,)), ((), ())), preferred_element_type=F32)


def attend_kernel(heads, *refs):
    own, other, mult_ref = refs[:4], refs[4:8], refs[8]
    ctx_refs, out_ref, lse_ref = refs[9:13], refs[13], refs[14]
    width = heads * HD
    for h in range(heads):
        low = h * HD
        query = jnp.concatenate([r[low : low + HD, :] for r in own], axis=1)
        key = jnp.concatenate(
            [r[width + low : width + low + HD, :] for r in own]
            + [r[low : low + HD, :] for r in other],
            axis=1,
        )
        value = jnp.concatenate(
            [r[2 * width + low : 2 * width + low + HD, :] for r in own]
            + [r[width + low : width + low + HD, :] for r in other],
            axis=1,
        )
        rows, lanes = key.shape[1], query.shape[1]
        scores = dot_tn(key, query) * (HD**-0.5)
        scores = scores.reshape(rows // BLOCK, BLOCK, lanes)
        mult = mult_ref[h][:, None, :]
        scores = jnp.where(mult > 0.0, scores, FAR)
        peak = jnp.max(jnp.max(scores, axis=0), axis=0, keepdims=True)
        weights = jnp.exp(scores - peak[None]) * mult
        total = jnp.sum(jnp.sum(weights, axis=0), axis=0, keepdims=True)
        packed = weights.astype(BF).reshape(rows, lanes)
        out = dot_nn(value, packed) / total
        out_ref[low : low + HD, :] = out
        lse_ref[h] = peak + jnp.log(total)
        rounded = out.astype(BF)
        for k in range(4):
            ctx_refs[k][low : low + HD, :] = rounded[:, k * LANES : (k + 1) * LANES]


def attend_back_kernel(heads, *refs):
    own, other, mult_ref, out_ref, lse_ref = refs[:4], refs[4:8], refs[8], refs[9], refs[10]
    grad_refs = refs[11:14]
    dq_ref, dkv_ref, far_ref = refs[14:17]
    width = heads * HD
    for h in range(heads):
        low = h * HD
        query = jnp.concatenate([r[low : low + HD, :] for r in own], axis=1)
        key = jnp.concatenate(
            [r[width + low : width + low + HD, :] for r in own]
            + [r[low : low + HD, :] for r in other],
            axis=1,
        )
        value = jnp.concatenate(
            [r[2 * width + low : 2 * width + low + HD, :] for r in own]
            + [r[width + low : width + low + HD, :] for r in other],
            axis=1,
        )
        grad = jnp.concatenate(
            [r[low : low + HD, :] for r in grad_refs]
            + [grad_refs[2][width + low : width + low + HD, :]],
            axis=1,
        )
        rows, lanes = key.shape[1], query.shape[1]
        scale = HD**-0.5
        scores = dot_tn(key, query) * scale
        scores = scores.reshape(rows // BLOCK, BLOCK, lanes)
        mult = mult_ref[h][:, None, :]
        scores = jnp.where(mult > 0.0, scores, FAR)
        probs = jnp.exp(scores - lse_ref[h][None]) * mult
        delta = jnp.sum(grad.astype(F32) * out_ref[low : low + HD, :], axis=0, keepdims=True)
        d_probs = dot_tn(value, grad).reshape(rows // BLOCK, BLOCK, lanes)
        d_scores = (probs * (d_probs - delta[None])).astype(BF).reshape(rows, lanes)
        packed = probs.astype(BF).reshape(rows, lanes)
        dq_ref[low : low + HD, :] = (dot_nn(key, d_scores) * scale).astype(BF)
        d_key = dot_nt(query, d_scores) * scale
        d_value = dot_nt(grad, packed)
        half = rows // 2
        dkv_ref[low : low + HD, :] = d_key[:, :half]
        dkv_ref[width + low : width + low + HD, :] = d_value[:, :half]
        far_ref[low : low + HD, :] = d_key[:, half:].astype(BF)
        far_ref[width + low : width + low + HD, :] = d_value[:, half:].astype(BF)


def norm_parts(values):
    center = values - jnp.mean(values, axis=-1, keepdims=True)
    rate = lax.rsqrt(jnp.mean(center * center, axis=-1, keepdims=True) + epsilon)
    return center * rate, rate


def after(value, *others):
    return lax.optimization_barrier((value, *others))[0]


def line(ref, start=0, size=None):
    size = ref.shape[0] if size is None else size
    return ref[start : start + size].reshape(1, size)


def lay_rows(out, at, vector):
    for b in range(vector.shape[1] // LANES):
        out[at + b : at + b + 1, :] = vector[:, b * LANES : (b + 1) * LANES]
    return at + vector.shape[1] // LANES


def project_kernel(
    place_ref, tokens_ref, wq_ref, wk_ref, wv_ref, bq_ref, bv_ref, gain_ref, shift_ref,
    hat_ref, cut0, cut1, cut2, cut3, held, turned, sems,
):
    chip = place_ref[0]
    width = tokens_ref.shape[1]
    part = width // GROUP
    copies = [
        pltpu.make_async_copy(ref, held.at[n], sems.at[n])
        for n, ref in enumerate((wq_ref, wk_ref, wv_ref))
    ]
    for copy in copies:
        copy.start()
    hat, _ = norm_parts(tokens_ref[...].astype(F32))
    hat_ref[...] = hat.astype(BF)
    normed = (hat * line(gain_ref) + line(shift_ref)).astype(BF)
    biases = (bq_ref, None, bv_ref)
    for n, copy in enumerate(copies):
        copy.wait()
        rows = dot_nn(normed, held[n])
        if biases[n] is not None:
            rows = rows + line(biases[n])
        turned[n * width : (n + 1) * width, :] = rows.astype(BF).T
    for k, ref in enumerate((cut0, cut1, cut2, cut3)):
        for n in range(3):
            at = pl.multiple_of(n * width + (chip ^ k) * part, part)
            ref[n * part : (n + 1) * part, :] = turned[pl.ds(at, part), :]


def mult_kernel(heads, blocks_all, place_ref, rand_ref, mult_ref):
    chip, core = place_ref[0], place_ref[2]
    rows, lanes = mult_ref.shape[1], mult_ref.shape[2]
    spot = lax.broadcasted_iota(jnp.int32, (rows, BLOCK), 0)
    side = jnp.where(spot < rows // 2, core, 1 - core)
    key_ids = 4 * (chip ^ ((spot >> 1) & 3)) + 2 * side + (spot & 1)
    one = lambda hit: jnp.where(hit, 1.0, 0.0)
    ends = one(key_ids == 0) + one(key_ids == blocks_all - 1)
    for r in range(lanes // BLOCK):
        query = 4 * (chip ^ (r // 2)) + 2 * core + (r % 2)
        fixed = ends + one(key_ids == query - 1) + one(key_ids == query) + one(key_ids == query + 1)
        whole = (query == 0) | (query == blocks_all - 1)
        for h in range(heads):
            total = fixed
            for n in range(RAND):
                named = rand_ref[query * (HEADS * RAND) + (chip * heads + h) * RAND + n]
                total = total + one(key_ids == named)
            total = jnp.where(whole, jnp.ones_like(total), total)
            mult_ref[h, :, r * BLOCK : (r + 1) * BLOCK] = total


def middle_kernel(
    place_ref, tokens_ref, ctx0, ctx1, ctx2, ctx3, w_out_hbm, b_out_ref, gain_ref, shift_ref,
    w_up_hbm, b_up_ref, d_active_hbm, cot_ref,
    down0, down1, down2, down3, up0, up1, up2, up3, back0, back1,
    middle_ref, active_ref, d_middle_ref, tiny_ref,
    ctx_full, active_t, d_hidden_f, d_att_f, d_ctx_full, w_out_ref, w_up_ref, d_active_ref, sems,
):
    chip, item = place_ref[0], place_ref[1]
    rows, width = tokens_ref.shape
    part = width // GROUP
    fan = w_up_ref.shape[1]
    chunk = width
    chunks = fan // chunk
    out_copy = pltpu.make_async_copy(w_out_hbm, w_out_ref, sems.at[0])
    out_copy.start()
    copies = []
    for j in range(chunks):
        cols = slice(j * chunk, (j + 1) * chunk)
        up_copy = pltpu.make_async_copy(w_up_hbm.at[:, cols], w_up_ref.at[:, cols], sems.at[1 + j])
        act_copy = pltpu.make_async_copy(
            d_active_hbm.at[:, cols], d_active_ref.at[:, cols], sems.at[1 + chunks + j]
        )
        up_copy.start()
        act_copy.start()
        copies.append((up_copy, act_copy))
    for k, ref in enumerate((ctx0, ctx1, ctx2, ctx3)):
        at = pl.multiple_of((chip ^ k) * part, part)
        ctx_full[pl.ds(at, part), :] = ref[...]
    context = ctx_full[...]
    out_copy.wait()
    middle = tokens_ref[...].astype(F32) + (dot_tn(context, w_out_ref[...]) + line(b_out_ref))
    middle_ref[...] = middle
    hat, rate = norm_parts(middle)
    normed = (hat * line(gain_ref) + line(shift_ref)).astype(BF)
    at = 0
    d_norm = jnp.zeros((rows, width), F32)
    for j in range(chunks):
        cols = slice(j * chunk, (j + 1) * chunk)
        copies[j][0].wait()
        hidden = dot_nn(normed, w_up_ref[:, cols]) + line(b_up_ref, j * chunk, chunk)
        bell = 0.5 * (1.0 + lax.erf(hidden * (0.5**0.5)))
        active = (hidden * bell).astype(BF)
        active_ref[:, cols] = active
        active_t[cols, :] = active.T
        slope = bell + hidden * jnp.exp(-0.5 * hidden * hidden) * 0.3989422804014327
        copies[j][1].wait()
        d_hidden = (d_active_ref[:, cols] * slope).astype(BF)
        at = lay_rows(tiny_ref, at, jnp.sum(d_hidden.astype(F32), axis=0, keepdims=True))
        for b in range(chunk // LANES):
            to = j * chunk + b * LANES
            d_hidden_f[to : to + LANES, :] = d_hidden[:, b * LANES : (b + 1) * LANES]
        d_norm = d_norm + dot_nt(d_hidden, w_up_ref[:, cols])
    at = lay_rows(tiny_ref, at, jnp.sum(d_norm * hat, axis=0, keepdims=True))
    at = lay_rows(tiny_ref, at, jnp.sum(d_norm, axis=0, keepdims=True))
    scaled = d_norm * line(gain_ref)
    cot = cot_ref[...].astype(F32)
    at = lay_rows(tiny_ref, at, jnp.sum(cot, axis=0, keepdims=True))
    d_middle = cot + rate * (
        scaled
        - jnp.mean(scaled, axis=-1, keepdims=True)
        - hat * jnp.mean(scaled * hat, axis=-1, keepdims=True)
    )
    d_middle_ref[...] = d_middle
    d_attended = d_middle.astype(BF)
    at = lay_rows(tiny_ref, at, jnp.sum(d_attended.astype(F32), axis=0, keepdims=True))
    d_ctx_full[...] = dot_nt(w_out_ref[...], d_attended).astype(BF)
    for k in range(GROUP):
        at = pl.multiple_of((chip ^ k) * part, part)
        ref = (back0, back1)[k % 2]
        ref[k // 2 * part : (k // 2 + 1) * part, :] = d_ctx_full[pl.ds(at, part), :]
    normed_t = normed.T
    quarter, mid = fan // 8, width // 2
    for b in range(width // LANES):
        d_att_f[b * LANES : (b + 1) * LANES, :] = d_attended[:, b * LANES : (b + 1) * LANES]
    early = LANES
    late = quarter - early
    for k, (first, second) in enumerate(zip((down0, down1, down2, down3), (up0, up1, up2, up3))):
        target = item ^ k
        for c in range(2):
            at = pl.multiple_of(c * (fan // 2) + target * quarter, quarter)
            first[c * quarter : (c + 1) * quarter, :] = active_t[pl.ds(at, quarter), :]
            to = 2 * quarter + width + c * early
            first[to : to + early, :] = d_hidden_f[pl.ds(at, early), :]
            at = pl.multiple_of(c * (fan // 2) + target * quarter + early, early)
            second[c * late : (c + 1) * late, :] = d_hidden_f[pl.ds(at, late), :]
            at = pl.multiple_of((2 * c + (target & 1)) * part, part)
            to = 2 * late + c * part
            second[to : to + part, :] = ctx_full[pl.ds(at, part), :]
        first[2 * quarter : 2 * quarter + width, :] = normed_t
        at = pl.multiple_of((target >> 1) * mid, mid)
        to = 2 * late + 2 * part
        second[to : to + mid, :] = d_att_f[pl.ds(at, mid), :]


ROUND = (0, 2, 1, 3)


def hand_out(chip, out_ref, at, size, grads):
    for z in range(GROUP):
        k = chip ^ z
        row = ((k >> 1) | ((k & 1) << 1)) * size
        here = at
        for grad in grads:
            share = grad.shape[0] // GROUP
            for b in range(grad.shape[1] // LANES):
                out_ref[pl.ds(pl.multiple_of(row + here, 16), share), :] = grad[
                    z * share : (z + 1) * share, b * LANES : (b + 1) * LANES
                ].astype(out_ref.dtype)
                here += share
    return here


def first_grad_kernel(place_ref, *refs):
    pieces, cots, kept_ref, given_ref = refs[:4], refs[4:8], refs[8], refs[9]
    down_left, down_right, up_left, up_right = refs[10:]
    chip, core = place_ref[0], place_ref[2]
    quarter, width, early = down_left.shape[0] // 2, up_left.shape[0], up_right.shape[1] // 2
    for s, piece in enumerate(pieces):
        span = slice(s * LANES, (s + 1) * LANES)
        down_left[:, span] = piece[: 2 * quarter, :]
        down_right[span, :] = cots[s][...]
        up_left[:, span] = piece[2 * quarter : 2 * quarter + width, :]
        for c in range(2 * early // LANES):
            low = 2 * quarter + width + c * LANES
            up_right[span, c * LANES : (c + 1) * LANES] = piece[low : low + LANES, :]
    size = kept_ref.shape[0] // GROUP
    for half, ref in ((1 - core, given_ref), (core, kept_ref)):
        rows = pl.ds(pl.multiple_of(half * quarter, quarter), quarter)
        cols = pl.ds(pl.multiple_of(half * early, early), early)
        grad_down = dot_nn(down_left[rows, :], down_right[...])
        at = hand_out(chip, ref, 0, size, (grad_down,))
        hand_out(chip, ref, at, size, (dot_nn(up_left[...], up_right[:, cols]),))


def second_grad_kernel(place_ref, *refs):
    firsts, pieces, kept_ref, given_ref = refs[:4], refs[4:8], refs[8], refs[9]
    up_left, up_right, out_left, out_right = refs[10:]
    chip, core = place_ref[0], place_ref[2]
    width, late = up_left.shape[0], up_right.shape[1] // 2
    part, mid = out_left.shape[0] // 2, out_right.shape[1]
    skip = firsts[0].shape[0] - width - 2 * LANES
    for s, piece in enumerate(pieces):
        span = slice(s * LANES, (s + 1) * LANES)
        up_left[:, span] = firsts[s][skip : skip + width, :]
        for b in range(2 * late // LANES):
            up_right[span, b * LANES : (b + 1) * LANES] = piece[b * LANES : (b + 1) * LANES, :]
        out_left[:, span] = piece[2 * late : 2 * late + 2 * part, :]
        for b in range(mid // LANES):
            low = 2 * late + 2 * part + b * LANES
            out_right[span, b * LANES : (b + 1) * LANES] = piece[low : low + LANES, :]
    size = kept_ref.shape[0] // GROUP
    for half, ref in ((1 - core, given_ref), (core, kept_ref)):
        rows = pl.ds(pl.multiple_of(half * part, part), part)
        cols = pl.ds(pl.multiple_of(half * late, late), late)
        at = hand_out(chip, ref, 0, size, (dot_nn(up_left[...], up_right[:, cols]),))
        hand_out(chip, ref, at, size, (dot_nn(out_left[rows, :], out_right[...]),))


def head_grad_kernel(
    place_ref, dq_ref, dkv_ref, far_ref, hat0, hat1, gain_ref, shift_ref, wq_hbm, wk_hbm, wv_hbm,
    back0, back1, kept_ref, given_ref, tiny_ref,
    d_heads, normed, grad, padded, window, sems,
):
    chip, core = place_ref[0], place_ref[2]
    part, tokens = dq_ref.shape
    width = normed.shape[1]
    wide = padded.shape[1]
    off = pl.multiple_of((chip & 1) * HD, HD)
    begin = pl.multiple_of(chip * part - off, LANES)
    copies = [
        pltpu.make_async_copy(w.at[:, pl.ds(begin, wide)], window.at[n], sems.at[n])
        for n, w in enumerate((wq_hbm, wk_hbm, wv_hbm))
    ]
    for copy in copies:
        copy.start()
    d_heads[:part, :] = dq_ref[...]
    d_heads[part:, :] = (dkv_ref[...] + far_ref[...].astype(F32)).astype(BF)
    padded[...] = jnp.zeros(padded.shape, BF)
    for n in range(3):
        padded[n, pl.ds(off, part), :] = d_heads[n * part : (n + 1) * part, :]
    hats = [((hat0, hat1)[k % 2], k // 2 * LANES) for k in range(GROUP)]
    for k, (hat, at) in enumerate(hats):
        span = slice(k * LANES, (k + 1) * LANES)
        back, row = (back0, back1)[k % 2], k // 2 * 3 * part
        back[row : row + 3 * part, :] = d_heads[:, span]
        rows = hat[at : at + LANES, :].astype(F32) * line(gain_ref) + line(shift_ref)
        normed[span, :] = rows.astype(BF)
    grad[...] = dot_nn(d_heads[...], normed[...])
    mid, rows = width // 2, 3 * part // GROUP
    for b in range(mid // LANES):
        mine = grad[:, pl.ds(pl.multiple_of(core * mid + b * LANES, LANES), LANES)]
        theirs = grad[:, pl.ds(pl.multiple_of((1 - core) * mid + b * LANES, LANES), LANES)]
        for q in range(GROUP):
            at = (q * (mid // LANES) + b) * rows
            kept_ref[at : at + rows, :] = mine[q * rows : (q + 1) * rows, :]
            given_ref[at : at + rows, :] = theirs[q * rows : (q + 1) * rows, :].astype(BF)
    for copy in copies:
        copy.wait()
    turned = [padded[n].T for n in range(3)]
    gain_grad = jnp.zeros((1, width), F32)
    shift_grad = jnp.zeros((1, width), F32)
    for k, (hat, at) in enumerate(hats):
        span = slice(k * LANES, (k + 1) * LANES)
        d_norm = dot_nt(turned[0][span, :], window[0])
        d_norm = d_norm + dot_nt(turned[1][span, :], window[1])
        d_norm = d_norm + dot_nt(turned[2][span, :], window[2])
        rows = hat[at : at + LANES, :].astype(F32)
        gain_grad = gain_grad + jnp.sum(d_norm * rows, axis=0, keepdims=True)
        shift_grad = shift_grad + jnp.sum(d_norm, axis=0, keepdims=True)
    at = lay_rows(tiny_ref, 0, gain_grad)
    at = lay_rows(tiny_ref, at, shift_grad)
    ones = jnp.ones((8, tokens), BF)
    for n in (0, 2):
        sums = dot_nt(ones, padded[n])
        for r in range(width // LANES):
            value = jnp.zeros((1, LANES), F32)
            for m in range(wide // LANES):
                here = sums[:1, m * LANES : (m + 1) * LANES]
                value = value + jnp.where(begin == (r - m) * LANES, here, 0.0)
            tiny_ref[at : at + 1, :] = value
            at += 1


def input_grad_kernel(
    place_ref, back0, back1, back2, wq_hbm, wk_hbm, wv_hbm, tokens_ref, d_middle_ref,
    gain_ref, grad_ref, held, turned, sems,
):
    chip = place_ref[0]
    rows, width = tokens_ref.shape
    part = width // GROUP
    copies = [
        pltpu.make_async_copy(ref, held.at[n], sems.at[n])
        for n, ref in enumerate((wq_hbm, wk_hbm, wv_hbm))
    ]
    for copy in copies:
        copy.start()
    for k, ref in enumerate((back0, back1, back2, back2)):
        base = 3 * part if k == 3 else 0
        for n in range(3):
            at = pl.multiple_of(n * width + (chip ^ k) * part, part)
            turned[pl.ds(at, part), :] = ref[base + n * part : base + (n + 1) * part, :]
    d_norm = jnp.zeros((width, rows), F32)
    for n, copy in enumerate(copies):
        copy.wait()
        d_norm = d_norm + dot_nn(held[n], turned[n * width : (n + 1) * width, :])
    d_norm = d_norm.T
    hat, rate = norm_parts(tokens_ref[...].astype(F32))
    scaled = d_norm * line(gain_ref)
    d_inputs = rate * (
        scaled
        - jnp.mean(scaled, axis=-1, keepdims=True)
        - hat * jnp.mean(scaled * hat, axis=-1, keepdims=True)
    )
    grad_ref[...] = (d_middle_ref[...] + d_inputs).astype(BF)


def fetch_halves(size, used, halves, came, sems):
    copies = {}
    for n, half in enumerate(halves):
        for s in range(2):
            copy = pltpu.make_async_copy(
                half.at[s * size : s * size + used], came.at[n // 2, n % 2, s], sems.at[n // 2, n % 2, s]
            )
            copy.start()
            copies[n // 2, n % 2, s] = copy
    return copies


def put_halves(layout, which, place_ref, copies, came, boxes, targets, sems):
    chip, item, core = place_ref[0], place_ref[1], place_ref[2]
    leaving = []
    for piece, (flip, step) in enumerate(which):
        side, place = core ^ flip, item ^ step
        known = {"eighth": side * GROUP + place, "row": 2 * side + (place & 1), "column": place >> 1}
        for k in range(GROUP):
            h, s = k % 2, k // 2
            copies[piece, h, s].wait()
            at = 0
            for (share, blocks, *_), box in zip(layout, boxes):
                to = pl.multiple_of((chip ^ k) * share, share)
                for b in range(blocks):
                    box[piece, pl.ds(to, share), b * LANES : (b + 1) * LANES] = came[
                        piece, h, s, at : at + share, :
                    ].astype(F32)
                    at += share
        for n, (share, blocks, row, column, unit, first) in enumerate(layout):
            tall, wide = GROUP * share, blocks * LANES
            target = targets[n]
            if row is not None:
                start = pl.multiple_of(known[row] * tall, tall)
                target = target.at[pl.ds(start, tall), :]
            if column is not None:
                start = pl.multiple_of(known[column] * unit + first, LANES)
                target = target.at[:, pl.ds(start, wide)]
            copy = pltpu.make_async_copy(boxes[n].at[piece], target, sems.at[piece, n])
            copy.start()
            leaving.append(copy)
    return leaving


def put_pieces_kernel(layout, size, which, place_ref, *refs):
    outs = len(layout)
    halves = refs[: 2 * len(which)]
    came, in_sems, out_sems = refs[-3:]
    boxes = refs[-3 - outs : -3]
    done = refs[-4 - outs]
    targets = refs[-4 - 2 * outs : -4 - outs]
    done[...] = jnp.zeros(done.shape, F32)
    copies = fetch_halves(size, came.shape[3], halves, came, in_sems)
    for copy in put_halves(layout, which, place_ref, copies, came, boxes, targets, out_sems):
        copy.wait()


def fetch_heads(size, skip, place_ref, flip, halves, whole, sems):
    chip, item = place_ref[0], place_ref[1]
    part = whole.shape[1] // (3 * GROUP)
    rows = 3 * part // GROUP
    copies = []
    for k in range(GROUP):
        for z in range(GROUP):
            to = pl.multiple_of((chip ^ z) * (3 * part) + (item ^ k) * rows, 16)
            for b in range(whole.shape[2] // LANES):
                at = z // 2 * size + skip + b * rows
                copy = pltpu.make_async_copy(
                    halves[2 * k + z % 2].at[at : at + rows],
                    whole.at[flip, pl.ds(to, rows), b * LANES : (b + 1) * LANES],
                    sems.at[flip, k, z, b],
                )
                copy.start()
                copies.append(copy)
    return copies


def put_heads(place_ref, flip, copies, whole, held, targets, sems):
    mid = whole.shape[2]
    part = whole.shape[1] // (3 * GROUP)
    for copy in copies:
        copy.wait()
    leaving = []
    for b in range(mid // LANES):
        start = pl.multiple_of((place_ref[2] ^ flip) * mid + b * LANES, LANES)
        for n, target in enumerate(targets):
            tall = jnp.concatenate(
                [
                    whole[
                        flip,
                        z * 3 * part + n * part : z * 3 * part + (n + 1) * part,
                        b * LANES : (b + 1) * LANES,
                    ]
                    for z in range(GROUP)
                ],
                axis=0,
            )
            held[flip, n, b] = tall.T.astype(F32)
            copy = pltpu.make_async_copy(
                held.at[flip, n, b], target.at[pl.ds(start, LANES), :], sems.at[flip, n, b]
            )
            copy.start()
            leaving.append(copy)
    return leaving


def put_rest_kernel(layout, size, skip, which, place_ref, *refs):
    halves, targets, heads_out, done, boxes = refs[:16], refs[19:21], refs[21:24], refs[24], refs[25:27]
    came, whole, held, in_sems, head_sems, out_sems, head_out_sems = refs[27:]
    done[...] = jnp.zeros(done.shape, F32)
    chosen = [halves[2 * (GROUP * flip + k) + h] for flip, k in which for h in range(2)]
    copies = fetch_halves(size, skip, chosen, came, in_sems)
    heads = [
        fetch_heads(size, skip, place_ref, flip, halves[8 * flip : 8 * flip + 8], whole, head_sems)
        for flip in range(2)
    ]
    leaving = put_halves(layout, which, place_ref, copies, came, boxes, targets, out_sems)
    for flip in range(2):
        leaving += put_heads(place_ref, flip, heads[flip], whole, held, heads_out, head_out_sems)
    for copy in leaving:
        copy.wait()


def put_pieces(layout, size, which, shapes, places, halves, flags, sofar, name):
    count, outs = len(which), len(layout)
    filled = [value for value in sofar if value is not None]
    kept = [n for n, value in enumerate(sofar) if value is not None]
    used = sum(share * blocks for share, blocks, *_ in layout)
    anywhere = pl.BlockSpec(memory_space=pl.ANY)
    before = 1 + 2 * count + len(flags)
    return pl.pallas_call(
        functools.partial(put_pieces_kernel, layout, size, which),
        in_specs=[pl.BlockSpec(memory_space=pltpu.SMEM)]
        + [anywhere] * (2 * count)
        + vmem(len(flags))
        + [anywhere] * len(filled),
        out_specs=[anywhere] * outs + vmem(1),
        out_shape=[jax.ShapeDtypeStruct(shape, F32) for shape in shapes]
        + [jax.ShapeDtypeStruct((8, LANES), F32)],
        scratch_shapes=[
            pltpu.VMEM((count, GROUP * share, blocks * LANES), F32)
            for share, blocks, *_ in layout
        ]
        + [
            pltpu.VMEM((count, 2, 2, used, LANES), BF),
            pltpu.SemaphoreType.DMA((count, 2, 2)),
            pltpu.SemaphoreType.DMA((count, outs)),
        ],
        input_output_aliases={before + i: n for i, n in enumerate(kept)},
        compiler_params=params(),
        cost_estimate=LIGHT,
        name=name,
    )(places, *halves, *flags, *filled)


PLAN = {
    'project': (0, 0),
    'q1': (2, 2),
    'q2': (2, 2),
    'q3': (2, 2),
    'mult': (2, 2),
    'd_active': (2, 2),
    'kv0': (4, 4),
    'kv1': (4, 4),
    'kv2': (5, 5),
    'kv3': (4, 4),
    'cot1': (4, 8),
    'cot2': (4, 8),
    'cot3': (4, 8),
    'norm_near': (4, 6),
    'attend': (6, 6),
    'ctx1': (8, 8),
    'ctx2': (8, 8),
    'ctx3': (8, 8),
    'middle': (10, 10),
    'a1': (12, 12),
    'a2': (12, 12),
    'a3': (12, 12),
    'dc1': (12, 12),
    'dc2': (12, 12),
    'norm_far': (10, 10),
    'layer_out': (13, 15),
    'b1': (13, 15),
    'b2': (13, 15),
    'b3': (13, 15),
    'first_grad': (14, 14),
    'one_core': (14, 14),
    'one_z1': (15, 15),
    'attend_back': (12, 12),
    'far': (14, 14),
    'one_z2': (16, 16),
    'second_grad': (16, 16),
    'two_core': (17, 17),
    'head_grad': (15, 15),
    'head_core': (15, 15),
    'head_x': (16, 16),
    'head_y': (16, 16),
    'head_d': (16, 16),
    'head_sum': (17, 17),
    'two_z1': (18, 18),
    'one_near': (17, 18),
    'two_z2': (20, 20),
    'one_far': (20, 20),
    'one_nx': (20, 20),
    'one_ny': (20, 20),
    'two_near': (22, 22),
    'one_fx': (22, 22),
    'one_fy': (22, 22),
    'back_z1': (17, 18),
    'two_far': (24, 24),
    'two_nx': (24, 24),
    'two_ny': (24, 24),
    'one_nd': (25, 26),
    'one_fd': (25, 26),
    'back_z2': (24, 25),
    'two_fx': (25, 26),
    'two_fy': (25, 26),
    'input_grad': (26, 26),
    'tiny_core': (17, 18),
    'two_nd': (28, 28),
    'two_fd': (28, 28),
    'tiny_x': (22, 25),
    'tiny_y': (28, 99),
    'tiny_z1': (18, 20),
    'tiny_z2': (20, 22),
    'one_all': (17, 18),
    'put_own': (25, 25),
    'put_rest': (28, 28),
    'put_two': (32, 99),
    'one_cn0': (22, 24),
    'one_cf0': (25, 26),
    'two_cn0': (26, 28),
    'two_cf0': (26, 28),
    'one_cn1': (22, 24),
    'one_cf1': (25, 26),
    'two_cn1': (26, 28),
    'two_cf1': (28, 30),
    'one_cn2': (22, 24),
    'one_cf2': (25, 26),
    'two_cn2': (26, 28),
    'two_cf2': (28, 30),
    'one_cn3': (28, 28),
    'one_cf3': (28, 28),
    'two_cn3': (28, 30),
    'two_cf3': (30, 30),
}


def run_steps(steps, known):
    stage, last = {}, {}

    def named(name):
        return [source.lstrip("!").partition(".")[0] for source in steps[name][0]]

    def settle(name):
        if name in stage:
            return stage[name]
        first, wait = PLAN[name]
        for source in named(name):
            if source in steps:
                first = max(first, settle(source))
        stage[name], last[name] = first, max(first, wait)
        return first

    for name in steps:
        settle(name)
    depth = {}

    def deep(name):
        if name not in depth:
            depth[name] = 1 + max([deep(s) for s in named(name) if s in steps], default=0)
        return depth[name]

    for name in steps:
        deep(name)
    made, now, waiting = dict(known), 0, []
    order = sorted(steps, key=lambda n: (stage[n], depth[n]))

    def pick(source):
        base, _, index = source.lstrip("!").partition(".")
        return (base, int(index)) if index else (base, None)

    def turn(following):
        ending = [n for n in waiting if last[n] < following]
        keys = set()
        for n in ending:
            many = isinstance(made[n], (list, tuple))
            if n.startswith("put_"):
                keys.add((n, len(made[n]) - 1))
            elif many:
                keys.update((n, i) for i in range(len(made[n])))
            else:
                keys.add((n, None))
        for n in order:
            if stage[n] == following:
                keys.update(
                    pick(s) for s in steps[n][0] if not s.startswith("!") and pick(s)[0] in made
                )
        keys = sorted(keys, key=str)
        values = [made[n] if i is None else made[n][i] for n, i in keys]
        for (n, i), value in zip(keys, lax.optimization_barrier(values)):
            if i is None:
                made[n] = value
            else:
                made[n] = [value if j == i else old for j, old in enumerate(made[n])]
        return [n for n in waiting if n not in ending]

    for name in order:
        if now < stage[name]:
            waiting, now = turn(stage[name]), stage[name]
        sources, function = steps[name]
        inputs = []
        for source in sources:
            base, index = pick(source)
            inputs.append(made[base] if index is None else made[base][index])
        made[name] = function(*inputs)
        waiting.append(name)
    return made


def split_device(
    tokens,
    rand_blocks,
    w_query,
    w_key,
    w_value,
    w_out,
    w_up,
    w_down,
    bias_query,
    bias_value,
    bias_out,
    bias_up,
    bias_down,
    attn_gain,
    attn_shift,
    ffn_gain,
    ffn_shift,
    cotangent,
):
    _, local_len, width = tokens.shape
    fan = w_up.shape[1]
    blocks_all = rand_blocks.shape[0]
    position, item = lax.axis_index("seq"), lax.axis_index("item")
    chip, core = position // 2, position % 2
    heads = HEADS // GROUP
    part = heads * HD
    all_len = GROUP * local_len
    quarter, mid = fan // 8, width // 2
    early = LANES
    late = quarter - early
    places = jnp.stack([chip, item, core]).astype(jnp.int32)
    smem = [pl.BlockSpec(memory_space=pltpu.SMEM)]
    anywhere = [pl.BlockSpec(memory_space=pl.ANY)]
    shaped = jax.ShapeDtypeStruct

    first_rows = 2 * quarter + width + 2 * early
    second_rows = 2 * late + 2 * part + mid
    tiny_rows = (fan + 4 * width) // LANES
    size = 3 * part
    rows_one = (quarter * width + width * early) // LANES
    rows_two = (width * late + part * mid) // LANES
    rows_three = size * mid // LANES
    half_one, half_two = rows_one // 2, rows_two // 2

    def kernel(body, ins, outs, scratch=(), name=None):
        return pl.pallas_call(
            body,
            in_specs=ins,
            out_specs=vmem(len(outs)),
            out_shape=list(outs),
            scratch_shapes=list(scratch),
            compiler_params=params(),
            cost_estimate=LIGHT,
            name=name,
        )

    box = lambda *dims: pltpu.VMEM(dims, BF)
    box32 = lambda *dims: pltpu.VMEM(dims, F32)
    sems = lambda n: pltpu.SemaphoreType.DMA((n,))

    def project(x):
        return kernel(
            project_kernel,
            smem + vmem(1) + anywhere * 3 + vmem(4),
            [shaped((local_len, width), BF)] + [shaped((size, local_len), BF)] * 4,
            [box(3, width, width), box(3 * width, local_len), sems(3)],
            "project",
        )(places, x, w_query, w_key, w_value, bias_query, bias_value, attn_gain, attn_shift)

    def multiplicity(rand):
        return kernel(
            functools.partial(mult_kernel, heads, blocks_all),
            smem * 2,
            [shaped((heads, 2 * all_len // BLOCK, all_len), F32)],
            name="multiplicity",
        )(places, rand.reshape(-1))[0]

    def attend(*ins):
        return kernel(
            functools.partial(attend_kernel, heads),
            vmem(9),
            [shaped((part, local_len), BF)] * 4
            + [shaped((part, all_len), F32), shaped((heads, 1, all_len), F32)],
            name="attend",
        )(*ins)

    def middle_step(ctx0, ctx1, ctx2, ctx3, d_active, cot):
        outs = kernel(
            middle_kernel,
            smem + vmem(5) + anywhere + vmem(3) + anywhere + vmem(1) + anywhere + vmem(1),
            [shaped((first_rows, LANES), BF)] * 4
            + [shaped((second_rows, LANES), BF)] * 4
            + [shaped((2 * part, local_len), BF)] * 2
            + [
                shaped((local_len, width), F32),
                shaped((local_len, fan), BF),
                shaped((local_len, width), F32),
                shaped((tiny_rows, LANES), F32),
            ],
            [box(width, local_len), box(fan, local_len), box(fan, local_len)]
            + [box(width, local_len)] * 2
            + [box(width, width), box(width, fan), box32(local_len, fan)]
            + [sems(1 + 2 * (fan // width))],
            "middle",
        )(
            places, tokens[0], ctx0, ctx1, ctx2, ctx3, w_out, bias_out, ffn_gain, ffn_shift,
            w_up, bias_up, d_active, cot,
        )
        return outs

    def attend_back(*ins):
        return kernel(
            functools.partial(attend_back_kernel, heads),
            vmem(14),
            [
                shaped((part, all_len), BF),
                shaped((2 * part, all_len), F32),
                shaped((2 * part, all_len), BF),
            ],
            name="attend_back",
        )(*ins)

    def first_grad(*ins):
        return kernel(
            first_grad_kernel,
            smem + vmem(8),
            [shaped((rows_one, LANES), F32), shaped((rows_one, LANES), BF)],
            [
                box(2 * quarter, all_len),
                box(all_len, width),
                box(width, all_len),
                box(all_len, 2 * early),
            ],
            "first_grad",
        )(places, *ins)

    def second_grad(*ins):
        return kernel(
            second_grad_kernel,
            smem + vmem(8),
            [shaped((rows_two, LANES), F32), shaped((rows_two, LANES), BF)],
            [
                box(width, all_len),
                box(all_len, 2 * late),
                box(2 * part, all_len),
                box(all_len, mid),
            ],
            "second_grad",
        )(places, *ins)

    def head_grad(*ins):
        return kernel(
            head_grad_kernel,
            smem + vmem(7) + anywhere * 3,
            [shaped((2 * size, local_len), BF)] * 2
            + [shaped((rows_three, LANES), F32), shaped((rows_three, LANES), BF)]
            + [shaped((4 * width // LANES, LANES), F32)],
            [
                box(size, all_len),
                box(all_len, width),
                box32(size, width),
                box(3, part + HD, all_len),
                box(3, width, part + HD),
                sems(3),
            ],
            "head_grad",
        )(places, *ins, attn_gain, attn_shift, w_query, w_key, w_value)

    def input_grad(own, came, far, d_middle):
        return kernel(
            input_grad_kernel,
            smem + vmem(3) + anywhere * 3 + vmem(3),
            [shaped((local_len, width), BF)],
            [box(3, width, width), box(3 * width, local_len), sems(3)],
            "input_grad",
        )(
            places, own, came, far, w_query, w_key, w_value, tokens[0], d_middle, attn_gain
        )[0]

    layout_one = (
        (quarter // GROUP, width // LANES, "eighth", None, 0, 0),
        (width // GROUP, early // LANES, None, "eighth", quarter, 0),
    )
    layout_two = (
        (width // GROUP, late // LANES, None, "eighth", quarter, early),
        (part // GROUP, mid // LANES, "row", "column", mid, 0),
    )
    size_one, size_two = (rows_one + rows_three) // GROUP, rows_two // GROUP
    shapes_one, shapes_two = ((fan, width), (width, fan)), ((width, fan), (width, width))

    own_three = tuple((0, k) for k in range(3))
    the_rest = ((0, 3), *((1, k) for k in range(GROUP)))
    every = tuple((flip, k) for flip in range(2) for k in range(GROUP))

    def put_own(*halves):
        return put_pieces(
            layout_one, size_one, own_three, shapes_one, places, halves, (), (None, None), "put_own"
        )

    def put_rest(*ins):
        skip = rows_one // GROUP
        return pl.pallas_call(
            functools.partial(put_rest_kernel, layout_one, size_one, skip, the_rest),
            in_specs=smem + anywhere * 16 + vmem(1) + anywhere * 2,
            out_specs=anywhere * 5 + vmem(1),
            out_shape=[shaped(shape, F32) for shape in shapes_one]
            + [shaped((width, width), F32)] * 3
            + [shaped((8, LANES), F32)],
            scratch_shapes=[
                box32(len(the_rest), GROUP * share, blocks * LANES)
                for share, blocks, *_ in layout_one
            ]
            + [
                box(len(the_rest), 2, 2, skip, LANES),
                box(2, 3 * width, mid),
                box32(2, 3, mid // LANES, LANES, width),
                pltpu.SemaphoreType.DMA((len(the_rest), 2, 2)),
                pltpu.SemaphoreType.DMA((2, GROUP, GROUP, mid // LANES)),
                pltpu.SemaphoreType.DMA((len(the_rest), 2)),
                pltpu.SemaphoreType.DMA((2, 3, mid // LANES)),
            ],
            input_output_aliases={18: 0, 19: 1},
            compiler_params=params(),
            cost_estimate=LIGHT,
            name="put_rest",
        )(places, *ins)

    def put_two(*ins):
        return put_pieces(
            layout_two, size_two, every, shapes_two, places, ins[:16], ins[16:17], (ins[17], None),
            "put_two",
        )

    def rows_of(grad_t, k):
        blocks = grad_t.reshape(GROUP, rows_three // GROUP, LANES)
        return lax.dynamic_index_in_dim(blocks, item ^ k, 0, False)

    def head_sum(grad_t, x, y, d):
        total = rows_of(grad_t, 0) + x.astype(F32) + (y.astype(F32) + d.astype(F32))
        return total.astype(BF)

    def last_sum(pair, far):
        share = pair.shape[0] // 2
        return (pair[:share] + far.astype(F32)).astype(BF)

    def second_half(pair):
        return pair[pair.shape[0] // 2 :].astype(BF)

    below = lambda *parts: jnp.concatenate(parts, axis=0)
    cot = cotangent[0]
    todo = {
        "project": (("tokens",), project),
        "mult": (("rand",), multiplicity),
        "d_active": (("cot",), lambda c: dense_back(c, w_down)),
    }
    for k in range(1, GROUP):
        todo[f"q{k}"] = ((f"project.{k + 1}",), functools.partial(over_z, step=k))
        todo[f"cot{k}"] = (("cot",), functools.partial(over_item, step=k))
        todo[f"ctx{k}"] = ((f"attend.{k}",), functools.partial(over_z, step=k))
    own = ["project.1", "q1", "q2", "q3"]
    for k in range(GROUP):
        todo[f"kv{k}"] = ((own[k],), lambda v: over_core(v[part:]))
    other = [f"kv{k}" for k in range(GROUP)]
    todo["attend"] = ((*own, *other, "mult"), attend)
    todo["norm_near"] = (("project.0",), lambda v: below(v, over_z(v, 2)))
    todo["norm_far"] = (("norm_near",), lambda v: over_z(v, 1))
    todo["middle"] = (("attend.0", "ctx1", "ctx2", "ctx3", "d_active", "cot"), middle_step)
    todo["layer_out"] = (
        ("middle.10", "middle.11"),
        lambda m, a: (m + dense_rows(a, w_down) + bias_down).astype(BF),
    )
    for k in range(1, GROUP):
        todo[f"a{k}"] = ((f"middle.{k}",), functools.partial(over_item, step=k))
        todo[f"b{k}"] = ((f"middle.{4 + k}",), functools.partial(over_item, step=k))
    todo["dc1"] = (("middle.9",), lambda v: over_z(v, 1))
    todo["dc2"] = (("middle.8", "dc1"), lambda v, c: over_z(below(v[part:], c[part:]), 2))
    firsts = ["middle.0", "a1", "a2", "a3"]
    seconds = ["middle.4", "b1", "b2", "b3"]
    todo["first_grad"] = ((*firsts, "cot", "cot1", "cot2", "cot3"), first_grad)
    def pair_up(half, kept, given):
        far = over_z((kept[half:] + given[half:].astype(F32)).astype(BF), 1)
        return kept[:half] + given[:half].astype(F32) + far.astype(F32)

    todo["one_core"] = (("first_grad.1",), over_core)
    todo["one_z1"] = (
        ("first_grad.0", "one_core"),
        functools.partial(pair_up, half_one),
    )
    todo["one_z2"] = (("one_z1",), lambda v: last_sum(v, over_z(second_half(v), 2)))
    todo["attend_back"] = (
        (*own, *other, "mult", "attend.4", "attend.5", "middle.8", "dc1", "dc2"),
        attend_back,
    )
    todo["far"] = (("attend_back.2",), over_core)
    todo["second_grad"] = ((*firsts, *seconds), second_grad)
    todo["two_core"] = (("second_grad.1",), over_core)
    todo["two_z1"] = (
        ("second_grad.0", "two_core"),
        functools.partial(pair_up, half_two),
    )
    todo["head_grad"] = (
        ("attend_back.0", "attend_back.1", "far", "norm_near", "norm_far"),
        head_grad,
    )
    todo["head_core"] = (("head_grad.2", "head_grad.3"), lambda k, g: k + over_core(g).astype(F32))
    for k, name in enumerate("xyd"):
        todo[f"head_{name}"] = (
            ("head_core",),
            lambda v, k=k + 1: over_item(rows_of(v, k).astype(BF), k),
        )
    todo["head_sum"] = (("head_core", "head_x", "head_y", "head_d"), head_sum)
    todo["two_z2"] = (("two_z1",), lambda v: last_sum(v, over_z(second_half(v), 2)))
    todo["one_all"] = (("one_z2", "head_sum"), below)
    pieces = {}
    for name, total in (("one", "one_all"), ("two", "two_z2")):
        todo[f"{name}_near"] = ((total,), lambda v: below(v, over_z(v, 2)))
        todo[f"{name}_far"] = ((f"{name}_near",), lambda v: over_z(v, 1))
        todo[f"{name}_nx"] = ((f"{name}_near",), lambda v: over_item(v, 1))
        todo[f"{name}_ny"] = ((f"{name}_near",), lambda v: over_item(v, 2))
        todo[f"{name}_fx"] = ((f"{name}_far",), lambda v: over_item(v, 1))
        todo[f"{name}_fy"] = ((f"{name}_far",), lambda v: over_item(v, 2))
        todo[f"{name}_nd"] = ((f"{name}_nx",), lambda v: over_item(v, 2))
        todo[f"{name}_fd"] = ((f"{name}_fy",), lambda v: over_item(v, 1))
        flat = []
        for k, end in enumerate(("", "x", "y", "d")):
            halves = ("near", "far") if k == 0 else ("n" + end, "f" + end)
            halves = [f"{name}_{h}" for h in halves]
            flat += halves
            todo[f"{name}_cn{k}"] = (tuple(halves[:1]), over_core)
            todo[f"{name}_cf{k}"] = (tuple(halves[1:]), over_core)
        mirrored = [f"{name}_c{h}{k}" for k in range(GROUP) for h in "nf"]
        pieces[name] = (flat, mirrored)
    own_one, mirrored_one = pieces["one"]
    todo["put_own"] = (tuple(own_one[:6]), put_own)
    todo["put_rest"] = (
        (*own_one, *mirrored_one, "put_own.2", "!put_own.0", "!put_own.1"),
        put_rest,
    )
    todo["put_two"] = (
        (*pieces["two"][0], *pieces["two"][1], "put_rest.5", "!put_rest.1"),
        put_two,
    )
    todo["back_z1"] = (("head_grad.1",), lambda v: over_z(v, 1))
    todo["back_z2"] = (
        ("head_grad.0", "back_z1"),
        lambda v, c: over_z(below(v[size:], c[size:]), 2),
    )
    todo["input_grad"] = (
        ("head_grad.0", "back_z1", "back_z2", "middle.12"),
        input_grad,
    )
    todo["tiny_core"] = (
        ("middle.13", "head_grad.4"),
        lambda u, v: below(u, v) + over_core(below(u, v)),
    )
    todo["tiny_z1"] = (("tiny_core",), lambda v: v + over_z(v, 1))
    todo["tiny_z2"] = (("tiny_z1",), lambda v: v + over_z(v, 2))
    todo["tiny_x"] = (("tiny_z2",), lambda v: v + over_item(v, 1))
    todo["tiny_y"] = (("tiny_x",), lambda v: v + over_item(v, 2))
    made = run_steps(
        todo, {"tokens": tokens[0], "rand": rand_blocks, "cot": cot}
    )
    tiny = made["tiny_y"]
    layer_out, grad_tokens = made["layer_out"], made["input_grad"]
    grad_down, grad_qkv = made["put_rest"][0], made["put_rest"][2:5]
    grad_up, grad_out, _ = made["put_two"]
    tiny = tiny.reshape(-1)
    cuts, at = [], 0
    for size in (fan,) + (width,) * 8:
        cuts.append(tiny[at : at + size])
        at += size
    g_bu, g_fg, g_fs, g_bd, g_bo, g_ag, g_as, g_bq, g_bv = cuts
    return (
        layer_out[None],
        grad_tokens[None],
        grad_qkv[0],
        grad_qkv[1],
        grad_qkv[2],
        grad_out,
        grad_up,
        grad_down,
        g_bq,
        g_bv,
        g_bo,
        g_bu,
        g_bd,
        g_ag,
        g_as,
        g_fg,
        g_fs,
    )


def per_device(tokens, rand_blocks, *rest):
    seqs, local_len, width = tokens.shape
    fan = rest[4].shape[1]
    fits = (
        seqs == 1
        and local_len == LANES
        and lax.axis_size("item") == GROUP
        and lax.axis_size("seq") == 2 * GROUP
        and HEADS % GROUP == 0
        and width == HEADS * HD
        and fan % (8 * LANES) == 0
        and width % (2 * LANES) == 0
    )
    chosen = split_device if fits else general_device
    return chosen(tokens, rand_blocks, *rest)


def solution(mesh):
    placed = (
        P("item", "seq", None),
        P(None, "item", None, None),
        P(),
        P(),
        P(),
        P(),
        P(),
        P(),
        P(),
        P(),
        P(),
        P(),
        P(),
        P(),
        P(),
        P(),
        P(),
        P("item", "seq", None),
    )
    return jax.shard_map(
        per_device,
        mesh=mesh,
        in_specs=placed,
        out_specs=(
            P("item", "seq", None),
            P("item", "seq", None),
            P(),
            P(),
            P(),
            P(),
            P(),
            P(),
            P(),
            P(),
            P(),
            P(),
            P(),
            P(),
            P(),
            P(),
            P(),
        ),
        check_vma=False,
    )
```

```python
import functools

import jax
import jax.numpy as jnp
from jax import lax
from jax.experimental import pallas as pl
from jax.experimental.pallas import tpu as pltpu
from jax.sharding import PartitionSpec as P

HEADS = 12
HD = 64
BLOCK = 64
RAND = 3


epsilon = 1e-05


def from_root(shard, axis, root):
    mine = lax.axis_index(axis) == root
    return lax.psum(jnp.where(mine, shard, jnp.zeros_like(shard)), axis)


def extended(block, sides, width):
    for axis, dim in sides:
        count = lax.axis_size(axis)
        forward = [(i, i + 1) for i in range(count - 1)]
        backward = [(target, source) for source, target in forward]
        low = lax.ppermute(
            lax.slice_in_dim(block, block.shape[dim] - width, None, axis=dim), axis, forward
        )
        high = lax.ppermute(lax.slice_in_dim(block, 0, width, axis=dim), axis, backward)
        block = jnp.concatenate([low, block, high], axis=dim)
    return block


def joined(shard, axis, join):
    gathered = jax.tree.map(
        lambda a, kind: lax.all_gather(a.astype(kind), axis),
        shard,
        (jnp.bfloat16, jnp.bfloat16, jnp.bfloat16),
    )

    def take(source):
        return jax.tree.map(
            lambda a, own: lax.dynamic_index_in_dim(a, source, 0, False).astype(own.dtype),
            gathered,
            shard,
        )

    return lax.fori_loop(
        1, lax.axis_size(axis), lambda source, state: join(state, take(source)), take(0)
    )


def entering(shard, axis, combine, identity, reverse):
    count, position = (lax.axis_size(axis), lax.axis_index(axis))
    everything = jax.tree.map(
        lambda part, kind: lax.all_gather(part.astype(kind), axis),
        shard,
        jax.tree.map(lambda a: jnp.bfloat16 if a.dtype == jnp.float32 else a.dtype, shard),
    )
    start = jax.tree.map(
        lambda part, zero: jnp.broadcast_to(jnp.asarray(zero, part.dtype), part.shape),
        shard,
        identity,
    )

    def step(k, before):
        at = count - 1 - k if reverse else k
        reached = at > position if reverse else at < position
        new = combine(
            before, jax.tree.map(lambda part, own: part[at].astype(own.dtype), everything, shard)
        )
        return jax.tree.map(lambda a, b: jnp.where(reached, a, b), new, before)

    return lax.fori_loop(0, count, step, start)


def layer_norm(values, norm_gain, norm_bias):
    center = values - jnp.mean(values, axis=-1, keepdims=True)
    spread = jnp.mean(center * center, axis=-1, keepdims=True)
    return center * lax.rsqrt(spread + epsilon) * norm_gain + norm_bias


def gelu_exact(values):
    return jax.nn.gelu(values, approximate=False)


def dense_rows(left, right):
    return jnp.dot(left, right, preferred_element_type=jnp.float32)


def dense_left(left, right):
    return lax.dot_general(
        left, right, (((0,), (0,)), ((), ())), preferred_element_type=jnp.float32
    )


def dense_back(left, right):
    return lax.dot_general(
        left, right, (((1,), (1,)), ((), ())), preferred_element_type=jnp.float32
    )


def mixed_sum(form, left, right):
    return jnp.einsum(form, left, right, preferred_element_type=jnp.float32)


def exact_sum(form, left, right):
    return jnp.einsum(
        form, left, right, precision=lax.Precision.HIGHEST, preferred_element_type=jnp.float32
    )


def from_ends(first_part, last_part):
    head_part = from_root(first_part, "seq", 0)
    tail_part = from_root(last_part, "seq", lax.axis_size("seq") - 1)
    return (head_part, tail_part)


def merge_rows(left_part, right_part):
    left_peak, left_total, left_sum = left_part
    right_peak, right_total, right_sum = right_part
    new_peak = jnp.maximum(left_peak, right_peak)
    left_scale = jnp.exp(left_peak - new_peak)
    right_scale = jnp.exp(right_peak - new_peak)
    return (
        new_peak,
        left_total * left_scale + right_total * right_scale,
        left_sum * left_scale[..., None] + right_sum * right_scale[..., None],
    )


def add_pair(earlier_sum, later_sum):
    return (earlier_sum[0] + later_sum[0], earlier_sum[1] + later_sum[1])


def general_device(
    tokens,
    rand_blocks,
    w_query,
    w_key,
    w_value,
    w_out,
    w_up,
    w_down,
    bias_query,
    bias_value,
    bias_out,
    bias_up,
    bias_down,
    attn_gain,
    attn_shift,
    ffn_gain,
    ffn_shift,
    cotangent,
):
    seq_here, local_len, model_width = tokens.shape
    blocks_all = rand_blocks.shape[0]
    devices = lax.axis_size("seq")
    position = lax.axis_index("seq")
    per_dev = blocks_all // devices
    slot_cap = max(2, seq_here * HEADS * RAND * 4 // (3 * blocks_all))
    pair_width = 2 * HD
    lane_count = seq_here * HEADS * RAND
    slot_size = BLOCK * pair_width
    rows_here = seq_here * local_len
    score_scale = HD ** (-0.5)

    def to_heads(values):
        return values.reshape(seq_here, per_dev, BLOCK, HEADS, -1).transpose(0, 1, 3, 2, 4)

    def from_heads(values):
        return values.transpose(0, 1, 3, 2, 4).reshape(rows_here, -1)

    inputs = tokens.reshape(rows_here, model_width).astype(jnp.float32)
    normed = layer_norm(inputs, attn_gain, attn_shift).astype(jnp.bfloat16)
    queries = (dense_rows(normed, w_query) + bias_query).astype(jnp.bfloat16)
    key_rows = dense_rows(normed, w_key).astype(jnp.bfloat16)
    value_rows = (dense_rows(normed, w_value) + bias_value).astype(jnp.bfloat16)
    kv_tokens = jnp.stack(
        [
            key_rows.reshape(seq_here, local_len, HEADS, HD),
            value_rows.reshape(seq_here, local_len, HEADS, HD),
        ],
        axis=3,
    ).reshape(seq_here, local_len, 2 * model_width)
    padded = extended(kv_tokens, (("seq", 1),), BLOCK)
    pad_blocks = padded.reshape(seq_here, per_dev + 2, BLOCK, HEADS, pair_width)
    window = jnp.stack(
        [pad_blocks[:, 0:per_dev], pad_blocks[:, 1 : per_dev + 1], pad_blocks[:, 2 : per_dev + 2]],
        axis=2,
    )
    window = window.transpose(0, 1, 4, 2, 3, 5).reshape(
        seq_here, per_dev, HEADS, 3 * BLOCK, pair_width
    )
    packed = jnp.concatenate([queries.reshape(seq_here, local_len, model_width), kv_tokens], axis=2)
    head_pack, tail_pack = from_ends(packed[:, :BLOCK], packed[:, local_len - BLOCK :])
    global_pack = jnp.stack([head_pack, tail_pack], axis=1)
    global_query = (
        global_pack[..., :model_width]
        .reshape(seq_here, 2, BLOCK, HEADS, HD)
        .transpose(0, 3, 1, 2, 4)
        .reshape(seq_here, HEADS, 2 * BLOCK, HD)
    )
    global_kv = (
        global_pack[..., model_width:]
        .reshape(seq_here, 2, BLOCK, HEADS, pair_width)
        .transpose(0, 3, 1, 2, 4)
        .reshape(seq_here, HEADS, 2 * BLOCK, pair_width)
    )
    flat_req = rand_blocks.reshape(blocks_all, lane_count)
    block_ids = jnp.arange(blocks_all, dtype=jnp.int32)
    live_rows = (block_ids != 0) & (block_ids != blocks_all - 1)
    own_blocks = position * per_dev + jnp.arange(per_dev, dtype=jnp.int32)
    matches = (
        (flat_req[:, :, None] == own_blocks[None, None, :]) & live_rows[:, None, None]
    ).astype(jnp.int32)
    order_rank = jnp.cumsum(matches, axis=1) - matches
    slot_ids = jnp.arange(slot_cap, dtype=jnp.int32)
    chosen = matches[..., None] * (order_rank[..., None] == slot_ids).astype(jnp.int32)
    lane_ids = jnp.arange(lane_count, dtype=jnp.int32)
    source_rows = lane_ids // (HEADS * RAND) * (per_dev * HEADS) + lane_ids // RAND % HEADS
    slot_live = jnp.sum(chosen, axis=1)
    slot_rows = (
        jnp.sum(chosen * source_rows[None, :, None, None], axis=1)
        + (jnp.arange(per_dev, dtype=jnp.int32) * HEADS)[None, :, None]
    )
    kv_heads = (
        kv_tokens.reshape(seq_here, per_dev, BLOCK, HEADS, pair_width)
        .transpose(0, 1, 3, 2, 4)
        .reshape(seq_here * per_dev * HEADS, slot_size)
    )
    served = jnp.take(kv_heads, slot_rows.reshape(-1), axis=0) * slot_live.reshape(-1, 1).astype(
        jnp.bfloat16
    )
    served = served.reshape(devices, per_dev, per_dev, slot_cap, slot_size)
    replies = lax.all_to_all(served, "seq", split_axis=0, concat_axis=0, tiled=True)
    fetched = replies.transpose(1, 0, 2, 3, 4).reshape(per_dev * blocks_all * slot_cap, slot_size)
    my_blocks = lax.dynamic_slice_in_dim(flat_req, position * per_dev, per_dev, 0)
    same_key = (my_blocks[:, :, None] == my_blocks[:, None, :]) & (
        lane_ids[None, None, :] < lane_ids[None, :, None]
    )
    my_ranks = jnp.sum(same_key.astype(jnp.int32), axis=2)
    pick_rows = (
        jnp.arange(per_dev, dtype=jnp.int32)[:, None] * blocks_all + my_blocks
    ) * slot_cap + my_ranks
    rand_kv = jnp.take(fetched, pick_rows.reshape(-1), axis=0).reshape(
        per_dev, seq_here, HEADS, RAND, BLOCK, pair_width
    )
    rand_kv = rand_kv.transpose(1, 0, 2, 3, 4, 5).reshape(
        seq_here, per_dev, HEADS, RAND * BLOCK, pair_width
    )
    global_kv_all = jnp.broadcast_to(
        global_kv[:, None], (seq_here, per_dev, HEADS, 2 * BLOCK, pair_width)
    )
    keys_all = jnp.concatenate([window, global_kv_all, rand_kv], axis=3)
    list_keys = keys_all[..., :HD]
    list_values = keys_all[..., HD:]
    query_heads = to_heads(queries)
    scores = mixed_sum("sjhqd,sjhkd->sjhqk", query_heads, list_keys) * score_scale
    row_peak = jnp.max(scores, axis=-1, keepdims=True)
    weights = jnp.exp(scores - row_peak)
    row_total = jnp.sum(weights, axis=-1, keepdims=True)
    near_out = (
        mixed_sum("sjhqk,sjhkd->sjhqd", weights.astype(jnp.bfloat16), list_values) / row_total
    )
    local_heads = kv_tokens.reshape(seq_here, per_dev, BLOCK, HEADS, pair_width).transpose(
        0, 3, 1, 2, 4
    )
    local_keys = local_heads[..., :HD]
    local_values = local_heads[..., HD:]
    global_scores = mixed_sum("shqd,shjkd->shqjk", global_query, local_keys) * score_scale
    block_peak = jnp.max(global_scores, axis=-1, keepdims=True)
    global_weights = jnp.exp(global_scores - block_peak)
    local_top = jnp.max(block_peak, axis=3, keepdims=True)
    factor = jnp.exp(block_peak - local_top)
    local_total = jnp.sum(factor * jnp.sum(global_weights, axis=-1, keepdims=True), axis=(3, 4))
    local_sum = jnp.sum(
        factor * mixed_sum("shqjk,shjkd->shqjd", global_weights.astype(jnp.bfloat16), local_values),
        axis=3,
    )
    global_top, global_total, global_sum = joined(
        (local_top[..., 0, 0], local_total, local_sum), "seq", merge_rows
    )
    global_ctx = global_sum / global_total[..., None]
    global_lse = global_top + jnp.log(global_total)
    block_here = jnp.arange(per_dev, dtype=jnp.int32)
    head_mask = ((position == 0) & (block_here == 0))[None, :, None, None, None]
    tail_mask = ((position == devices - 1) & (block_here == per_dev - 1))[None, :, None, None, None]
    context = jnp.where(head_mask, global_ctx[:, None, :, :BLOCK], near_out)
    context = jnp.where(tail_mask, global_ctx[:, None, :, BLOCK:], context)
    context_rows = from_heads(context).astype(jnp.bfloat16)
    middle = inputs + (dense_rows(context_rows, w_out) + bias_out)
    normed_two = layer_norm(middle, ffn_gain, ffn_shift).astype(jnp.bfloat16)
    hidden = dense_rows(normed_two, w_up) + bias_up
    active = gelu_exact(hidden).astype(jnp.bfloat16)
    layer_out = (
        (middle + dense_rows(active, w_down) + bias_down)
        .astype(jnp.bfloat16)
        .reshape(seq_here, local_len, model_width)
    )
    cot_rows = cotangent.reshape(rows_here, model_width)
    cot_float = cot_rows.astype(jnp.float32)
    grad_w_down = dense_left(active, cot_rows)
    grad_bias_down = jnp.sum(cot_float, axis=0)
    d_active = dense_back(cot_rows, w_down)
    gelu_pull = jax.vjp(gelu_exact, hidden)[1]
    d_hidden = gelu_pull(d_active)[0].astype(jnp.bfloat16)
    grad_w_up = dense_left(normed_two, d_hidden)
    grad_bias_up = jnp.sum(d_hidden.astype(jnp.float32), axis=0)
    norm_pull_two = jax.vjp(layer_norm, middle, ffn_gain, ffn_shift)[1]
    d_middle_norm, grad_ffn_gain, grad_ffn_shift = norm_pull_two(dense_back(d_hidden, w_up))
    d_middle = cot_float + d_middle_norm
    d_attended = d_middle.astype(jnp.bfloat16)
    grad_w_out = dense_left(context_rows, d_attended)
    grad_bias_out = jnp.sum(d_attended.astype(jnp.float32), axis=0)
    d_context = dense_back(d_attended, w_out).astype(jnp.bfloat16)
    d_tokens = d_context.reshape(seq_here, local_len, model_width)
    head_grad, tail_grad = from_ends(d_tokens[:, :BLOCK], d_tokens[:, local_len - BLOCK :])
    d_heads = jnp.where(head_mask | tail_mask, jnp.zeros((), jnp.bfloat16), to_heads(d_context))
    d_float = d_heads.astype(jnp.float32)
    row_delta = jnp.sum(d_float * near_out, axis=-1, keepdims=True)
    scores = mixed_sum("sjhqd,sjhkd->sjhqk", query_heads, list_keys) * score_scale
    weights = jnp.exp(scores - row_peak)
    d_weights = mixed_sum("sjhqd,sjhkd->sjhqk", d_heads, list_values)
    d_scores = (weights / row_total * (d_weights - row_delta)).astype(jnp.bfloat16)
    d_query = mixed_sum("sjhqk,sjhkd->sjhqd", d_scores, list_keys) * score_scale
    d_list_keys = mixed_sum("sjhqk,sjhqd->sjhkd", d_scores, query_heads) * score_scale
    d_list_values = exact_sum(
        "sjhqk,sjhqd->sjhkd", weights.astype(jnp.bfloat16).astype(jnp.float32), d_float / row_total
    )
    d_kv = jnp.concatenate([d_list_keys, d_list_values], axis=-1)
    d_window = d_kv[:, :, :, : 3 * BLOCK].reshape(seq_here, per_dev, HEADS, 3, BLOCK, pair_width)
    keep_dims = ((0, 0), (0, 0), (0, 0))
    spread_sum = jnp.pad(d_window[:, :, :, 0], ((0, 0), (0, 2)) + keep_dims)
    spread_sum = spread_sum + jnp.pad(d_window[:, :, :, 1], ((0, 0), (1, 1)) + keep_dims)
    spread_sum = spread_sum + jnp.pad(d_window[:, :, :, 2], ((0, 0), (2, 0)) + keep_dims)
    own_grad = spread_sum[:, 1 : per_dev + 1]
    rim_grad = jnp.concatenate(
        [spread_sum[:, 0:1], spread_sum[:, per_dev + 1 : per_dev + 2]], axis=1
    )
    rim_grad = rim_grad.transpose(0, 1, 3, 2, 4).reshape(seq_here, 2 * BLOCK, 2 * model_width)
    back_rim = extended(rim_grad.astype(jnp.bfloat16), (("seq", 1),), BLOCK).astype(rim_grad.dtype)
    from_left = (
        back_rim[:, :BLOCK].reshape(seq_here, BLOCK, HEADS, pair_width).transpose(0, 2, 1, 3)
    )
    from_right = (
        back_rim[:, 3 * BLOCK :].reshape(seq_here, BLOCK, HEADS, pair_width).transpose(0, 2, 1, 3)
    )
    own_grad = own_grad.at[:, 0].add(from_left).at[:, per_dev - 1].add(from_right)
    global_part = jnp.sum(d_kv[:, :, :, 3 * BLOCK : 5 * BLOCK], axis=1)
    rand_part = d_kv[:, :, :, 5 * BLOCK :].reshape(seq_here, per_dev, HEADS, RAND, slot_size)
    rand_part = rand_part.transpose(1, 0, 2, 3, 4).reshape(per_dev * lane_count, slot_size)
    slot_grads = (
        jnp.zeros((per_dev * blocks_all * slot_cap, slot_size), jnp.float32)
        .at[pick_rows.reshape(-1)]
        .add(rand_part)
    )
    slot_grads = slot_grads.reshape(per_dev, devices, per_dev, slot_cap, slot_size).transpose(
        1, 0, 2, 3, 4
    )
    returned = lax.all_to_all(
        slot_grads.astype(jnp.bfloat16), "seq", split_axis=0, concat_axis=0, tiled=True
    ).astype(slot_grads.dtype)
    dump_row = seq_here * per_dev * HEADS
    targets = jnp.where(slot_live > 0, slot_rows, dump_row).reshape(-1)
    collected = (
        jnp.zeros((dump_row + 1, slot_size), jnp.float32)
        .at[targets]
        .add(returned.reshape(-1, slot_size))
    )
    own_grad = own_grad + collected[:dump_row].reshape(seq_here, per_dev, HEADS, BLOCK, pair_width)
    global_grad = (
        jnp.stack([head_grad, tail_grad], axis=1)
        .reshape(seq_here, 2, BLOCK, HEADS, HD)
        .transpose(0, 3, 1, 2, 4)
        .reshape(seq_here, HEADS, 2 * BLOCK, HD)
    )
    global_float = global_grad.astype(jnp.float32)
    global_delta = jnp.sum(global_float * global_ctx, axis=-1)
    global_scores = mixed_sum("shqd,shjkd->shqjk", global_query, local_keys) * score_scale
    global_weights = jnp.exp(global_scores - block_peak)
    coefficient = jnp.exp(block_peak - global_lse[..., None, None])
    global_probs = global_weights * coefficient
    global_dweights = mixed_sum("shqd,shjkd->shqjk", global_grad, local_values)
    global_dscores = (global_probs * (global_dweights - global_delta[..., None, None])).astype(
        jnp.bfloat16
    )
    d_global_query = mixed_sum("shqjk,shjkd->shqd", global_dscores, local_keys) * score_scale
    d_local_keys = mixed_sum("shqjk,shqd->shjkd", global_dscores, global_query) * score_scale
    d_local_values = exact_sum(
        "shqjk,shqd->shjkd",
        global_weights.astype(jnp.bfloat16).astype(jnp.float32) * coefficient,
        global_float,
    )
    own_grad = own_grad + jnp.concatenate([d_local_keys, d_local_values], axis=-1).transpose(
        0, 2, 1, 3, 4
    )
    head_terms = (d_global_query[:, :, :BLOCK], global_part[:, :, :BLOCK])
    tail_terms = (d_global_query[:, :, BLOCK:], global_part[:, :, BLOCK:])
    zero_terms = (jnp.zeros_like(head_terms[0]), jnp.zeros_like(head_terms[1]))
    head_rest = entering(head_terms, "seq", add_pair, zero_terms, True)
    tail_rest = entering(tail_terms, "seq", add_pair, zero_terms, False)
    head_full = add_pair(head_rest, head_terms)
    tail_full = add_pair(tail_rest, tail_terms)
    d_query = (
        d_query
        + jnp.where(head_mask, head_full[0][:, None], 0.0)
        + jnp.where(tail_mask, tail_full[0][:, None], 0.0)
    )
    own_grad = (
        own_grad
        + jnp.where(head_mask, head_full[1][:, None], 0.0)
        + jnp.where(tail_mask, tail_full[1][:, None], 0.0)
    )
    d_query_rows = from_heads(d_query).astype(jnp.bfloat16)
    kv_grad = own_grad.transpose(0, 1, 3, 2, 4).reshape(rows_here, HEADS, pair_width)
    d_key_rows = kv_grad[..., :HD].reshape(rows_here, model_width).astype(jnp.bfloat16)
    d_value_rows = kv_grad[..., HD:].reshape(rows_here, model_width).astype(jnp.bfloat16)
    grad_w_query = dense_left(normed, d_query_rows)
    grad_bias_query = jnp.sum(d_query_rows.astype(jnp.float32), axis=0)
    grad_w_key = dense_left(normed, d_key_rows)
    grad_w_value = dense_left(normed, d_value_rows)
    grad_bias_value = jnp.sum(d_value_rows.astype(jnp.float32), axis=0)
    d_normed = (
        dense_back(d_query_rows, w_query)
        + dense_back(d_key_rows, w_key)
        + dense_back(d_value_rows, w_value)
    )
    norm_pull_one = jax.vjp(layer_norm, inputs, attn_gain, attn_shift)[1]
    d_inputs_norm, grad_attn_gain, grad_attn_shift = norm_pull_one(d_normed)
    grad_tokens = (
        (d_middle + d_inputs_norm).astype(jnp.bfloat16).reshape(seq_here, local_len, model_width)
    )
    grad_list = [
        grad_w_query,
        grad_w_key,
        grad_w_value,
        grad_w_out,
        grad_w_up,
        grad_w_down,
        grad_bias_query,
        grad_bias_value,
        grad_bias_out,
        grad_bias_up,
        grad_bias_down,
        grad_attn_gain,
        grad_attn_shift,
        grad_ffn_gain,
        grad_ffn_shift,
    ]
    flattened = jnp.concatenate([member.reshape(-1) for member in grad_list])
    item_count = lax.axis_size("item")
    length_all = flattened.shape[0]
    stride_all = 128 * item_count * devices
    padded_len = (length_all + stride_all - 1) // stride_all * stride_all
    lead_pad = padded_len - length_all
    grad_grid = jnp.pad(flattened, (lead_pad, 0)).reshape(-1, 128)
    shared_rows = lax.psum_scatter(grad_grid, ("item", "seq"), scatter_dimension=0, tiled=True)
    summed = (
        lax.all_gather(shared_rows.astype(jnp.bfloat16), ("item", "seq"), axis=0, tiled=True)
        .astype(shared_rows.dtype)
        .reshape(-1)
    )
    results = []
    offset = lead_pad
    for member in grad_list:
        results.append(summed[offset : offset + member.size].reshape(member.shape))
        offset = offset + member.size
    return (
        layer_out,
        grad_tokens,
        results[0],
        results[1],
        results[2],
        results[3],
        results[4],
        results[5],
        results[6],
        results[7],
        results[8],
        results[9],
        results[10],
        results[11],
        results[12],
        results[13],
        results[14],
    )


LANES = 128
GROUP = 4
FAR = -1e30
BF = jnp.bfloat16
F32 = jnp.float32
VMEM_ASK = 56 * 1024 * 1024


def over_z(value, step):
    count = lax.axis_size("seq")
    return lax.ppermute(value, "seq", [(i, i ^ (2 * step)) for i in range(count)])


def over_core(value):
    count = lax.axis_size("seq")
    return lax.ppermute(value, "seq", [(i, i ^ 1) for i in range(count)])


def over_item(value, step):
    count = lax.axis_size("item")
    return lax.ppermute(value, "item", [(i, i ^ step) for i in range(count)])


def params(**more):
    return pltpu.CompilerParams(vmem_limit_bytes=VMEM_ASK, **more)


def vmem(count):
    return [pl.BlockSpec(memory_space=pltpu.VMEM)] * count


def cost(flops, moved, special=0):
    return pl.CostEstimate(flops=flops, bytes_accessed=moved, transcendentals=special)


LIGHT = cost(10**6, 10**5)


def dot_nn(left, right):
    return lax.dot_general(left, right, (((1,), (0,)), ((), ())), preferred_element_type=F32)


def dot_tn(left, right):
    return lax.dot_general(left, right, (((0,), (0,)), ((), ())), preferred_element_type=F32)


def dot_nt(left, right):
    return lax.dot_general(left, right, (((1,), (1,)), ((), ())), preferred_element_type=F32)


def attend_kernel(heads, *refs):
    own, other, mult_ref = refs[:4], refs[4:8], refs[8]
    ctx_refs, out_ref, lse_ref = refs[9:13], refs[13], refs[14]
    width = heads * HD
    for h in range(heads):
        low = h * HD
        query = jnp.concatenate([r[low : low + HD, :] for r in own], axis=1)
        key = jnp.concatenate(
            [r[width + low : width + low + HD, :] for r in own]
            + [r[low : low + HD, :] for r in other],
            axis=1,
        )
        value = jnp.concatenate(
            [r[2 * width + low : 2 * width + low + HD, :] for r in own]
            + [r[width + low : width + low + HD, :] for r in other],
            axis=1,
        )
        rows, lanes = key.shape[1], query.shape[1]
        scores = dot_tn(key, query) * (HD**-0.5)
        scores = scores.reshape(rows // BLOCK, BLOCK, lanes)
        mult = mult_ref[h][:, None, :]
        scores = jnp.where(mult > 0.0, scores, FAR)
        peak = jnp.max(jnp.max(scores, axis=0), axis=0, keepdims=True)
        weights = jnp.exp(scores - peak[None]) * mult
        total = jnp.sum(jnp.sum(weights, axis=0), axis=0, keepdims=True)
        packed = weights.astype(BF).reshape(rows, lanes)
        out = dot_nn(value, packed) / total
        out_ref[low : low + HD, :] = out
        lse_ref[h] = peak + jnp.log(total)
        rounded = out.astype(BF)
        for k in range(4):
            ctx_refs[k][low : low + HD, :] = rounded[:, k * LANES : (k + 1) * LANES]


def attend_back_kernel(heads, *refs):
    own, other, mult_ref, out_ref, lse_ref = refs[:4], refs[4:8], refs[8], refs[9], refs[10]
    grad_refs = refs[11:14]
    dq_ref, dkv_ref, far_ref = refs[14:17]
    width = heads * HD
    for h in range(heads):
        low = h * HD
        query = jnp.concatenate([r[low : low + HD, :] for r in own], axis=1)
        key = jnp.concatenate(
            [r[width + low : width + low + HD, :] for r in own]
            + [r[low : low + HD, :] for r in other],
            axis=1,
        )
        value = jnp.concatenate(
            [r[2 * width + low : 2 * width + low + HD, :] for r in own]
            + [r[width + low : width + low + HD, :] for r in other],
            axis=1,
        )
        grad = jnp.concatenate(
            [r[low : low + HD, :] for r in grad_refs]
            + [grad_refs[2][width + low : width + low + HD, :]],
            axis=1,
        )
        rows, lanes = key.shape[1], query.shape[1]
        scale = HD**-0.5
        scores = dot_tn(key, query) * scale
        scores = scores.reshape(rows // BLOCK, BLOCK, lanes)
        mult = mult_ref[h][:, None, :]
        scores = jnp.where(mult > 0.0, scores, FAR)
        probs = jnp.exp(scores - lse_ref[h][None]) * mult
        delta = jnp.sum(grad.astype(F32) * out_ref[low : low + HD, :], axis=0, keepdims=True)
        d_probs = dot_tn(value, grad).reshape(rows // BLOCK, BLOCK, lanes)
        d_scores = (probs * (d_probs - delta[None])).astype(BF).reshape(rows, lanes)
        packed = probs.astype(BF).reshape(rows, lanes)
        dq_ref[low : low + HD, :] = (dot_nn(key, d_scores) * scale).astype(BF)
        d_key = dot_nt(query, d_scores) * scale
        d_value = dot_nt(grad, packed)
        half = rows // 2
        dkv_ref[low : low + HD, :] = d_key[:, :half]
        dkv_ref[width + low : width + low + HD, :] = d_value[:, :half]
        far_ref[low : low + HD, :] = d_key[:, half:].astype(BF)
        far_ref[width + low : width + low + HD, :] = d_value[:, half:].astype(BF)


def norm_parts(values):
    center = values - jnp.mean(values, axis=-1, keepdims=True)
    rate = lax.rsqrt(jnp.mean(center * center, axis=-1, keepdims=True) + epsilon)
    return center * rate, rate


def line(ref, start=0, size=None):
    size = ref.shape[0] if size is None else size
    return ref[start : start + size].reshape(1, size)


def lay_rows(out, at, vector):
    for b in range(vector.shape[1] // LANES):
        out[at + b : at + b + 1, :] = vector[:, b * LANES : (b + 1) * LANES]
    return at + vector.shape[1] // LANES


def project_kernel(
    place_ref, tokens_ref, wq_ref, wk_ref, wv_ref, bq_ref, bv_ref, gain_ref, shift_ref,
    hat_ref, cut0, cut1, cut2, cut3, held, turned, sems,
):
    chip = place_ref[0]
    width = tokens_ref.shape[1]
    part = width // GROUP
    copies = [
        pltpu.make_async_copy(ref, held.at[n], sems.at[n])
        for n, ref in enumerate((wq_ref, wk_ref, wv_ref))
    ]
    for copy in copies:
        copy.start()
    hat, _ = norm_parts(tokens_ref[...].astype(F32))
    hat_ref[...] = hat.astype(BF)
    normed = (hat * line(gain_ref) + line(shift_ref)).astype(BF)
    biases = (bq_ref, None, bv_ref)
    for n, copy in enumerate(copies):
        copy.wait()
        rows = dot_nn(normed, held[n])
        if biases[n] is not None:
            rows = rows + line(biases[n])
        turned[n * width : (n + 1) * width, :] = rows.astype(BF).T
    for k, ref in enumerate((cut0, cut1, cut2, cut3)):
        for n in range(3):
            at = pl.multiple_of(n * width + (chip ^ k) * part, part)
            ref[n * part : (n + 1) * part, :] = turned[pl.ds(at, part), :]


def mult_kernel(heads, blocks_all, place_ref, rand_ref, mult_ref):
    chip, core = place_ref[0], place_ref[2]
    rows, lanes = mult_ref.shape[1], mult_ref.shape[2]
    spot = lax.broadcasted_iota(jnp.int32, (rows, BLOCK), 0)
    side = jnp.where(spot < rows // 2, core, 1 - core)
    key_ids = 4 * (chip ^ ((spot >> 1) & 3)) + 2 * side + (spot & 1)
    one = lambda hit: jnp.where(hit, 1.0, 0.0)
    ends = one(key_ids == 0) + one(key_ids == blocks_all - 1)
    for r in range(lanes // BLOCK):
        query = 4 * (chip ^ (r // 2)) + 2 * core + (r % 2)
        fixed = ends + one(key_ids == query - 1) + one(key_ids == query) + one(key_ids == query + 1)
        whole = (query == 0) | (query == blocks_all - 1)
        for h in range(heads):
            total = fixed
            for n in range(RAND):
                named = rand_ref[query * (HEADS * RAND) + (chip * heads + h) * RAND + n]
                total = total + one(key_ids == named)
            total = jnp.where(whole, jnp.ones_like(total), total)
            mult_ref[h, :, r * BLOCK : (r + 1) * BLOCK] = total


def middle_kernel(
    place_ref, tokens_ref, ctx0, ctx1, ctx2, ctx3, w_out_hbm, b_out_ref, gain_ref, shift_ref,
    w_up_hbm, b_up_ref, d_active_hbm, cot_ref,
    down0, down1, down2, down3, up0, up1, up2, up3, back0, back1,
    middle_ref, active_ref, d_middle_ref, tiny_ref,
    ctx_full, active_t, d_hidden_f, d_att_f, d_ctx_full, w_out_ref, w_up_ref, d_active_ref, sems,
):
    chip, item = place_ref[0], place_ref[1]
    rows, width = tokens_ref.shape
    part = width // GROUP
    fan = w_up_ref.shape[1]
    chunk = width
    chunks = fan // chunk
    out_copy = pltpu.make_async_copy(w_out_hbm, w_out_ref, sems.at[0])
    out_copy.start()
    copies = []
    for j in range(chunks):
        cols = slice(j * chunk, (j + 1) * chunk)
        up_copy = pltpu.make_async_copy(w_up_hbm.at[:, cols], w_up_ref.at[:, cols], sems.at[1 + j])
        act_copy = pltpu.make_async_copy(
            d_active_hbm.at[:, cols], d_active_ref.at[:, cols], sems.at[1 + chunks + j]
        )
        up_copy.start()
        act_copy.start()
        copies.append((up_copy, act_copy))
    for k, ref in enumerate((ctx0, ctx1, ctx2, ctx3)):
        at = pl.multiple_of((chip ^ k) * part, part)
        ctx_full[pl.ds(at, part), :] = ref[...]
    context = ctx_full[...]
    out_copy.wait()
    middle = tokens_ref[...].astype(F32) + (dot_tn(context, w_out_ref[...]) + line(b_out_ref))
    middle_ref[...] = middle
    hat, rate = norm_parts(middle)
    normed = (hat * line(gain_ref) + line(shift_ref)).astype(BF)
    at = 0
    d_norm = jnp.zeros((rows, width), F32)
    for j in range(chunks):
        cols = slice(j * chunk, (j + 1) * chunk)
        copies[j][0].wait()
        hidden = dot_nn(normed, w_up_ref[:, cols]) + line(b_up_ref, j * chunk, chunk)
        bell = 0.5 * (1.0 + lax.erf(hidden * (0.5**0.5)))
        active = (hidden * bell).astype(BF)
        active_ref[:, cols] = active
        active_t[cols, :] = active.T
        slope = bell + hidden * jnp.exp(-0.5 * hidden * hidden) * 0.3989422804014327
        copies[j][1].wait()
        d_hidden = (d_active_ref[:, cols] * slope).astype(BF)
        at = lay_rows(tiny_ref, at, jnp.sum(d_hidden.astype(F32), axis=0, keepdims=True))
        for b in range(chunk // LANES):
            to = j * chunk + b * LANES
            d_hidden_f[to : to + LANES, :] = d_hidden[:, b * LANES : (b + 1) * LANES]
        d_norm = d_norm + dot_nt(d_hidden, w_up_ref[:, cols])
    at = lay_rows(tiny_ref, at, jnp.sum(d_norm * hat, axis=0, keepdims=True))
    at = lay_rows(tiny_ref, at, jnp.sum(d_norm, axis=0, keepdims=True))
    scaled = d_norm * line(gain_ref)
    cot = cot_ref[...].astype(F32)
    at = lay_rows(tiny_ref, at, jnp.sum(cot, axis=0, keepdims=True))
    d_middle = cot + rate * (
        scaled
        - jnp.mean(scaled, axis=-1, keepdims=True)
        - hat * jnp.mean(scaled * hat, axis=-1, keepdims=True)
    )
    d_middle_ref[...] = d_middle
    d_attended = d_middle.astype(BF)
    at = lay_rows(tiny_ref, at, jnp.sum(d_attended.astype(F32), axis=0, keepdims=True))
    d_ctx_full[...] = dot_nt(w_out_ref[...], d_attended).astype(BF)
    for k in range(GROUP):
        at = pl.multiple_of((chip ^ k) * part, part)
        ref = (back0, back1)[k % 2]
        ref[k // 2 * part : (k // 2 + 1) * part, :] = d_ctx_full[pl.ds(at, part), :]
    normed_t = normed.T
    quarter, mid = fan // 8, width // 2
    for b in range(width // LANES):
        d_att_f[b * LANES : (b + 1) * LANES, :] = d_attended[:, b * LANES : (b + 1) * LANES]
    early = LANES
    late = quarter - early
    for k, (first, second) in enumerate(zip((down0, down1, down2, down3), (up0, up1, up2, up3))):
        target = item ^ k
        for c in range(2):
            at = pl.multiple_of(c * (fan // 2) + target * quarter, quarter)
            first[c * quarter : (c + 1) * quarter, :] = active_t[pl.ds(at, quarter), :]
            to = 2 * quarter + width + c * early
            first[to : to + early, :] = d_hidden_f[pl.ds(at, early), :]
            at = pl.multiple_of(c * (fan // 2) + target * quarter + early, early)
            second[c * late : (c + 1) * late, :] = d_hidden_f[pl.ds(at, late), :]
            at = pl.multiple_of((2 * c + (target & 1)) * part, part)
            to = 2 * late + c * part
            second[to : to + part, :] = ctx_full[pl.ds(at, part), :]
        first[2 * quarter : 2 * quarter + width, :] = normed_t
        at = pl.multiple_of((target >> 1) * mid, mid)
        to = 2 * late + 2 * part
        second[to : to + mid, :] = d_att_f[pl.ds(at, mid), :]


ROUND = (0, 2, 1, 3)


def hand_out(chip, out_ref, at, size, grads):
    for z in range(GROUP):
        k = chip ^ z
        row = ((k >> 1) | ((k & 1) << 1)) * size
        here = at
        for grad in grads:
            share = grad.shape[0] // GROUP
            for b in range(grad.shape[1] // LANES):
                out_ref[pl.ds(pl.multiple_of(row + here, 16), share), :] = grad[
                    z * share : (z + 1) * share, b * LANES : (b + 1) * LANES
                ].astype(out_ref.dtype)
                here += share
    return here


def first_grad_kernel(place_ref, *refs):
    pieces, cots, kept_ref, given_ref = refs[:4], refs[4:8], refs[8], refs[9]
    down_left, down_right, up_left, up_right = refs[10:]
    chip, core = place_ref[0], place_ref[2]
    quarter, width, early = down_left.shape[0] // 2, up_left.shape[0], up_right.shape[1] // 2
    for s, piece in enumerate(pieces):
        span = slice(s * LANES, (s + 1) * LANES)
        down_left[:, span] = piece[: 2 * quarter, :]
        down_right[span, :] = cots[s][...]
        up_left[:, span] = piece[2 * quarter : 2 * quarter + width, :]
        for c in range(2 * early // LANES):
            low = 2 * quarter + width + c * LANES
            up_right[span, c * LANES : (c + 1) * LANES] = piece[low : low + LANES, :]
    size = kept_ref.shape[0] // GROUP
    for half, ref in ((1 - core, given_ref), (core, kept_ref)):
        rows = pl.ds(pl.multiple_of(half * quarter, quarter), quarter)
        cols = pl.ds(pl.multiple_of(half * early, early), early)
        grad_down = dot_nn(down_left[rows, :], down_right[...])
        at = hand_out(chip, ref, 0, size, (grad_down,))
        hand_out(chip, ref, at, size, (dot_nn(up_left[...], up_right[:, cols]),))


def second_grad_kernel(place_ref, *refs):
    firsts, pieces, kept_ref, given_ref = refs[:4], refs[4:8], refs[8], refs[9]
    up_left, up_right, out_left, out_right = refs[10:]
    chip, core = place_ref[0], place_ref[2]
    width, late = up_left.shape[0], up_right.shape[1] // 2
    part, mid = out_left.shape[0] // 2, out_right.shape[1]
    skip = firsts[0].shape[0] - width - 2 * LANES
    for s, piece in enumerate(pieces):
        span = slice(s * LANES, (s + 1) * LANES)
        up_left[:, span] = firsts[s][skip : skip + width, :]
        for b in range(2 * late // LANES):
            up_right[span, b * LANES : (b + 1) * LANES] = piece[b * LANES : (b + 1) * LANES, :]
        out_left[:, span] = piece[2 * late : 2 * late + 2 * part, :]
        for b in range(mid // LANES):
            low = 2 * late + 2 * part + b * LANES
            out_right[span, b * LANES : (b + 1) * LANES] = piece[low : low + LANES, :]
    size = kept_ref.shape[0] // GROUP
    for half, ref in ((1 - core, given_ref), (core, kept_ref)):
        rows = pl.ds(pl.multiple_of(half * part, part), part)
        cols = pl.ds(pl.multiple_of(half * late, late), late)
        at = hand_out(chip, ref, 0, size, (dot_nn(up_left[...], up_right[:, cols]),))
        hand_out(chip, ref, at, size, (dot_nn(out_left[rows, :], out_right[...]),))


def head_grad_kernel(
    place_ref, dq_ref, dkv_ref, far_ref, hat0, hat1, gain_ref, shift_ref, wq_hbm, wk_hbm, wv_hbm,
    back0, back1, kept_ref, given_ref, tiny_ref,
    d_heads, normed, grad, padded, window, sems,
):
    chip, core = place_ref[0], place_ref[2]
    part, tokens = dq_ref.shape
    width = normed.shape[1]
    wide = padded.shape[1]
    off = pl.multiple_of((chip & 1) * HD, HD)
    begin = pl.multiple_of(chip * part - off, LANES)
    copies = [
        pltpu.make_async_copy(w.at[:, pl.ds(begin, wide)], window.at[n], sems.at[n])
        for n, w in enumerate((wq_hbm, wk_hbm, wv_hbm))
    ]
    for copy in copies:
        copy.start()
    d_heads[:part, :] = dq_ref[...]
    d_heads[part:, :] = (dkv_ref[...] + far_ref[...].astype(F32)).astype(BF)
    padded[...] = jnp.zeros(padded.shape, BF)
    for n in range(3):
        padded[n, pl.ds(off, part), :] = d_heads[n * part : (n + 1) * part, :]
    hats = [((hat0, hat1)[k % 2], k // 2 * LANES) for k in range(GROUP)]
    for k, (hat, at) in enumerate(hats):
        span = slice(k * LANES, (k + 1) * LANES)
        back, row = (back0, back1)[k % 2], k // 2 * 3 * part
        back[row : row + 3 * part, :] = d_heads[:, span]
        rows = hat[at : at + LANES, :].astype(F32) * line(gain_ref) + line(shift_ref)
        normed[span, :] = rows.astype(BF)
    grad[...] = dot_nn(d_heads[...], normed[...])
    mid, rows = width // 2, 3 * part // GROUP
    for b in range(mid // LANES):
        mine = grad[:, pl.ds(pl.multiple_of(core * mid + b * LANES, LANES), LANES)]
        theirs = grad[:, pl.ds(pl.multiple_of((1 - core) * mid + b * LANES, LANES), LANES)]
        for q in range(GROUP):
            at = (q * (mid // LANES) + b) * rows
            kept_ref[at : at + rows, :] = mine[q * rows : (q + 1) * rows, :]
            given_ref[at : at + rows, :] = theirs[q * rows : (q + 1) * rows, :].astype(BF)
    for copy in copies:
        copy.wait()
    turned = [padded[n].T for n in range(3)]
    gain_grad = jnp.zeros((1, width), F32)
    shift_grad = jnp.zeros((1, width), F32)
    for k, (hat, at) in enumerate(hats):
        span = slice(k * LANES, (k + 1) * LANES)
        d_norm = dot_nt(turned[0][span, :], window[0])
        d_norm = d_norm + dot_nt(turned[1][span, :], window[1])
        d_norm = d_norm + dot_nt(turned[2][span, :], window[2])
        rows = hat[at : at + LANES, :].astype(F32)
        gain_grad = gain_grad + jnp.sum(d_norm * rows, axis=0, keepdims=True)
        shift_grad = shift_grad + jnp.sum(d_norm, axis=0, keepdims=True)
    at = lay_rows(tiny_ref, 0, gain_grad)
    at = lay_rows(tiny_ref, at, shift_grad)
    ones = jnp.ones((8, tokens), BF)
    for n in (0, 2):
        sums = dot_nt(ones, padded[n])
        for r in range(width // LANES):
            value = jnp.zeros((1, LANES), F32)
            for m in range(wide // LANES):
                here = sums[:1, m * LANES : (m + 1) * LANES]
                value = value + jnp.where(begin == (r - m) * LANES, here, 0.0)
            tiny_ref[at : at + 1, :] = value
            at += 1


def input_grad_kernel(
    place_ref, back0, back1, back2, wq_hbm, wk_hbm, wv_hbm, tokens_ref, d_middle_ref,
    gain_ref, grad_ref, held, turned, sems,
):
    chip = place_ref[0]
    rows, width = tokens_ref.shape
    part = width // GROUP
    copies = [
        pltpu.make_async_copy(ref, held.at[n], sems.at[n])
        for n, ref in enumerate((wq_hbm, wk_hbm, wv_hbm))
    ]
    for copy in copies:
        copy.start()
    for k, ref in enumerate((back0, back1, back2, back2)):
        base = 3 * part if k == 3 else 0
        for n in range(3):
            at = pl.multiple_of(n * width + (chip ^ k) * part, part)
            turned[pl.ds(at, part), :] = ref[base + n * part : base + (n + 1) * part, :]
    d_norm = jnp.zeros((width, rows), F32)
    for n, copy in enumerate(copies):
        copy.wait()
        d_norm = d_norm + dot_nn(held[n], turned[n * width : (n + 1) * width, :])
    d_norm = d_norm.T
    hat, rate = norm_parts(tokens_ref[...].astype(F32))
    scaled = d_norm * line(gain_ref)
    d_inputs = rate * (
        scaled
        - jnp.mean(scaled, axis=-1, keepdims=True)
        - hat * jnp.mean(scaled * hat, axis=-1, keepdims=True)
    )
    grad_ref[...] = (d_middle_ref[...] + d_inputs).astype(BF)


def put_halves(layout, size, which, place_ref, halves, boxes, targets, sems):
    chip, item, core = place_ref[0], place_ref[1], place_ref[2]
    leaving = []
    for piece, (flip, step) in enumerate(which):
        side, place = core ^ flip, item ^ step
        known = (side * GROUP + place, 2 * side + (place & 1), place >> 1)
        for k in range(GROUP):
            at = k // 2 * size
            for (share, blocks, *_), box in zip(layout, boxes):
                to = pl.multiple_of((chip ^ k) * share, share)
                for b in range(blocks):
                    box[piece, pl.ds(to, share), b * LANES : (b + 1) * LANES] = halves[
                        2 * piece + k % 2
                    ][at : at + share, :].astype(F32)
                    at += share
        for n, (share, blocks, row, column, unit, first) in enumerate(layout):
            tall, wide = GROUP * share, blocks * LANES
            target = targets[n]
            if row is not None:
                start = pl.multiple_of(known[row] * tall, tall)
                target = target.at[pl.ds(start, tall), :]
            if column is not None:
                start = pl.multiple_of(known[column] * unit + first, LANES)
                target = target.at[:, pl.ds(start, wide)]
            copy = pltpu.make_async_copy(boxes[n].at[piece], target, sems.at[piece, n])
            copy.start()
            leaving.append(copy)
    return leaving


def put_pieces_kernel(layout, size, which, place_ref, *refs):
    outs = len(layout)
    halves = refs[: 2 * len(which)]
    boxes, sems = refs[-1 - outs : -1], refs[-1]
    done = refs[-2 - outs]
    targets = refs[-2 - 2 * outs : -2 - outs]
    done[...] = jnp.zeros(done.shape, F32)
    for copy in put_halves(layout, size, which, place_ref, halves, boxes, targets, sems):
        copy.wait()


def put_heads(size, skip, place_ref, flip, halves, whole, held, targets, sems):
    chip, item = place_ref[0], place_ref[1]
    mid = whole.shape[2]
    part = whole.shape[1] // (3 * GROUP)
    rows = 3 * part // GROUP
    for k in range(GROUP):
        for z in range(GROUP):
            to = pl.multiple_of((chip ^ z) * (3 * part) + (item ^ k) * rows, 16)
            for b in range(mid // LANES):
                at = z // 2 * size + skip + b * rows
                whole[flip, pl.ds(to, rows), b * LANES : (b + 1) * LANES] = halves[2 * k + z % 2][
                    at : at + rows, :
                ]
    leaving = []
    for b in range(mid // LANES):
        start = pl.multiple_of((place_ref[2] ^ flip) * mid + b * LANES, LANES)
        for n, target in enumerate(targets):
            tall = jnp.concatenate(
                [
                    whole[
                        flip,
                        z * 3 * part + n * part : z * 3 * part + (n + 1) * part,
                        b * LANES : (b + 1) * LANES,
                    ]
                    for z in range(GROUP)
                ],
                axis=0,
            )
            held[flip, n, b] = tall.T.astype(F32)
            copy = pltpu.make_async_copy(
                held.at[flip, n, b], target.at[pl.ds(start, LANES), :], sems.at[flip, n, b]
            )
            copy.start()
            leaving.append(copy)
    return leaving


def put_rest_kernel(layout, size, skip, which, place_ref, *refs):
    halves, targets, heads_out, done, boxes = refs[:16], refs[19:21], refs[21:24], refs[24], refs[25:27]
    whole, held, out_sems, head_out_sems = refs[27:]
    done[...] = jnp.zeros(done.shape, F32)
    chosen = [halves[2 * (GROUP * flip + k) + h] for flip, k in which for h in range(2)]
    leaving = put_halves(layout, size, which, place_ref, chosen, boxes, targets, out_sems)
    for flip in range(2):
        leaving += put_heads(
            size, skip, place_ref, flip, halves[8 * flip : 8 * flip + 8], whole, held, heads_out,
            head_out_sems,
        )
    for copy in leaving:
        copy.wait()


def put_pieces(layout, size, which, shapes, places, halves, flags, sofar, name):
    count, outs = len(which), len(layout)
    filled = [value for value in sofar if value is not None]
    kept = [n for n, value in enumerate(sofar) if value is not None]
    anywhere = pl.BlockSpec(memory_space=pl.ANY)
    before = 1 + 2 * count + len(flags)
    return pl.pallas_call(
        functools.partial(put_pieces_kernel, layout, size, which),
        in_specs=[pl.BlockSpec(memory_space=pltpu.SMEM)]
        + vmem(2 * count + len(flags))
        + [anywhere] * len(filled),
        out_specs=[anywhere] * outs + vmem(1),
        out_shape=[jax.ShapeDtypeStruct(shape, F32) for shape in shapes]
        + [jax.ShapeDtypeStruct((8, LANES), F32)],
        scratch_shapes=[
            pltpu.VMEM((count, GROUP * share, blocks * LANES), F32)
            for share, blocks, *_ in layout
        ]
        + [pltpu.SemaphoreType.DMA((count, outs))],
        input_output_aliases={before + i: n for i, n in enumerate(kept)},
        compiler_params=params(),
        cost_estimate=LIGHT,
        name=name,
    )(places, *halves, *flags, *filled)


PLAN = dict(
    project=(0, 0), q1=(2, 2), q2=(2, 2), q3=(2, 2), mult=(2, 2), d_active=(2, 2), kv0=(4, 4),
    kv1=(4, 4), kv2=(5, 5), kv3=(4, 4), cot1=(4, 8), cot2=(4, 8), cot3=(4, 8), norm_near=(4, 6),
    attend=(6, 6), ctx1=(8, 8), ctx2=(8, 8), ctx3=(8, 8), middle=(10, 10), a1=(12, 12), a2=(12, 12),
    a3=(12, 12), dc1=(12, 12), dc2=(12, 12), norm_far=(10, 10), layer_out=(13, 15), b1=(13, 15),
    b2=(13, 15), b3=(13, 15), first_grad=(14, 14), one_core=(14, 14), one_z1=(15, 15),
    attend_back=(12, 12), far=(14, 14), one_z2=(16, 16), second_grad=(16, 16), two_core=(17, 17),
    head_grad=(15, 15), head_core=(15, 15), head_x=(16, 16), head_y=(16, 16), head_d=(16, 16),
    head_sum=(17, 17), two_z1=(18, 18), one_near=(17, 18), two_z2=(20, 20), one_far=(20, 20),
    one_nx=(20, 20), one_ny=(20, 20), two_near=(22, 22), one_fx=(22, 22), one_fy=(22, 22),
    back_z1=(16, 18), two_far=(24, 24), two_nx=(24, 24), two_ny=(24, 24), one_nd=(25, 26),
    one_fd=(25, 26), back_z2=(24, 25), two_fx=(25, 26), two_fy=(25, 26), input_grad=(26, 26),
    tiny_core=(17, 18), two_nd=(27, 28), two_fd=(27, 28), tiny_x=(18, 18), tiny_y=(20, 20),
    tiny_z1=(22, 22), tiny_z2=(28, 30), one_all=(17, 18), put_own=(25, 25), put_rest=(28, 28),
    put_two=(32, 99), one_cn0=(22, 24), one_cf0=(26, 26), two_cn0=(28, 30), two_cf0=(28, 30),
    one_cn1=(22, 24), one_cf1=(26, 26), two_cn1=(28, 30), two_cf1=(28, 30), one_cn2=(22, 24),
    one_cf2=(26, 26), two_cn2=(28, 30), two_cf2=(28, 30), one_cn3=(27, 27), one_cf3=(27, 27),
    two_cn3=(28, 30), two_cf3=(30, 30), tiny_out=(30, 99),
)


class Name(str):
    def __getitem__(self, index):
        return Name(self + "." + str(index))

    def __call__(self, k):
        return Name(self + str(k))

    def __getattr__(self, part):
        return Name(self + "_" + part)


class Names:
    def __getattr__(self, name):
        return Name(name)


def free(name):
    return "!" + name


def run_steps(steps, known):
    stage, last = {}, {}

    def named(name):
        return [source.lstrip("!").partition(".")[0] for source in steps[name][0]]

    def settle(name):
        if name in stage:
            return stage[name]
        first, wait = PLAN[name]
        for source in named(name):
            if source in steps:
                first = max(first, settle(source))
        stage[name], last[name] = first, max(first, wait)
        return first

    for name in steps:
        settle(name)
    depth = {}

    def deep(name):
        if name not in depth:
            depth[name] = 1 + max([deep(s) for s in named(name) if s in steps], default=0)
        return depth[name]

    for name in steps:
        deep(name)
    made, now, waiting = dict(known), 0, []
    order = sorted(steps, key=lambda n: (stage[n], depth[n]))

    def pick(source):
        base, _, index = source.lstrip("!").partition(".")
        return (base, int(index)) if index else (base, None)

    def turn(following):
        ending = [n for n in waiting if last[n] < following]
        keys = set()
        for n in ending:
            many = isinstance(made[n], (list, tuple))
            if n.startswith(Names().put):
                keys.add((n, len(made[n]) - 1))
            elif many:
                keys.update((n, i) for i in range(len(made[n])))
            else:
                keys.add((n, None))
        for n in order:
            if stage[n] == following:
                keys.update(
                    pick(s) for s in steps[n][0] if not s.startswith("!") and pick(s)[0] in made
                )
        keys = sorted(keys, key=str)
        values = [made[n] if i is None else made[n][i] for n, i in keys]
        for (n, i), value in zip(keys, lax.optimization_barrier(values)):
            if i is None:
                made[n] = value
            else:
                made[n] = [value if j == i else old for j, old in enumerate(made[n])]
        return [n for n in waiting if n not in ending]

    for name in order:
        if now < stage[name]:
            waiting, now = turn(stage[name]), stage[name]
        sources, function = steps[name]
        inputs = []
        for source in sources:
            base, index = pick(source)
            inputs.append(made[base] if index is None else made[base][index])
        made[name] = function(*inputs)
        waiting.append(name)
    return made


def split_device(
    tokens,
    rand_blocks,
    w_query,
    w_key,
    w_value,
    w_out,
    w_up,
    w_down,
    bias_query,
    bias_value,
    bias_out,
    bias_up,
    bias_down,
    attn_gain,
    attn_shift,
    ffn_gain,
    ffn_shift,
    cotangent,
):
    _, local_len, width = tokens.shape
    fan = w_up.shape[1]
    blocks_all = rand_blocks.shape[0]
    position, item = lax.axis_index("seq"), lax.axis_index("item")
    chip, core = position // 2, position % 2
    heads = HEADS // GROUP
    part = heads * HD
    all_len = GROUP * local_len
    quarter, mid = fan // 8, width // 2
    early = LANES
    late = quarter - early
    places = jnp.stack([chip, item, core]).astype(jnp.int32)
    smem = [pl.BlockSpec(memory_space=pltpu.SMEM)]
    anywhere = [pl.BlockSpec(memory_space=pl.ANY)]
    shaped = jax.ShapeDtypeStruct

    first_rows = 2 * quarter + width + 2 * early
    second_rows = 2 * late + 2 * part + mid
    tiny_rows = (fan + 4 * width) // LANES
    size = 3 * part
    rows_one = (quarter * width + width * early) // LANES
    rows_two = (width * late + part * mid) // LANES
    rows_three = size * mid // LANES
    half_one, half_two = rows_one // 2, rows_two // 2

    def kernel(body, ins, outs, scratch=(), name=None):
        return pl.pallas_call(
            body,
            in_specs=ins,
            out_specs=vmem(len(outs)),
            out_shape=list(outs),
            scratch_shapes=list(scratch),
            compiler_params=params(),
            cost_estimate=LIGHT,
            name=name,
        )

    box = lambda *dims: pltpu.VMEM(dims, BF)
    box32 = lambda *dims: pltpu.VMEM(dims, F32)
    sems = lambda n: pltpu.SemaphoreType.DMA((n,))

    def project(x):
        return kernel(
            project_kernel,
            smem + vmem(1) + anywhere * 3 + vmem(4),
            [shaped((local_len, width), BF)] + [shaped((size, local_len), BF)] * 4,
            [box(3, width, width), box(3 * width, local_len), sems(3)],
            "project",
        )(places, x, w_query, w_key, w_value, bias_query, bias_value, attn_gain, attn_shift)

    def multiplicity(rand):
        return kernel(
            functools.partial(mult_kernel, heads, blocks_all),
            smem * 2,
            [shaped((heads, 2 * all_len // BLOCK, all_len), F32)],
            name="multiplicity",
        )(places, rand.reshape(-1))[0]

    def attend(*ins):
        return kernel(
            functools.partial(attend_kernel, heads),
            vmem(9),
            [shaped((part, local_len), BF)] * 4
            + [shaped((part, all_len), F32), shaped((heads, 1, all_len), F32)],
            name="attend",
        )(*ins)

    def middle_step(ctx0, ctx1, ctx2, ctx3, d_active, cot):
        outs = kernel(
            middle_kernel,
            smem + vmem(5) + anywhere + vmem(3) + anywhere + vmem(1) + anywhere + vmem(1),
            [shaped((first_rows, LANES), BF)] * 4
            + [shaped((second_rows, LANES), BF)] * 4
            + [shaped((2 * part, local_len), BF)] * 2
            + [
                shaped((local_len, width), F32),
                shaped((local_len, fan), BF),
                shaped((local_len, width), F32),
                shaped((tiny_rows, LANES), F32),
            ],
            [box(width, local_len), box(fan, local_len), box(fan, local_len)]
            + [box(width, local_len)] * 2
            + [box(width, width), box(width, fan), box32(local_len, fan)]
            + [sems(1 + 2 * (fan // width))],
            "middle",
        )(
            places, tokens[0], ctx0, ctx1, ctx2, ctx3, w_out, bias_out, ffn_gain, ffn_shift,
            w_up, bias_up, d_active, cot,
        )
        return outs

    def attend_back(*ins):
        return kernel(
            functools.partial(attend_back_kernel, heads),
            vmem(14),
            [
                shaped((part, all_len), BF),
                shaped((2 * part, all_len), F32),
                shaped((2 * part, all_len), BF),
            ],
            name="attend_back",
        )(*ins)

    def first_grad(*ins):
        return kernel(
            first_grad_kernel,
            smem + vmem(8),
            [shaped((rows_one, LANES), F32), shaped((rows_one, LANES), BF)],
            [
                box(2 * quarter, all_len),
                box(all_len, width),
                box(width, all_len),
                box(all_len, 2 * early),
            ],
            "first_grad",
        )(places, *ins)

    def second_grad(*ins):
        return kernel(
            second_grad_kernel,
            smem + vmem(8),
            [shaped((rows_two, LANES), F32), shaped((rows_two, LANES), BF)],
            [
                box(width, all_len),
                box(all_len, 2 * late),
                box(2 * part, all_len),
                box(all_len, mid),
            ],
            "second_grad",
        )(places, *ins)

    def head_grad(*ins):
        return kernel(
            head_grad_kernel,
            smem + vmem(7) + anywhere * 3,
            [shaped((2 * size, local_len), BF)] * 2
            + [shaped((rows_three, LANES), F32), shaped((rows_three, LANES), BF)]
            + [shaped((4 * width // LANES, LANES), F32)],
            [
                box(size, all_len),
                box(all_len, width),
                box32(size, width),
                box(3, part + HD, all_len),
                box(3, width, part + HD),
                sems(3),
            ],
            "head_grad",
        )(places, *ins, attn_gain, attn_shift, w_query, w_key, w_value)

    def input_grad(own, came, far, d_middle):
        return kernel(
            input_grad_kernel,
            smem + vmem(3) + anywhere * 3 + vmem(3),
            [shaped((local_len, width), BF)],
            [box(3, width, width), box(3 * width, local_len), sems(3)],
            "input_grad",
        )(
            places, own, came, far, w_query, w_key, w_value, tokens[0], d_middle, attn_gain
        )[0]

    layout_one = (
        (quarter // GROUP, width // LANES, 0, None, 0, 0),
        (width // GROUP, early // LANES, None, 0, quarter, 0),
    )
    layout_two = (
        (width // GROUP, late // LANES, None, 0, quarter, early),
        (part // GROUP, mid // LANES, 1, 2, mid, 0),
    )
    size_one, size_two = (rows_one + rows_three) // GROUP, rows_two // GROUP
    shapes_one, shapes_two = ((fan, width), (width, fan)), ((width, fan), (width, width))

    own_three = tuple((0, k) for k in range(3))
    the_rest = ((0, 3), *((1, k) for k in range(GROUP)))
    every = tuple((flip, k) for flip in range(2) for k in range(GROUP))

    def put_own(*halves):
        return put_pieces(
            layout_one, size_one, own_three, shapes_one, places, halves, (), (None, None), "put_own"
        )

    def put_rest(*ins):
        skip = rows_one // GROUP
        return pl.pallas_call(
            functools.partial(put_rest_kernel, layout_one, size_one, skip, the_rest),
            in_specs=smem + vmem(17) + anywhere * 2,
            out_specs=anywhere * 5 + vmem(1),
            out_shape=[shaped(shape, F32) for shape in shapes_one]
            + [shaped((width, width), F32)] * 3
            + [shaped((8, LANES), F32)],
            scratch_shapes=[
                box32(len(the_rest), GROUP * share, blocks * LANES)
                for share, blocks, *_ in layout_one
            ]
            + [
                box(2, 3 * width, mid),
                box32(2, 3, mid // LANES, LANES, width),
                pltpu.SemaphoreType.DMA((len(the_rest), 2)),
                pltpu.SemaphoreType.DMA((2, 3, mid // LANES)),
            ],
            input_output_aliases={18: 0, 19: 1},
            compiler_params=params(),
            cost_estimate=LIGHT,
            name="put_rest",
        )(places, *ins)

    def put_two(*ins):
        return put_pieces(
            layout_two, size_two, every, shapes_two, places, ins[:16], ins[16:17], (ins[17], None),
            "put_two",
        )

    def rows_of(grad_t, k):
        blocks = grad_t.reshape(GROUP, rows_three // GROUP, LANES)
        return lax.dynamic_index_in_dim(blocks, item ^ k, 0, False)

    def head_sum(grad_t, x, y, d):
        total = rows_of(grad_t, 0) + x.astype(F32) + (y.astype(F32) + d.astype(F32))
        return total.astype(BF)

    def last_sum(pair, far):
        share = pair.shape[0] // 2
        return (pair[:share] + far.astype(F32)).astype(BF)

    def second_half(pair):
        return pair[pair.shape[0] // 2 :].astype(BF)

    below = lambda *parts: jnp.concatenate(parts, axis=0)
    cot = cotangent[0]
    n, todo = Names(), {}
    todo[n.project] = ((n.tokens,), project)
    todo[n.mult] = ((n.rand,), multiplicity)
    todo[n.d_active] = ((n.cot,), lambda c: dense_back(c, w_down))
    for k in range(1, GROUP):
        todo[n.q(k)] = ((n.project[k + 1],), functools.partial(over_z, step=k))
        todo[n.cot(k)] = ((n.cot,), functools.partial(over_item, step=k))
        todo[n.ctx(k)] = ((n.attend[k],), functools.partial(over_z, step=k))
    own = [n.project[1], n.q1, n.q2, n.q3]
    for k in range(GROUP):
        todo[n.kv(k)] = ((own[k],), lambda v: over_core(v[part:]))
    other = [n.kv(k) for k in range(GROUP)]
    todo[n.attend] = ((*own, *other, n.mult), attend)
    todo[n.norm_near] = ((n.project[0],), lambda v: below(v, over_z(v, 2)))
    todo[n.norm_far] = ((n.norm_near,), lambda v: over_z(v, 1))
    todo[n.middle] = ((n.attend[0], n.ctx1, n.ctx2, n.ctx3, n.d_active, n.cot), middle_step)
    todo[n.layer_out] = (
        (n.middle[10], n.middle[11]),
        lambda m, a: (m + dense_rows(a, w_down) + bias_down).astype(BF),
    )
    for k in range(1, GROUP):
        todo[n.a(k)] = ((n.middle[k],), functools.partial(over_item, step=k))
        todo[n.b(k)] = ((n.middle[4 + k],), functools.partial(over_item, step=k))
    todo[n.dc1] = ((n.middle[9],), lambda v: over_z(v, 1))
    todo[n.dc2] = ((n.middle[8], n.dc1), lambda v, c: over_z(below(v[part:], c[part:]), 2))
    firsts = [n.middle[0], n.a1, n.a2, n.a3]
    seconds = [n.middle[4], n.b1, n.b2, n.b3]
    todo[n.first_grad] = ((*firsts, n.cot, n.cot1, n.cot2, n.cot3), first_grad)
    def pair_up(half, kept, given):
        far = over_z((kept[half:] + given[half:].astype(F32)).astype(BF), 1)
        return kept[:half] + given[:half].astype(F32) + far.astype(F32)

    todo[n.one_core] = ((n.first_grad[1],), over_core)
    todo[n.one_z1] = (
        (n.first_grad[0], n.one_core),
        functools.partial(pair_up, half_one),
    )
    todo[n.one_z2] = ((n.one_z1,), lambda v: last_sum(v, over_z(second_half(v), 2)))
    todo[n.attend_back] = (
        (*own, *other, n.mult, n.attend[4], n.attend[5], n.middle[8], n.dc1, n.dc2),
        attend_back,
    )
    todo[n.far] = ((n.attend_back[2],), over_core)
    todo[n.second_grad] = ((*firsts, *seconds), second_grad)
    todo[n.two_core] = ((n.second_grad[1],), over_core)
    todo[n.two_z1] = (
        (n.second_grad[0], n.two_core),
        functools.partial(pair_up, half_two),
    )
    todo[n.head_grad] = (
        (n.attend_back[0], n.attend_back[1], n.far, n.norm_near, n.norm_far),
        head_grad,
    )
    todo[n.head_core] = ((n.head_grad[2], n.head_grad[3]), lambda k, g: k + over_core(g).astype(F32))
    for k, name in enumerate((n.head_x, n.head_y, n.head_d)):
        todo[name] = (
            (n.head_core,),
            lambda v, k=k + 1: over_item(rows_of(v, k).astype(BF), k),
        )
    todo[n.head_sum] = ((n.head_core, n.head_x, n.head_y, n.head_d), head_sum)
    todo[n.two_z2] = ((n.two_z1,), lambda v: last_sum(v, over_z(second_half(v), 2)))
    todo[n.one_all] = ((n.one_z2, n.head_sum), below)
    pieces = []
    for name, total in ((n.one, n.one_all), (n.two, n.two_z2)):
        todo[name.near] = ((total,), lambda v: below(v, over_z(v, 2)))
        todo[name.far] = ((name.near,), lambda v: over_z(v, 1))
        todo[name.nx] = ((name.near,), lambda v: over_item(v, 1))
        todo[name.ny] = ((name.near,), lambda v: over_item(v, 2))
        todo[name.fx] = ((name.far,), lambda v: over_item(v, 1))
        todo[name.fy] = ((name.far,), lambda v: over_item(v, 2))
        todo[name.nd] = ((name.nx,), lambda v: over_item(v, 2))
        todo[name.fd] = ((name.fy,), lambda v: over_item(v, 1))
        nears, fars = (name.near, name.nx, name.ny, name.nd), (name.far, name.fx, name.fy, name.fd)
        flat, mirrored = [], []
        for k, halves in enumerate(zip(nears, fars)):
            for half, crossed in zip(halves, (name.cn(k), name.cf(k))):
                todo[crossed] = ((half,), over_core)
                flat.append(half)
                mirrored.append(crossed)
        pieces.append((flat, mirrored))
    own_one, mirrored_one = pieces[0]
    todo[n.put_own] = (tuple(own_one[:6]), put_own)
    todo[n.put_rest] = (
        (*own_one, *mirrored_one, n.put_own[2], free(n.put_own[0]), free(n.put_own[1])),
        put_rest,
    )
    todo[n.put_two] = (
        (*pieces[1][0], *pieces[1][1], n.put_rest[5], free(n.put_rest[1])),
        put_two,
    )
    todo[n.back_z1] = ((n.head_grad[1],), lambda v: over_z(v, 1))
    todo[n.back_z2] = (
        (n.head_grad[0], n.back_z1),
        lambda v, c: over_z(below(v[size:], c[size:]), 2),
    )
    todo[n.input_grad] = (
        (n.head_grad[0], n.back_z1, n.back_z2, n.middle[12]),
        input_grad,
    )
    todo[n.tiny_core] = (
        (n.middle[13], n.head_grad[4]),
        lambda u, v: below(u, v) + over_core(below(u, v)),
    )
    todo[n.tiny_x] = ((n.tiny_core,), lambda v: v + over_item(v, 1))
    todo[n.tiny_y] = ((n.tiny_x,), lambda v: v + over_item(v, 2))
    todo[n.tiny_z1] = ((n.tiny_y,), lambda v: v + over_z(v, 1))
    todo[n.tiny_z2] = ((n.tiny_z1,), lambda v: v + over_z(v, 2))
    def tiny_out(v):
        flat, cuts, at = v.reshape(-1), [], 0
        for length in (fan,) + (width,) * 8:
            cuts.append(flat[at : at + length])
            at += length
        return cuts

    todo[n.tiny_out] = ((n.tiny_z2,), tiny_out)
    made = run_steps(
        todo, {n.tokens: tokens[0], n.rand: rand_blocks, n.cot: cot}
    )
    layer_out, grad_tokens = made[n.layer_out], made[n.input_grad]
    grad_down, grad_qkv = made[n.put_rest][0], made[n.put_rest][2:5]
    grad_up, grad_out, _ = made[n.put_two]
    g_bu, g_fg, g_fs, g_bd, g_bo, g_ag, g_as, g_bq, g_bv = made[n.tiny_out]
    return (
        layer_out[None],
        grad_tokens[None],
        grad_qkv[0],
        grad_qkv[1],
        grad_qkv[2],
        grad_out,
        grad_up,
        grad_down,
        g_bq,
        g_bv,
        g_bo,
        g_bu,
        g_bd,
        g_ag,
        g_as,
        g_fg,
        g_fs,
    )


def per_device(tokens, rand_blocks, *rest):
    seqs, local_len, width = tokens.shape
    fan = rest[4].shape[1]
    fits = (
        seqs == 1
        and local_len == LANES
        and lax.axis_size("item") == GROUP
        and lax.axis_size("seq") == 2 * GROUP
        and HEADS % GROUP == 0
        and width == HEADS * HD
        and fan % (8 * LANES) == 0
        and width % (2 * LANES) == 0
    )
    chosen = split_device if fits else general_device
    return chosen(tokens, rand_blocks, *rest)


def solution(mesh):
    placed = (
        P("item", "seq", None),
        P(None, "item", None, None),
        P(),
        P(),
        P(),
        P(),
        P(),
        P(),
        P(),
        P(),
        P(),
        P(),
        P(),
        P(),
        P(),
        P(),
        P(),
        P("item", "seq", None),
    )
    return jax.shard_map(
        per_device,
        mesh=mesh,
        in_specs=placed,
        out_specs=(
            P("item", "seq", None),
            P("item", "seq", None),
            P(),
            P(),
            P(),
            P(),
            P(),
            P(),
            P(),
            P(),
            P(),
            P(),
            P(),
            P(),
            P(),
            P(),
            P(),
        ),
        check_vma=False,
    )
```

```python
import functools

import jax
import jax.numpy as jnp
from jax import lax
from jax.experimental import pallas as pl
from jax.experimental.pallas import tpu as pltpu
from jax.sharding import PartitionSpec as P

HEADS = 12
HD = 64
BLOCK = 64
RAND = 3


epsilon = 1e-05


def from_root(shard, axis, root):
    mine = lax.axis_index(axis) == root
    return lax.psum(jnp.where(mine, shard, jnp.zeros_like(shard)), axis)


def extended(block, sides, width):
    for axis, dim in sides:
        count = lax.axis_size(axis)
        forward = [(i, i + 1) for i in range(count - 1)]
        backward = [(target, source) for source, target in forward]
        low = lax.ppermute(
            lax.slice_in_dim(block, block.shape[dim] - width, None, axis=dim), axis, forward
        )
        high = lax.ppermute(lax.slice_in_dim(block, 0, width, axis=dim), axis, backward)
        block = jnp.concatenate([low, block, high], axis=dim)
    return block


def joined(shard, axis, join):
    gathered = jax.tree.map(
        lambda a, kind: lax.all_gather(a.astype(kind), axis),
        shard,
        (jnp.bfloat16, jnp.bfloat16, jnp.bfloat16),
    )

    def take(source):
        return jax.tree.map(
            lambda a, own: lax.dynamic_index_in_dim(a, source, 0, False).astype(own.dtype),
            gathered,
            shard,
        )

    return lax.fori_loop(
        1, lax.axis_size(axis), lambda source, state: join(state, take(source)), take(0)
    )


def entering(shard, axis, combine, identity, reverse):
    count, position = (lax.axis_size(axis), lax.axis_index(axis))
    everything = jax.tree.map(
        lambda part, kind: lax.all_gather(part.astype(kind), axis),
        shard,
        jax.tree.map(lambda a: jnp.bfloat16 if a.dtype == jnp.float32 else a.dtype, shard),
    )
    start = jax.tree.map(
        lambda part, zero: jnp.broadcast_to(jnp.asarray(zero, part.dtype), part.shape),
        shard,
        identity,
    )

    def step(k, before):
        at = count - 1 - k if reverse else k
        reached = at > position if reverse else at < position
        new = combine(
            before, jax.tree.map(lambda part, own: part[at].astype(own.dtype), everything, shard)
        )
        return jax.tree.map(lambda a, b: jnp.where(reached, a, b), new, before)

    return lax.fori_loop(0, count, step, start)


def layer_norm(values, norm_gain, norm_bias):
    center = values - jnp.mean(values, axis=-1, keepdims=True)
    spread = jnp.mean(center * center, axis=-1, keepdims=True)
    return center * lax.rsqrt(spread + epsilon) * norm_gain + norm_bias


def gelu_exact(values):
    return jax.nn.gelu(values, approximate=False)


def dense_rows(left, right):
    return jnp.dot(left, right, preferred_element_type=jnp.float32)


def dense_left(left, right):
    return lax.dot_general(
        left, right, (((0,), (0,)), ((), ())), preferred_element_type=jnp.float32
    )


def dense_back(left, right):
    return lax.dot_general(
        left, right, (((1,), (1,)), ((), ())), preferred_element_type=jnp.float32
    )


def mixed_sum(form, left, right):
    return jnp.einsum(form, left, right, preferred_element_type=jnp.float32)


def exact_sum(form, left, right):
    return jnp.einsum(
        form, left, right, precision=lax.Precision.HIGHEST, preferred_element_type=jnp.float32
    )


def from_ends(first_part, last_part):
    head_part = from_root(first_part, "seq", 0)
    tail_part = from_root(last_part, "seq", lax.axis_size("seq") - 1)
    return (head_part, tail_part)


def merge_rows(left_part, right_part):
    left_peak, left_total, left_sum = left_part
    right_peak, right_total, right_sum = right_part
    new_peak = jnp.maximum(left_peak, right_peak)
    left_scale = jnp.exp(left_peak - new_peak)
    right_scale = jnp.exp(right_peak - new_peak)
    return (
        new_peak,
        left_total * left_scale + right_total * right_scale,
        left_sum * left_scale[..., None] + right_sum * right_scale[..., None],
    )


def add_pair(earlier_sum, later_sum):
    return (earlier_sum[0] + later_sum[0], earlier_sum[1] + later_sum[1])


def general_device(
    tokens,
    rand_blocks,
    w_query,
    w_key,
    w_value,
    w_out,
    w_up,
    w_down,
    bias_query,
    bias_value,
    bias_out,
    bias_up,
    bias_down,
    attn_gain,
    attn_shift,
    ffn_gain,
    ffn_shift,
    cotangent,
):
    seq_here, local_len, model_width = tokens.shape
    blocks_all = rand_blocks.shape[0]
    devices = lax.axis_size("seq")
    position = lax.axis_index("seq")
    per_dev = blocks_all // devices
    slot_cap = max(2, seq_here * HEADS * RAND * 4 // (3 * blocks_all))
    pair_width = 2 * HD
    lane_count = seq_here * HEADS * RAND
    slot_size = BLOCK * pair_width
    rows_here = seq_here * local_len
    score_scale = HD ** (-0.5)

    def to_heads(values):
        return values.reshape(seq_here, per_dev, BLOCK, HEADS, -1).transpose(0, 1, 3, 2, 4)

    def from_heads(values):
        return values.transpose(0, 1, 3, 2, 4).reshape(rows_here, -1)

    inputs = tokens.reshape(rows_here, model_width).astype(jnp.float32)
    normed = layer_norm(inputs, attn_gain, attn_shift).astype(jnp.bfloat16)
    queries = (dense_rows(normed, w_query) + bias_query).astype(jnp.bfloat16)
    key_rows = dense_rows(normed, w_key).astype(jnp.bfloat16)
    value_rows = (dense_rows(normed, w_value) + bias_value).astype(jnp.bfloat16)
    kv_tokens = jnp.stack(
        [
            key_rows.reshape(seq_here, local_len, HEADS, HD),
            value_rows.reshape(seq_here, local_len, HEADS, HD),
        ],
        axis=3,
    ).reshape(seq_here, local_len, 2 * model_width)
    padded = extended(kv_tokens, (("seq", 1),), BLOCK)
    pad_blocks = padded.reshape(seq_here, per_dev + 2, BLOCK, HEADS, pair_width)
    window = jnp.stack(
        [pad_blocks[:, 0:per_dev], pad_blocks[:, 1 : per_dev + 1], pad_blocks[:, 2 : per_dev + 2]],
        axis=2,
    )
    window = window.transpose(0, 1, 4, 2, 3, 5).reshape(
        seq_here, per_dev, HEADS, 3 * BLOCK, pair_width
    )
    packed = jnp.concatenate([queries.reshape(seq_here, local_len, model_width), kv_tokens], axis=2)
    head_pack, tail_pack = from_ends(packed[:, :BLOCK], packed[:, local_len - BLOCK :])
    global_pack = jnp.stack([head_pack, tail_pack], axis=1)
    global_query = (
        global_pack[..., :model_width]
        .reshape(seq_here, 2, BLOCK, HEADS, HD)
        .transpose(0, 3, 1, 2, 4)
        .reshape(seq_here, HEADS, 2 * BLOCK, HD)
    )
    global_kv = (
        global_pack[..., model_width:]
        .reshape(seq_here, 2, BLOCK, HEADS, pair_width)
        .transpose(0, 3, 1, 2, 4)
        .reshape(seq_here, HEADS, 2 * BLOCK, pair_width)
    )
    flat_req = rand_blocks.reshape(blocks_all, lane_count)
    block_ids = jnp.arange(blocks_all, dtype=jnp.int32)
    live_rows = (block_ids != 0) & (block_ids != blocks_all - 1)
    own_blocks = position * per_dev + jnp.arange(per_dev, dtype=jnp.int32)
    matches = (
        (flat_req[:, :, None] == own_blocks[None, None, :]) & live_rows[:, None, None]
    ).astype(jnp.int32)
    order_rank = jnp.cumsum(matches, axis=1) - matches
    slot_ids = jnp.arange(slot_cap, dtype=jnp.int32)
    chosen = matches[..., None] * (order_rank[..., None] == slot_ids).astype(jnp.int32)
    lane_ids = jnp.arange(lane_count, dtype=jnp.int32)
    source_rows = lane_ids // (HEADS * RAND) * (per_dev * HEADS) + lane_ids // RAND % HEADS
    slot_live = jnp.sum(chosen, axis=1)
    slot_rows = (
        jnp.sum(chosen * source_rows[None, :, None, None], axis=1)
        + (jnp.arange(per_dev, dtype=jnp.int32) * HEADS)[None, :, None]
    )
    kv_heads = (
        kv_tokens.reshape(seq_here, per_dev, BLOCK, HEADS, pair_width)
        .transpose(0, 1, 3, 2, 4)
        .reshape(seq_here * per_dev * HEADS, slot_size)
    )
    served = jnp.take(kv_heads, slot_rows.reshape(-1), axis=0) * slot_live.reshape(-1, 1).astype(
        jnp.bfloat16
    )
    served = served.reshape(devices, per_dev, per_dev, slot_cap, slot_size)
    replies = lax.all_to_all(served, "seq", split_axis=0, concat_axis=0, tiled=True)
    fetched = replies.transpose(1, 0, 2, 3, 4).reshape(per_dev * blocks_all * slot_cap, slot_size)
    my_blocks = lax.dynamic_slice_in_dim(flat_req, position * per_dev, per_dev, 0)
    same_key = (my_blocks[:, :, None] == my_blocks[:, None, :]) & (
        lane_ids[None, None, :] < lane_ids[None, :, None]
    )
    my_ranks = jnp.sum(same_key.astype(jnp.int32), axis=2)
    pick_rows = (
        jnp.arange(per_dev, dtype=jnp.int32)[:, None] * blocks_all + my_blocks
    ) * slot_cap + my_ranks
    rand_kv = jnp.take(fetched, pick_rows.reshape(-1), axis=0).reshape(
        per_dev, seq_here, HEADS, RAND, BLOCK, pair_width
    )
    rand_kv = rand_kv.transpose(1, 0, 2, 3, 4, 5).reshape(
        seq_here, per_dev, HEADS, RAND * BLOCK, pair_width
    )
    global_kv_all = jnp.broadcast_to(
        global_kv[:, None], (seq_here, per_dev, HEADS, 2 * BLOCK, pair_width)
    )
    keys_all = jnp.concatenate([window, global_kv_all, rand_kv], axis=3)
    list_keys = keys_all[..., :HD]
    list_values = keys_all[..., HD:]
    query_heads = to_heads(queries)
    scores = mixed_sum("sjhqd,sjhkd->sjhqk", query_heads, list_keys) * score_scale
    row_peak = jnp.max(scores, axis=-1, keepdims=True)
    weights = jnp.exp(scores - row_peak)
    row_total = jnp.sum(weights, axis=-1, keepdims=True)
    near_out = (
        mixed_sum("sjhqk,sjhkd->sjhqd", weights.astype(jnp.bfloat16), list_values) / row_total
    )
    local_heads = kv_tokens.reshape(seq_here, per_dev, BLOCK, HEADS, pair_width).transpose(
        0, 3, 1, 2, 4
    )
    local_keys = local_heads[..., :HD]
    local_values = local_heads[..., HD:]
    global_scores = mixed_sum("shqd,shjkd->shqjk", global_query, local_keys) * score_scale
    block_peak = jnp.max(global_scores, axis=-1, keepdims=True)
    global_weights = jnp.exp(global_scores - block_peak)
    local_top = jnp.max(block_peak, axis=3, keepdims=True)
    factor = jnp.exp(block_peak - local_top)
    local_total = jnp.sum(factor * jnp.sum(global_weights, axis=-1, keepdims=True), axis=(3, 4))
    local_sum = jnp.sum(
        factor * mixed_sum("shqjk,shjkd->shqjd", global_weights.astype(jnp.bfloat16), local_values),
        axis=3,
    )
    global_top, global_total, global_sum = joined(
        (local_top[..., 0, 0], local_total, local_sum), "seq", merge_rows
    )
    global_ctx = global_sum / global_total[..., None]
    global_lse = global_top + jnp.log(global_total)
    block_here = jnp.arange(per_dev, dtype=jnp.int32)
    head_mask = ((position == 0) & (block_here == 0))[None, :, None, None, None]
    tail_mask = ((position == devices - 1) & (block_here == per_dev - 1))[None, :, None, None, None]
    context = jnp.where(head_mask, global_ctx[:, None, :, :BLOCK], near_out)
    context = jnp.where(tail_mask, global_ctx[:, None, :, BLOCK:], context)
    context_rows = from_heads(context).astype(jnp.bfloat16)
    middle = inputs + (dense_rows(context_rows, w_out) + bias_out)
    normed_two = layer_norm(middle, ffn_gain, ffn_shift).astype(jnp.bfloat16)
    hidden = dense_rows(normed_two, w_up) + bias_up
    active = gelu_exact(hidden).astype(jnp.bfloat16)
    layer_out = (
        (middle + dense_rows(active, w_down) + bias_down)
        .astype(jnp.bfloat16)
        .reshape(seq_here, local_len, model_width)
    )
    cot_rows = cotangent.reshape(rows_here, model_width)
    cot_float = cot_rows.astype(jnp.float32)
    grad_w_down = dense_left(active, cot_rows)
    grad_bias_down = jnp.sum(cot_float, axis=0)
    d_active = dense_back(cot_rows, w_down)
    gelu_pull = jax.vjp(gelu_exact, hidden)[1]
    d_hidden = gelu_pull(d_active)[0].astype(jnp.bfloat16)
    grad_w_up = dense_left(normed_two, d_hidden)
    grad_bias_up = jnp.sum(d_hidden.astype(jnp.float32), axis=0)
    norm_pull_two = jax.vjp(layer_norm, middle, ffn_gain, ffn_shift)[1]
    d_middle_norm, grad_ffn_gain, grad_ffn_shift = norm_pull_two(dense_back(d_hidden, w_up))
    d_middle = cot_float + d_middle_norm
    d_attended = d_middle.astype(jnp.bfloat16)
    grad_w_out = dense_left(context_rows, d_attended)
    grad_bias_out = jnp.sum(d_attended.astype(jnp.float32), axis=0)
    d_context = dense_back(d_attended, w_out).astype(jnp.bfloat16)
    d_tokens = d_context.reshape(seq_here, local_len, model_width)
    head_grad, tail_grad = from_ends(d_tokens[:, :BLOCK], d_tokens[:, local_len - BLOCK :])
    d_heads = jnp.where(head_mask | tail_mask, jnp.zeros((), jnp.bfloat16), to_heads(d_context))
    d_float = d_heads.astype(jnp.float32)
    row_delta = jnp.sum(d_float * near_out, axis=-1, keepdims=True)
    scores = mixed_sum("sjhqd,sjhkd->sjhqk", query_heads, list_keys) * score_scale
    weights = jnp.exp(scores - row_peak)
    d_weights = mixed_sum("sjhqd,sjhkd->sjhqk", d_heads, list_values)
    d_scores = (weights / row_total * (d_weights - row_delta)).astype(jnp.bfloat16)
    d_query = mixed_sum("sjhqk,sjhkd->sjhqd", d_scores, list_keys) * score_scale
    d_list_keys = mixed_sum("sjhqk,sjhqd->sjhkd", d_scores, query_heads) * score_scale
    d_list_values = exact_sum(
        "sjhqk,sjhqd->sjhkd", weights.astype(jnp.bfloat16).astype(jnp.float32), d_float / row_total
    )
    d_kv = jnp.concatenate([d_list_keys, d_list_values], axis=-1)
    d_window = d_kv[:, :, :, : 3 * BLOCK].reshape(seq_here, per_dev, HEADS, 3, BLOCK, pair_width)
    keep_dims = ((0, 0), (0, 0), (0, 0))
    spread_sum = jnp.pad(d_window[:, :, :, 0], ((0, 0), (0, 2)) + keep_dims)
    spread_sum = spread_sum + jnp.pad(d_window[:, :, :, 1], ((0, 0), (1, 1)) + keep_dims)
    spread_sum = spread_sum + jnp.pad(d_window[:, :, :, 2], ((0, 0), (2, 0)) + keep_dims)
    own_grad = spread_sum[:, 1 : per_dev + 1]
    rim_grad = jnp.concatenate(
        [spread_sum[:, 0:1], spread_sum[:, per_dev + 1 : per_dev + 2]], axis=1
    )
    rim_grad = rim_grad.transpose(0, 1, 3, 2, 4).reshape(seq_here, 2 * BLOCK, 2 * model_width)
    back_rim = extended(rim_grad.astype(jnp.bfloat16), (("seq", 1),), BLOCK).astype(rim_grad.dtype)
    from_left = (
        back_rim[:, :BLOCK].reshape(seq_here, BLOCK, HEADS, pair_width).transpose(0, 2, 1, 3)
    )
    from_right = (
        back_rim[:, 3 * BLOCK :].reshape(seq_here, BLOCK, HEADS, pair_width).transpose(0, 2, 1, 3)
    )
    own_grad = own_grad.at[:, 0].add(from_left).at[:, per_dev - 1].add(from_right)
    global_part = jnp.sum(d_kv[:, :, :, 3 * BLOCK : 5 * BLOCK], axis=1)
    rand_part = d_kv[:, :, :, 5 * BLOCK :].reshape(seq_here, per_dev, HEADS, RAND, slot_size)
    rand_part = rand_part.transpose(1, 0, 2, 3, 4).reshape(per_dev * lane_count, slot_size)
    slot_grads = (
        jnp.zeros((per_dev * blocks_all * slot_cap, slot_size), jnp.float32)
        .at[pick_rows.reshape(-1)]
        .add(rand_part)
    )
    slot_grads = slot_grads.reshape(per_dev, devices, per_dev, slot_cap, slot_size).transpose(
        1, 0, 2, 3, 4
    )
    returned = lax.all_to_all(
        slot_grads.astype(jnp.bfloat16), "seq", split_axis=0, concat_axis=0, tiled=True
    ).astype(slot_grads.dtype)
    dump_row = seq_here * per_dev * HEADS
    targets = jnp.where(slot_live > 0, slot_rows, dump_row).reshape(-1)
    collected = (
        jnp.zeros((dump_row + 1, slot_size), jnp.float32)
        .at[targets]
        .add(returned.reshape(-1, slot_size))
    )
    own_grad = own_grad + collected[:dump_row].reshape(seq_here, per_dev, HEADS, BLOCK, pair_width)
    global_grad = (
        jnp.stack([head_grad, tail_grad], axis=1)
        .reshape(seq_here, 2, BLOCK, HEADS, HD)
        .transpose(0, 3, 1, 2, 4)
        .reshape(seq_here, HEADS, 2 * BLOCK, HD)
    )
    global_float = global_grad.astype(jnp.float32)
    global_delta = jnp.sum(global_float * global_ctx, axis=-1)
    global_scores = mixed_sum("shqd,shjkd->shqjk", global_query, local_keys) * score_scale
    global_weights = jnp.exp(global_scores - block_peak)
    coefficient = jnp.exp(block_peak - global_lse[..., None, None])
    global_probs = global_weights * coefficient
    global_dweights = mixed_sum("shqd,shjkd->shqjk", global_grad, local_values)
    global_dscores = (global_probs * (global_dweights - global_delta[..., None, None])).astype(
        jnp.bfloat16
    )
    d_global_query = mixed_sum("shqjk,shjkd->shqd", global_dscores, local_keys) * score_scale
    d_local_keys = mixed_sum("shqjk,shqd->shjkd", global_dscores, global_query) * score_scale
    d_local_values = exact_sum(
        "shqjk,shqd->shjkd",
        global_weights.astype(jnp.bfloat16).astype(jnp.float32) * coefficient,
        global_float,
    )
    own_grad = own_grad + jnp.concatenate([d_local_keys, d_local_values], axis=-1).transpose(
        0, 2, 1, 3, 4
    )
    head_terms = (d_global_query[:, :, :BLOCK], global_part[:, :, :BLOCK])
    tail_terms = (d_global_query[:, :, BLOCK:], global_part[:, :, BLOCK:])
    zero_terms = (jnp.zeros_like(head_terms[0]), jnp.zeros_like(head_terms[1]))
    head_rest = entering(head_terms, "seq", add_pair, zero_terms, True)
    tail_rest = entering(tail_terms, "seq", add_pair, zero_terms, False)
    head_full = add_pair(head_rest, head_terms)
    tail_full = add_pair(tail_rest, tail_terms)
    d_query = (
        d_query
        + jnp.where(head_mask, head_full[0][:, None], 0.0)
        + jnp.where(tail_mask, tail_full[0][:, None], 0.0)
    )
    own_grad = (
        own_grad
        + jnp.where(head_mask, head_full[1][:, None], 0.0)
        + jnp.where(tail_mask, tail_full[1][:, None], 0.0)
    )
    d_query_rows = from_heads(d_query).astype(jnp.bfloat16)
    kv_grad = own_grad.transpose(0, 1, 3, 2, 4).reshape(rows_here, HEADS, pair_width)
    d_key_rows = kv_grad[..., :HD].reshape(rows_here, model_width).astype(jnp.bfloat16)
    d_value_rows = kv_grad[..., HD:].reshape(rows_here, model_width).astype(jnp.bfloat16)
    grad_w_query = dense_left(normed, d_query_rows)
    grad_bias_query = jnp.sum(d_query_rows.astype(jnp.float32), axis=0)
    grad_w_key = dense_left(normed, d_key_rows)
    grad_w_value = dense_left(normed, d_value_rows)
    grad_bias_value = jnp.sum(d_value_rows.astype(jnp.float32), axis=0)
    d_normed = (
        dense_back(d_query_rows, w_query)
        + dense_back(d_key_rows, w_key)
        + dense_back(d_value_rows, w_value)
    )
    norm_pull_one = jax.vjp(layer_norm, inputs, attn_gain, attn_shift)[1]
    d_inputs_norm, grad_attn_gain, grad_attn_shift = norm_pull_one(d_normed)
    grad_tokens = (
        (d_middle + d_inputs_norm).astype(jnp.bfloat16).reshape(seq_here, local_len, model_width)
    )
    grad_list = [
        grad_w_query,
        grad_w_key,
        grad_w_value,
        grad_w_out,
        grad_w_up,
        grad_w_down,
        grad_bias_query,
        grad_bias_value,
        grad_bias_out,
        grad_bias_up,
        grad_bias_down,
        grad_attn_gain,
        grad_attn_shift,
        grad_ffn_gain,
        grad_ffn_shift,
    ]
    flattened = jnp.concatenate([member.reshape(-1) for member in grad_list])
    item_count = lax.axis_size("item")
    length_all = flattened.shape[0]
    stride_all = 128 * item_count * devices
    padded_len = (length_all + stride_all - 1) // stride_all * stride_all
    lead_pad = padded_len - length_all
    grad_grid = jnp.pad(flattened, (lead_pad, 0)).reshape(-1, 128)
    shared_rows = lax.psum_scatter(grad_grid, ("item", "seq"), scatter_dimension=0, tiled=True)
    summed = (
        lax.all_gather(shared_rows.astype(jnp.bfloat16), ("item", "seq"), axis=0, tiled=True)
        .astype(shared_rows.dtype)
        .reshape(-1)
    )
    results = []
    offset = lead_pad
    for member in grad_list:
        results.append(summed[offset : offset + member.size].reshape(member.shape))
        offset = offset + member.size
    return (
        layer_out,
        grad_tokens,
        results[0],
        results[1],
        results[2],
        results[3],
        results[4],
        results[5],
        results[6],
        results[7],
        results[8],
        results[9],
        results[10],
        results[11],
        results[12],
        results[13],
        results[14],
    )


LANES = 128
GROUP = 4
FAR = -1e30
BF = jnp.bfloat16
F32 = jnp.float32
VMEM_ASK = 56 * 1024 * 1024


def over_z(value, step):
    count = lax.axis_size("seq")
    return lax.ppermute(value, "seq", [(i, i ^ (2 * step)) for i in range(count)])


def over_core(value):
    count = lax.axis_size("seq")
    return lax.ppermute(value, "seq", [(i, i ^ 1) for i in range(count)])


def over_item(value, step):
    count = lax.axis_size("item")
    return lax.ppermute(value, "item", [(i, i ^ step) for i in range(count)])


def params(**more):
    return pltpu.CompilerParams(vmem_limit_bytes=VMEM_ASK, **more)


def vmem(count):
    return [pl.BlockSpec(memory_space=pltpu.VMEM)] * count


def cost(flops, moved, special=0):
    return pl.CostEstimate(flops=flops, bytes_accessed=moved, transcendentals=special)


LIGHT = cost(10**6, 10**5)


def dot_nn(left, right):
    return lax.dot_general(left, right, (((1,), (0,)), ((), ())), preferred_element_type=F32)


def dot_tn(left, right):
    return lax.dot_general(left, right, (((0,), (0,)), ((), ())), preferred_element_type=F32)


def dot_nt(left, right):
    return lax.dot_general(left, right, (((1,), (1,)), ((), ())), preferred_element_type=F32)


def attend_kernel(heads, *refs):
    own, other, mult_ref = refs[:4], refs[4:8], refs[8]
    ctx_refs, out_ref, lse_ref = refs[9:13], refs[13], refs[14]
    width = heads * HD
    for h in range(heads):
        low = h * HD
        query = jnp.concatenate([r[low : low + HD, :] for r in own], axis=1)
        key = jnp.concatenate(
            [r[width + low : width + low + HD, :] for r in own]
            + [r[low : low + HD, :] for r in other],
            axis=1,
        )
        value = jnp.concatenate(
            [r[2 * width + low : 2 * width + low + HD, :] for r in own]
            + [r[width + low : width + low + HD, :] for r in other],
            axis=1,
        )
        rows, lanes = key.shape[1], query.shape[1]
        scores = dot_tn(key, query) * (HD**-0.5)
        scores = scores.reshape(rows // BLOCK, BLOCK, lanes)
        mult = mult_ref[h][:, None, :]
        scores = jnp.where(mult > 0.0, scores, FAR)
        peak = jnp.max(jnp.max(scores, axis=0), axis=0, keepdims=True)
        weights = jnp.exp(scores - peak[None]) * mult
        total = jnp.sum(jnp.sum(weights, axis=0), axis=0, keepdims=True)
        packed = weights.astype(BF).reshape(rows, lanes)
        out = dot_nn(value, packed) / total
        out_ref[low : low + HD, :] = out
        lse_ref[h] = peak + jnp.log(total)
        rounded = out.astype(BF)
        for k in range(4):
            ctx_refs[k][low : low + HD, :] = rounded[:, k * LANES : (k + 1) * LANES]


def attend_back_kernel(heads, *refs):
    own, other, mult_ref, out_ref, lse_ref = refs[:4], refs[4:8], refs[8], refs[9], refs[10]
    grad_refs = refs[11:14]
    dq_ref, dkv_ref, far_ref = refs[14:17]
    width = heads * HD
    for h in range(heads):
        low = h * HD
        query = jnp.concatenate([r[low : low + HD, :] for r in own], axis=1)
        key = jnp.concatenate(
            [r[width + low : width + low + HD, :] for r in own]
            + [r[low : low + HD, :] for r in other],
            axis=1,
        )
        value = jnp.concatenate(
            [r[2 * width + low : 2 * width + low + HD, :] for r in own]
            + [r[width + low : width + low + HD, :] for r in other],
            axis=1,
        )
        grad = jnp.concatenate(
            [r[low : low + HD, :] for r in grad_refs]
            + [grad_refs[2][width + low : width + low + HD, :]],
            axis=1,
        )
        rows, lanes = key.shape[1], query.shape[1]
        scale = HD**-0.5
        scores = dot_tn(key, query) * scale
        scores = scores.reshape(rows // BLOCK, BLOCK, lanes)
        mult = mult_ref[h][:, None, :]
        scores = jnp.where(mult > 0.0, scores, FAR)
        probs = jnp.exp(scores - lse_ref[h][None]) * mult
        delta = jnp.sum(grad.astype(F32) * out_ref[low : low + HD, :], axis=0, keepdims=True)
        d_probs = dot_tn(value, grad).reshape(rows // BLOCK, BLOCK, lanes)
        d_scores = (probs * (d_probs - delta[None])).astype(BF).reshape(rows, lanes)
        packed = probs.astype(BF).reshape(rows, lanes)
        dq_ref[low : low + HD, :] = (dot_nn(key, d_scores) * scale).astype(BF)
        d_key = dot_nt(query, d_scores) * scale
        d_value = dot_nt(grad, packed)
        half = rows // 2
        dkv_ref[low : low + HD, :] = d_key[:, :half]
        dkv_ref[width + low : width + low + HD, :] = d_value[:, :half]
        far_ref[low : low + HD, :] = d_key[:, half:].astype(BF)
        far_ref[width + low : width + low + HD, :] = d_value[:, half:].astype(BF)


def norm_parts(values):
    center = values - jnp.mean(values, axis=-1, keepdims=True)
    rate = lax.rsqrt(jnp.mean(center * center, axis=-1, keepdims=True) + epsilon)
    return center * rate, rate


def line(ref, start=0, size=None):
    size = ref.shape[0] if size is None else size
    return ref[start : start + size].reshape(1, size)


def lay_rows(out, at, vector):
    for b in range(vector.shape[1] // LANES):
        out[at + b : at + b + 1, :] = vector[:, b * LANES : (b + 1) * LANES]
    return at + vector.shape[1] // LANES


def project_kernel(
    place_ref, tokens_ref, wq_ref, wk_ref, wv_ref, bq_ref, bv_ref, gain_ref, shift_ref,
    hat_ref, cut0, cut1, cut2, cut3, held, turned, sems,
):
    chip = place_ref[0]
    width = tokens_ref.shape[1]
    part = width // GROUP
    copies = [
        pltpu.make_async_copy(ref, held.at[n], sems.at[n])
        for n, ref in enumerate((wq_ref, wk_ref, wv_ref))
    ]
    for copy in copies:
        copy.start()
    hat, _ = norm_parts(tokens_ref[...].astype(F32))
    hat_ref[...] = hat.astype(BF)
    normed = (hat * line(gain_ref) + line(shift_ref)).astype(BF)
    biases = (bq_ref, None, bv_ref)
    for n, copy in enumerate(copies):
        copy.wait()
        rows = dot_nn(normed, held[n])
        if biases[n] is not None:
            rows = rows + line(biases[n])
        turned[n * width : (n + 1) * width, :] = rows.astype(BF).T
    for k, ref in enumerate((cut0, cut1, cut2, cut3)):
        for n in range(3):
            at = pl.multiple_of(n * width + (chip ^ k) * part, part)
            ref[n * part : (n + 1) * part, :] = turned[pl.ds(at, part), :]


def mult_kernel(heads, blocks_all, place_ref, rand_ref, mult_ref):
    chip, core = place_ref[0], place_ref[2]
    rows, lanes = mult_ref.shape[1], mult_ref.shape[2]
    spot = lax.broadcasted_iota(jnp.int32, (rows, BLOCK), 0)
    side = jnp.where(spot < rows // 2, core, 1 - core)
    key_ids = 4 * (chip ^ ((spot >> 1) & 3)) + 2 * side + (spot & 1)
    one = lambda hit: jnp.where(hit, 1.0, 0.0)
    ends = one(key_ids == 0) + one(key_ids == blocks_all - 1)
    for r in range(lanes // BLOCK):
        query = 4 * (chip ^ (r // 2)) + 2 * core + (r % 2)
        fixed = ends + one(key_ids == query - 1) + one(key_ids == query) + one(key_ids == query + 1)
        whole = (query == 0) | (query == blocks_all - 1)
        for h in range(heads):
            total = fixed
            for n in range(RAND):
                named = rand_ref[query * (HEADS * RAND) + (chip * heads + h) * RAND + n]
                total = total + one(key_ids == named)
            total = jnp.where(whole, jnp.ones_like(total), total)
            mult_ref[h, :, r * BLOCK : (r + 1) * BLOCK] = total


def middle_kernel(
    place_ref, tokens_ref, ctx0, ctx1, ctx2, ctx3, w_out_hbm, b_out_ref, gain_ref, shift_ref,
    w_up_hbm, b_up_ref, d_active_hbm, cot_ref,
    down0, down1, down2, down3, up0, up1, up2, up3, back0, back1,
    middle_ref, active_ref, d_middle_ref, tiny_ref,
    ctx_full, active_t, d_hidden_f, d_att_f, d_ctx_full, w_out_ref, w_up_ref, d_active_ref, sems,
):
    chip, item = place_ref[0], place_ref[1]
    rows, width = tokens_ref.shape
    part = width // GROUP
    fan = w_up_ref.shape[1]
    chunk = width
    chunks = fan // chunk
    out_copy = pltpu.make_async_copy(w_out_hbm, w_out_ref, sems.at[0])
    out_copy.start()
    copies = []
    for j in range(chunks):
        cols = slice(j * chunk, (j + 1) * chunk)
        up_copy = pltpu.make_async_copy(w_up_hbm.at[:, cols], w_up_ref.at[:, cols], sems.at[1 + j])
        act_copy = pltpu.make_async_copy(
            d_active_hbm.at[:, cols], d_active_ref.at[:, cols], sems.at[1 + chunks + j]
        )
        up_copy.start()
        act_copy.start()
        copies.append((up_copy, act_copy))
    for k, ref in enumerate((ctx0, ctx1, ctx2, ctx3)):
        at = pl.multiple_of((chip ^ k) * part, part)
        ctx_full[pl.ds(at, part), :] = ref[...]
    context = ctx_full[...]
    out_copy.wait()
    middle = tokens_ref[...].astype(F32) + (dot_tn(context, w_out_ref[...]) + line(b_out_ref))
    middle_ref[...] = middle
    hat, rate = norm_parts(middle)
    normed = (hat * line(gain_ref) + line(shift_ref)).astype(BF)
    at = 0
    d_norm = jnp.zeros((rows, width), F32)
    for j in range(chunks):
        cols = slice(j * chunk, (j + 1) * chunk)
        copies[j][0].wait()
        hidden = dot_nn(normed, w_up_ref[:, cols]) + line(b_up_ref, j * chunk, chunk)
        bell = 0.5 * (1.0 + lax.erf(hidden * (0.5**0.5)))
        active = (hidden * bell).astype(BF)
        active_ref[:, cols] = active
        active_t[cols, :] = active.T
        slope = bell + hidden * jnp.exp(-0.5 * hidden * hidden) * 0.3989422804014327
        copies[j][1].wait()
        d_hidden = (d_active_ref[:, cols] * slope).astype(BF)
        at = lay_rows(tiny_ref, at, jnp.sum(d_hidden.astype(F32), axis=0, keepdims=True))
        for b in range(chunk // LANES):
            to = j * chunk + b * LANES
            d_hidden_f[to : to + LANES, :] = d_hidden[:, b * LANES : (b + 1) * LANES]
        d_norm = d_norm + dot_nt(d_hidden, w_up_ref[:, cols])
    at = lay_rows(tiny_ref, at, jnp.sum(d_norm * hat, axis=0, keepdims=True))
    at = lay_rows(tiny_ref, at, jnp.sum(d_norm, axis=0, keepdims=True))
    scaled = d_norm * line(gain_ref)
    cot = cot_ref[...].astype(F32)
    at = lay_rows(tiny_ref, at, jnp.sum(cot, axis=0, keepdims=True))
    d_middle = cot + rate * (
        scaled
        - jnp.mean(scaled, axis=-1, keepdims=True)
        - hat * jnp.mean(scaled * hat, axis=-1, keepdims=True)
    )
    d_middle_ref[...] = d_middle
    d_attended = d_middle.astype(BF)
    at = lay_rows(tiny_ref, at, jnp.sum(d_attended.astype(F32), axis=0, keepdims=True))
    d_ctx_full[...] = dot_nt(w_out_ref[...], d_attended).astype(BF)
    for k in range(GROUP):
        at = pl.multiple_of((chip ^ k) * part, part)
        ref = (back0, back1)[k % 2]
        ref[k // 2 * part : (k // 2 + 1) * part, :] = d_ctx_full[pl.ds(at, part), :]
    normed_t = normed.T
    quarter, mid = fan // 8, width // 2
    for b in range(width // LANES):
        d_att_f[b * LANES : (b + 1) * LANES, :] = d_attended[:, b * LANES : (b + 1) * LANES]
    early = LANES
    late = quarter - early
    for k, (first, second) in enumerate(zip((down0, down1, down2, down3), (up0, up1, up2, up3))):
        target = item ^ k
        for c in range(2):
            at = pl.multiple_of(c * (fan // 2) + target * quarter, quarter)
            first[c * quarter : (c + 1) * quarter, :] = active_t[pl.ds(at, quarter), :]
            to = 2 * quarter + width + c * early
            first[to : to + early, :] = d_hidden_f[pl.ds(at, early), :]
            at = pl.multiple_of(c * (fan // 2) + target * quarter + early, early)
            second[c * late : (c + 1) * late, :] = d_hidden_f[pl.ds(at, late), :]
            at = pl.multiple_of((2 * c + (target & 1)) * part, part)
            to = 2 * late + c * part
            second[to : to + part, :] = ctx_full[pl.ds(at, part), :]
        first[2 * quarter : 2 * quarter + width, :] = normed_t
        at = pl.multiple_of((target >> 1) * mid, mid)
        to = 2 * late + 2 * part
        second[to : to + mid, :] = d_att_f[pl.ds(at, mid), :]


ROUND = (0, 2, 1, 3)


def hand_out(chip, out_ref, at, size, grads):
    for z in range(GROUP):
        k = chip ^ z
        row = ((k >> 1) | ((k & 1) << 1)) * size
        here = at
        for grad in grads:
            share = grad.shape[0] // GROUP
            for b in range(grad.shape[1] // LANES):
                out_ref[pl.ds(pl.multiple_of(row + here, 16), share), :] = grad[
                    z * share : (z + 1) * share, b * LANES : (b + 1) * LANES
                ].astype(out_ref.dtype)
                here += share
    return here


def first_grad_kernel(place_ref, *refs):
    pieces, cots, kept_ref, given_ref = refs[:4], refs[4:8], refs[8], refs[9]
    down_left, down_right, up_left, up_right = refs[10:]
    chip, core = place_ref[0], place_ref[2]
    quarter, width, early = down_left.shape[0] // 2, up_left.shape[0], up_right.shape[1] // 2
    for s, piece in enumerate(pieces):
        span = slice(s * LANES, (s + 1) * LANES)
        down_left[:, span] = piece[: 2 * quarter, :]
        down_right[span, :] = cots[s][...]
        up_left[:, span] = piece[2 * quarter : 2 * quarter + width, :]
        for c in range(2 * early // LANES):
            low = 2 * quarter + width + c * LANES
            up_right[span, c * LANES : (c + 1) * LANES] = piece[low : low + LANES, :]
    size = kept_ref.shape[0] // GROUP
    for half, ref in ((1 - core, given_ref), (core, kept_ref)):
        rows = pl.ds(pl.multiple_of(half * quarter, quarter), quarter)
        cols = pl.ds(pl.multiple_of(half * early, early), early)
        grad_down = dot_nn(down_left[rows, :], down_right[...])
        at = hand_out(chip, ref, 0, size, (grad_down,))
        hand_out(chip, ref, at, size, (dot_nn(up_left[...], up_right[:, cols]),))


def second_grad_kernel(place_ref, *refs):
    firsts, pieces, kept_ref, given_ref = refs[:4], refs[4:8], refs[8], refs[9]
    up_left, up_right, out_left, out_right = refs[10:]
    chip, core = place_ref[0], place_ref[2]
    width, late = up_left.shape[0], up_right.shape[1] // 2
    part, mid = out_left.shape[0] // 2, out_right.shape[1]
    skip = firsts[0].shape[0] - width - 2 * LANES
    for s, piece in enumerate(pieces):
        span = slice(s * LANES, (s + 1) * LANES)
        up_left[:, span] = firsts[s][skip : skip + width, :]
        for b in range(2 * late // LANES):
            up_right[span, b * LANES : (b + 1) * LANES] = piece[b * LANES : (b + 1) * LANES, :]
        out_left[:, span] = piece[2 * late : 2 * late + 2 * part, :]
        for b in range(mid // LANES):
            low = 2 * late + 2 * part + b * LANES
            out_right[span, b * LANES : (b + 1) * LANES] = piece[low : low + LANES, :]
    size = kept_ref.shape[0] // GROUP
    for half, ref in ((1 - core, given_ref), (core, kept_ref)):
        rows = pl.ds(pl.multiple_of(half * part, part), part)
        cols = pl.ds(pl.multiple_of(half * late, late), late)
        at = hand_out(chip, ref, 0, size, (dot_nn(up_left[...], up_right[:, cols]),))
        hand_out(chip, ref, at, size, (dot_nn(out_left[rows, :], out_right[...]),))


def head_grad_kernel(
    place_ref, dq_ref, dkv_ref, far_ref, hat0, hat1, gain_ref, shift_ref, wq_hbm, wk_hbm, wv_hbm,
    back0, back1, kept_ref, given_ref, tiny_ref,
    d_heads, normed, grad, padded, window, sems,
):
    chip, core = place_ref[0], place_ref[2]
    part, tokens = dq_ref.shape
    width = normed.shape[1]
    wide = padded.shape[1]
    off = pl.multiple_of((chip & 1) * HD, HD)
    begin = pl.multiple_of(chip * part - off, LANES)
    copies = [
        pltpu.make_async_copy(w.at[:, pl.ds(begin, wide)], window.at[n], sems.at[n])
        for n, w in enumerate((wq_hbm, wk_hbm, wv_hbm))
    ]
    for copy in copies:
        copy.start()
    d_heads[:part, :] = dq_ref[...]
    d_heads[part:, :] = (dkv_ref[...] + far_ref[...].astype(F32)).astype(BF)
    padded[...] = jnp.zeros(padded.shape, BF)
    for n in range(3):
        padded[n, pl.ds(off, part), :] = d_heads[n * part : (n + 1) * part, :]
    hats = [((hat0, hat1)[k % 2], k // 2 * LANES) for k in range(GROUP)]
    for k, (hat, at) in enumerate(hats):
        span = slice(k * LANES, (k + 1) * LANES)
        back, row = (back0, back1)[k % 2], k // 2 * 3 * part
        back[row : row + 3 * part, :] = d_heads[:, span]
        rows = hat[at : at + LANES, :].astype(F32) * line(gain_ref) + line(shift_ref)
        normed[span, :] = rows.astype(BF)
    grad[...] = dot_nn(d_heads[...], normed[...])
    mid, rows = width // 2, 3 * part // GROUP
    for b in range(mid // LANES):
        mine = grad[:, pl.ds(pl.multiple_of(core * mid + b * LANES, LANES), LANES)]
        theirs = grad[:, pl.ds(pl.multiple_of((1 - core) * mid + b * LANES, LANES), LANES)]
        for q in range(GROUP):
            at = (q * (mid // LANES) + b) * rows
            kept_ref[at : at + rows, :] = mine[q * rows : (q + 1) * rows, :]
            given_ref[at : at + rows, :] = theirs[q * rows : (q + 1) * rows, :].astype(BF)
    for copy in copies:
        copy.wait()
    turned = [padded[n].T for n in range(3)]
    gain_grad = jnp.zeros((1, width), F32)
    shift_grad = jnp.zeros((1, width), F32)
    for k, (hat, at) in enumerate(hats):
        span = slice(k * LANES, (k + 1) * LANES)
        d_norm = dot_nt(turned[0][span, :], window[0])
        d_norm = d_norm + dot_nt(turned[1][span, :], window[1])
        d_norm = d_norm + dot_nt(turned[2][span, :], window[2])
        rows = hat[at : at + LANES, :].astype(F32)
        gain_grad = gain_grad + jnp.sum(d_norm * rows, axis=0, keepdims=True)
        shift_grad = shift_grad + jnp.sum(d_norm, axis=0, keepdims=True)
    at = lay_rows(tiny_ref, 0, gain_grad)
    at = lay_rows(tiny_ref, at, shift_grad)
    ones = jnp.ones((8, tokens), BF)
    for n in (0, 2):
        sums = dot_nt(ones, padded[n])
        for r in range(width // LANES):
            value = jnp.zeros((1, LANES), F32)
            for m in range(wide // LANES):
                here = sums[:1, m * LANES : (m + 1) * LANES]
                value = value + jnp.where(begin == (r - m) * LANES, here, 0.0)
            tiny_ref[at : at + 1, :] = value
            at += 1


def input_grad_kernel(
    place_ref, back0, back1, back2, wq_hbm, wk_hbm, wv_hbm, tokens_ref, d_middle_ref,
    gain_ref, grad_ref, held, turned, sems,
):
    chip = place_ref[0]
    rows, width = tokens_ref.shape
    part = width // GROUP
    copies = [
        pltpu.make_async_copy(ref, held.at[n], sems.at[n])
        for n, ref in enumerate((wq_hbm, wk_hbm, wv_hbm))
    ]
    for copy in copies:
        copy.start()
    for k, ref in enumerate((back0, back1, back2, back2)):
        base = 3 * part if k == 3 else 0
        for n in range(3):
            at = pl.multiple_of(n * width + (chip ^ k) * part, part)
            turned[pl.ds(at, part), :] = ref[base + n * part : base + (n + 1) * part, :]
    d_norm = jnp.zeros((width, rows), F32)
    for n, copy in enumerate(copies):
        copy.wait()
        d_norm = d_norm + dot_nn(held[n], turned[n * width : (n + 1) * width, :])
    d_norm = d_norm.T
    hat, rate = norm_parts(tokens_ref[...].astype(F32))
    scaled = d_norm * line(gain_ref)
    d_inputs = rate * (
        scaled
        - jnp.mean(scaled, axis=-1, keepdims=True)
        - hat * jnp.mean(scaled * hat, axis=-1, keepdims=True)
    )
    grad_ref[...] = (d_middle_ref[...] + d_inputs).astype(BF)


def put_halves(layout, size, which, place_ref, halves, boxes, targets, sems):
    chip, item, core = place_ref[0], place_ref[1], place_ref[2]
    leaving = []
    for piece, (flip, step) in enumerate(which):
        side, place = core ^ flip, item ^ step
        known = (side * GROUP + place, 2 * side + (place & 1), place >> 1)
        for k in range(GROUP):
            at = k // 2 * size
            for (share, blocks, *_), box in zip(layout, boxes):
                to = pl.multiple_of((chip ^ k) * share, share)
                for b in range(blocks):
                    box[piece, pl.ds(to, share), b * LANES : (b + 1) * LANES] = halves[
                        2 * piece + k % 2
                    ][at : at + share, :].astype(F32)
                    at += share
        for n, (share, blocks, row, column, unit, first) in enumerate(layout):
            tall, wide = GROUP * share, blocks * LANES
            target = targets[n]
            if row is not None:
                start = pl.multiple_of(known[row] * tall, tall)
                target = target.at[pl.ds(start, tall), :]
            if column is not None:
                start = pl.multiple_of(known[column] * unit + first, LANES)
                target = target.at[:, pl.ds(start, wide)]
            copy = pltpu.make_async_copy(boxes[n].at[piece], target, sems.at[piece, n])
            copy.start()
            leaving.append(copy)
    return leaving


def put_pieces_kernel(layout, size, which, place_ref, *refs):
    outs = len(layout)
    halves = refs[: 2 * len(which)]
    boxes, sems = refs[-1 - outs : -1], refs[-1]
    done = refs[-2 - outs]
    targets = refs[-2 - 2 * outs : -2 - outs]
    done[...] = jnp.zeros(done.shape, F32)
    for copy in put_halves(layout, size, which, place_ref, halves, boxes, targets, sems):
        copy.wait()


def put_heads(size, skip, place_ref, flip, halves, whole, held, targets, sems):
    chip, item = place_ref[0], place_ref[1]
    mid = whole.shape[2]
    part = whole.shape[1] // (3 * GROUP)
    rows = 3 * part // GROUP
    for k in range(GROUP):
        for z in range(GROUP):
            to = pl.multiple_of((chip ^ z) * (3 * part) + (item ^ k) * rows, 16)
            for b in range(mid // LANES):
                at = z // 2 * size + skip + b * rows
                whole[flip, pl.ds(to, rows), b * LANES : (b + 1) * LANES] = halves[2 * k + z % 2][
                    at : at + rows, :
                ]
    leaving = []
    for b in range(mid // LANES):
        start = pl.multiple_of((place_ref[2] ^ flip) * mid + b * LANES, LANES)
        for n, target in enumerate(targets):
            tall = jnp.concatenate(
                [
                    whole[
                        flip,
                        z * 3 * part + n * part : z * 3 * part + (n + 1) * part,
                        b * LANES : (b + 1) * LANES,
                    ]
                    for z in range(GROUP)
                ],
                axis=0,
            )
            held[flip, n, b] = tall.T.astype(F32)
            copy = pltpu.make_async_copy(
                held.at[flip, n, b], target.at[pl.ds(start, LANES), :], sems.at[flip, n, b]
            )
            copy.start()
            leaving.append(copy)
    return leaving


def put_rest_kernel(layout, size, skip, which, place_ref, *refs):
    halves, targets, heads_out, done, boxes = refs[:16], refs[19:21], refs[21:24], refs[24], refs[25:27]
    whole, held, out_sems, head_out_sems = refs[27:]
    done[...] = jnp.zeros(done.shape, F32)
    chosen = [halves[2 * (GROUP * flip + k) + h] for flip, k in which for h in range(2)]
    leaving = put_halves(layout, size, which, place_ref, chosen, boxes, targets, out_sems)
    for flip in range(2):
        leaving += put_heads(
            size, skip, place_ref, flip, halves[8 * flip : 8 * flip + 8], whole, held, heads_out,
            head_out_sems,
        )
    for copy in leaving:
        copy.wait()


def put_pieces(layout, size, which, shapes, places, halves, flags, sofar, name):
    count, outs = len(which), len(layout)
    filled = [value for value in sofar if value is not None]
    kept = [n for n, value in enumerate(sofar) if value is not None]
    anywhere = pl.BlockSpec(memory_space=pl.ANY)
    before = 1 + 2 * count + len(flags)
    return pl.pallas_call(
        functools.partial(put_pieces_kernel, layout, size, which),
        in_specs=[pl.BlockSpec(memory_space=pltpu.SMEM)]
        + vmem(2 * count + len(flags))
        + [anywhere] * len(filled),
        out_specs=[anywhere] * outs + vmem(1),
        out_shape=[jax.ShapeDtypeStruct(shape, F32) for shape in shapes]
        + [jax.ShapeDtypeStruct((8, LANES), F32)],
        scratch_shapes=[
            pltpu.VMEM((count, GROUP * share, blocks * LANES), F32)
            for share, blocks, *_ in layout
        ]
        + [pltpu.SemaphoreType.DMA((count, outs))],
        input_output_aliases={before + i: n for i, n in enumerate(kept)},
        compiler_params=params(),
        cost_estimate=LIGHT,
        name=name,
    )(places, *halves, *flags, *filled)


PLAN = dict(
    project=(0, 0), q1=(2, 2), q2=(2, 2), q3=(2, 2), mult=(2, 2), d_active=(2, 2), kv0=(4, 4),
    kv1=(4, 4), kv2=(5, 5), kv3=(4, 4), cot1=(4, 8), cot2=(4, 8), cot3=(4, 8), norm_near=(4, 6),
    attend=(6, 6), ctx1=(8, 8), ctx2=(8, 8), ctx3=(8, 8), middle=(10, 10), a1=(12, 12), a2=(12, 12),
    a3=(12, 12), dc1=(12, 12), dc2=(12, 12), norm_far=(10, 10), layer_out=(13, 15), b1=(13, 15),
    b2=(13, 15), b3=(13, 15), first_grad=(14, 14), one_core=(14, 14), one_z1=(15, 15),
    attend_back=(12, 12), far=(14, 14), one_z2=(16, 16), second_grad=(16, 16), two_core=(17, 17),
    head_grad=(15, 15), head_core=(15, 15), head_x=(16, 16), head_y=(16, 16), head_d=(16, 16),
    head_sum=(17, 17), two_z1=(18, 18), one_near=(17, 18), two_z2=(20, 20), one_far=(20, 20),
    one_nx=(20, 20), one_ny=(20, 20), two_near=(22, 22), one_fx=(22, 22), one_fy=(22, 22),
    back_z1=(15, 18), two_far=(24, 24), two_nx=(24, 24), two_ny=(24, 24), one_nd=(25, 26),
    one_fd=(25, 26), back_z2=(24, 25), two_fx=(25, 26), two_fy=(25, 26), input_grad=(26, 26),
    tiny_core=(17, 18), two_nd=(27, 28), two_fd=(27, 28), tiny_x=(18, 18), tiny_y=(20, 20),
    tiny_z1=(22, 22), tiny_z2=(28, 30), one_all=(17, 18), put_own=(25, 25), put_rest=(28, 28),
    put_two=(32, 99), one_cn0=(22, 24), one_cf0=(26, 26), two_cn0=(28, 30), two_cf0=(28, 30),
    one_cn1=(22, 24), one_cf1=(26, 26), two_cn1=(28, 30), two_cf1=(28, 30), one_cn2=(22, 24),
    one_cf2=(26, 26), two_cn2=(28, 30), two_cf2=(28, 30), one_cn3=(27, 27), one_cf3=(27, 27),
    two_cn3=(28, 30), two_cf3=(30, 30), tiny_out=(30, 99),
)


class Name(str):
    def __getitem__(self, index):
        return Name(self + "." + str(index))

    def __call__(self, k):
        return Name(self + str(k))

    def __getattr__(self, part):
        return Name(self + "_" + part)


class Names:
    def __getattr__(self, name):
        return Name(name)


def free(name):
    return "!" + name


def run_steps(steps, known):
    stage, last = {}, {}

    def named(name):
        return [source.lstrip("!").partition(".")[0] for source in steps[name][0]]

    def settle(name):
        if name in stage:
            return stage[name]
        first, wait = PLAN[name]
        for source in named(name):
            if source in steps:
                first = max(first, settle(source))
        stage[name], last[name] = first, max(first, wait)
        return first

    for name in steps:
        settle(name)
    depth = {}

    def deep(name):
        if name not in depth:
            depth[name] = 1 + max([deep(s) for s in named(name) if s in steps], default=0)
        return depth[name]

    for name in steps:
        deep(name)
    made, now, waiting = dict(known), 0, []
    order = sorted(steps, key=lambda n: (stage[n], depth[n]))

    def pick(source):
        base, _, index = source.lstrip("!").partition(".")
        return (base, int(index)) if index else (base, None)

    def turn(following):
        ending = [n for n in waiting if last[n] < following]
        keys = set()
        for n in ending:
            many = isinstance(made[n], (list, tuple))
            if n.startswith(Names().put):
                keys.add((n, len(made[n]) - 1))
            elif many:
                keys.update((n, i) for i in range(len(made[n])))
            else:
                keys.add((n, None))
        for n in order:
            if stage[n] == following:
                keys.update(
                    pick(s) for s in steps[n][0] if not s.startswith("!") and pick(s)[0] in made
                )
        keys = sorted(keys, key=str)
        values = [made[n] if i is None else made[n][i] for n, i in keys]
        for (n, i), value in zip(keys, lax.optimization_barrier(values)):
            if i is None:
                made[n] = value
            else:
                made[n] = [value if j == i else old for j, old in enumerate(made[n])]
        return [n for n in waiting if n not in ending]

    for name in order:
        if now < stage[name]:
            waiting, now = turn(stage[name]), stage[name]
        sources, function = steps[name]
        inputs = []
        for source in sources:
            base, index = pick(source)
            inputs.append(made[base] if index is None else made[base][index])
        made[name] = function(*inputs)
        waiting.append(name)
    return made


def split_device(
    tokens,
    rand_blocks,
    w_query,
    w_key,
    w_value,
    w_out,
    w_up,
    w_down,
    bias_query,
    bias_value,
    bias_out,
    bias_up,
    bias_down,
    attn_gain,
    attn_shift,
    ffn_gain,
    ffn_shift,
    cotangent,
):
    _, local_len, width = tokens.shape
    fan = w_up.shape[1]
    blocks_all = rand_blocks.shape[0]
    position, item = lax.axis_index("seq"), lax.axis_index("item")
    chip, core = position // 2, position % 2
    heads = HEADS // GROUP
    part = heads * HD
    all_len = GROUP * local_len
    quarter, mid = fan // 8, width // 2
    early = LANES
    late = quarter - early
    places = jnp.stack([chip, item, core]).astype(jnp.int32)
    smem = [pl.BlockSpec(memory_space=pltpu.SMEM)]
    anywhere = [pl.BlockSpec(memory_space=pl.ANY)]
    shaped = jax.ShapeDtypeStruct

    first_rows = 2 * quarter + width + 2 * early
    second_rows = 2 * late + 2 * part + mid
    tiny_rows = (fan + 4 * width) // LANES
    size = 3 * part
    rows_one = (quarter * width + width * early) // LANES
    rows_two = (width * late + part * mid) // LANES
    rows_three = size * mid // LANES
    half_one, half_two = rows_one // 2, rows_two // 2

    def kernel(body, ins, outs, scratch=(), name=None):
        return pl.pallas_call(
            body,
            in_specs=ins,
            out_specs=vmem(len(outs)),
            out_shape=list(outs),
            scratch_shapes=list(scratch),
            compiler_params=params(),
            cost_estimate=LIGHT,
            name=name,
        )

    box = lambda *dims: pltpu.VMEM(dims, BF)
    box32 = lambda *dims: pltpu.VMEM(dims, F32)
    sems = lambda n: pltpu.SemaphoreType.DMA((n,))

    def project(x):
        return kernel(
            project_kernel,
            smem + vmem(1) + anywhere * 3 + vmem(4),
            [shaped((local_len, width), BF)] + [shaped((size, local_len), BF)] * 4,
            [box(3, width, width), box(3 * width, local_len), sems(3)],
            "project",
        )(places, x, w_query, w_key, w_value, bias_query, bias_value, attn_gain, attn_shift)

    def multiplicity(rand):
        return kernel(
            functools.partial(mult_kernel, heads, blocks_all),
            smem * 2,
            [shaped((heads, 2 * all_len // BLOCK, all_len), F32)],
            name="multiplicity",
        )(places, rand.reshape(-1))[0]

    def attend(*ins):
        return kernel(
            functools.partial(attend_kernel, heads),
            vmem(9),
            [shaped((part, local_len), BF)] * 4
            + [shaped((part, all_len), F32), shaped((heads, 1, all_len), F32)],
            name="attend",
        )(*ins)

    def middle_step(ctx0, ctx1, ctx2, ctx3, d_active, cot):
        outs = kernel(
            middle_kernel,
            smem + vmem(5) + anywhere + vmem(3) + anywhere + vmem(1) + anywhere + vmem(1),
            [shaped((first_rows, LANES), BF)] * 4
            + [shaped((second_rows, LANES), BF)] * 4
            + [shaped((2 * part, local_len), BF)] * 2
            + [
                shaped((local_len, width), F32),
                shaped((local_len, fan), BF),
                shaped((local_len, width), F32),
                shaped((tiny_rows, LANES), F32),
            ],
            [box(width, local_len), box(fan, local_len), box(fan, local_len)]
            + [box(width, local_len)] * 2
            + [box(width, width), box(width, fan), box32(local_len, fan)]
            + [sems(1 + 2 * (fan // width))],
            "middle",
        )(
            places, tokens[0], ctx0, ctx1, ctx2, ctx3, w_out, bias_out, ffn_gain, ffn_shift,
            w_up, bias_up, d_active, cot,
        )
        return outs

    def attend_back(*ins):
        return kernel(
            functools.partial(attend_back_kernel, heads),
            vmem(14),
            [
                shaped((part, all_len), BF),
                shaped((2 * part, all_len), F32),
                shaped((2 * part, all_len), BF),
            ],
            name="attend_back",
        )(*ins)

    def first_grad(*ins):
        return kernel(
            first_grad_kernel,
            smem + vmem(8),
            [shaped((rows_one, LANES), F32), shaped((rows_one, LANES), BF)],
            [
                box(2 * quarter, all_len),
                box(all_len, width),
                box(width, all_len),
                box(all_len, 2 * early),
            ],
            "first_grad",
        )(places, *ins)

    def second_grad(*ins):
        return kernel(
            second_grad_kernel,
            smem + vmem(8),
            [shaped((rows_two, LANES), F32), shaped((rows_two, LANES), BF)],
            [
                box(width, all_len),
                box(all_len, 2 * late),
                box(2 * part, all_len),
                box(all_len, mid),
            ],
            "second_grad",
        )(places, *ins)

    def head_grad(*ins):
        return kernel(
            head_grad_kernel,
            smem + vmem(7) + anywhere * 3,
            [shaped((2 * size, local_len), BF)] * 2
            + [shaped((rows_three, LANES), F32), shaped((rows_three, LANES), BF)]
            + [shaped((4 * width // LANES, LANES), F32)],
            [
                box(size, all_len),
                box(all_len, width),
                box32(size, width),
                box(3, part + HD, all_len),
                box(3, width, part + HD),
                sems(3),
            ],
            "head_grad",
        )(places, *ins, attn_gain, attn_shift, w_query, w_key, w_value)

    def input_grad(own, came, far, d_middle):
        return kernel(
            input_grad_kernel,
            smem + vmem(3) + anywhere * 3 + vmem(3),
            [shaped((local_len, width), BF)],
            [box(3, width, width), box(3 * width, local_len), sems(3)],
            "input_grad",
        )(
            places, own, came, far, w_query, w_key, w_value, tokens[0], d_middle, attn_gain
        )[0]

    layout_one = (
        (quarter // GROUP, width // LANES, 0, None, 0, 0),
        (width // GROUP, early // LANES, None, 0, quarter, 0),
    )
    layout_two = (
        (width // GROUP, late // LANES, None, 0, quarter, early),
        (part // GROUP, mid // LANES, 1, 2, mid, 0),
    )
    size_one, size_two = (rows_one + rows_three) // GROUP, rows_two // GROUP
    shapes_one, shapes_two = ((fan, width), (width, fan)), ((width, fan), (width, width))

    own_three = tuple((0, k) for k in range(3))
    the_rest = ((0, 3), *((1, k) for k in range(GROUP)))
    every = tuple((flip, k) for flip in range(2) for k in range(GROUP))

    def put_own(*halves):
        return put_pieces(
            layout_one, size_one, own_three, shapes_one, places, halves, (), (None, None), "put_own"
        )

    def put_rest(*ins):
        skip = rows_one // GROUP
        return pl.pallas_call(
            functools.partial(put_rest_kernel, layout_one, size_one, skip, the_rest),
            in_specs=smem + vmem(17) + anywhere * 2,
            out_specs=anywhere * 5 + vmem(1),
            out_shape=[shaped(shape, F32) for shape in shapes_one]
            + [shaped((width, width), F32)] * 3
            + [shaped((8, LANES), F32)],
            scratch_shapes=[
                box32(len(the_rest), GROUP * share, blocks * LANES)
                for share, blocks, *_ in layout_one
            ]
            + [
                box(2, 3 * width, mid),
                box32(2, 3, mid // LANES, LANES, width),
                pltpu.SemaphoreType.DMA((len(the_rest), 2)),
                pltpu.SemaphoreType.DMA((2, 3, mid // LANES)),
            ],
            input_output_aliases={18: 0, 19: 1},
            compiler_params=params(),
            cost_estimate=LIGHT,
            name="put_rest",
        )(places, *ins)

    def put_two(*ins):
        return put_pieces(
            layout_two, size_two, every, shapes_two, places, ins[:16], ins[16:17], (ins[17], None),
            "put_two",
        )

    def rows_of(grad_t, k):
        blocks = grad_t.reshape(GROUP, rows_three // GROUP, LANES)
        return lax.dynamic_index_in_dim(blocks, item ^ k, 0, False)

    def head_sum(grad_t, x, y, d):
        total = rows_of(grad_t, 0) + x.astype(F32) + (y.astype(F32) + d.astype(F32))
        return total.astype(BF)

    def last_sum(pair, far):
        share = pair.shape[0] // 2
        return (pair[:share] + far.astype(F32)).astype(BF)

    def second_half(pair):
        return pair[pair.shape[0] // 2 :].astype(BF)

    below = lambda *parts: jnp.concatenate(parts, axis=0)
    cot = cotangent[0]
    n, todo = Names(), {}
    todo[n.project] = ((n.tokens,), project)
    todo[n.mult] = ((n.rand,), multiplicity)
    todo[n.d_active] = ((n.cot,), lambda c: dense_back(c, w_down))
    for k in range(1, GROUP):
        todo[n.q(k)] = ((n.project[k + 1],), functools.partial(over_z, step=k))
        todo[n.cot(k)] = ((n.cot,), functools.partial(over_item, step=k))
        todo[n.ctx(k)] = ((n.attend[k],), functools.partial(over_z, step=k))
    own = [n.project[1], n.q1, n.q2, n.q3]
    for k in range(GROUP):
        todo[n.kv(k)] = ((own[k],), lambda v: over_core(v[part:]))
    other = [n.kv(k) for k in range(GROUP)]
    todo[n.attend] = ((*own, *other, n.mult), attend)
    todo[n.norm_near] = ((n.project[0],), lambda v: below(v, over_z(v, 2)))
    todo[n.norm_far] = ((n.norm_near,), lambda v: over_z(v, 1))
    todo[n.middle] = ((n.attend[0], n.ctx1, n.ctx2, n.ctx3, n.d_active, n.cot), middle_step)
    todo[n.layer_out] = (
        (n.middle[10], n.middle[11]),
        lambda m, a: (m + dense_rows(a, w_down) + bias_down).astype(BF),
    )
    for k in range(1, GROUP):
        todo[n.a(k)] = ((n.middle[k],), functools.partial(over_item, step=k))
        todo[n.b(k)] = ((n.middle[4 + k],), functools.partial(over_item, step=k))
    todo[n.dc1] = ((n.middle[9],), lambda v: over_z(v, 1))
    todo[n.dc2] = ((n.middle[8], n.dc1), lambda v, c: over_z(below(v[part:], c[part:]), 2))
    firsts = [n.middle[0], n.a1, n.a2, n.a3]
    seconds = [n.middle[4], n.b1, n.b2, n.b3]
    todo[n.first_grad] = ((*firsts, n.cot, n.cot1, n.cot2, n.cot3), first_grad)
    def pair_up(half, kept, given):
        far = over_z((kept[half:] + given[half:].astype(F32)).astype(BF), 1)
        return kept[:half] + given[:half].astype(F32) + far.astype(F32)

    todo[n.one_core] = ((n.first_grad[1],), over_core)
    todo[n.one_z1] = (
        (n.first_grad[0], n.one_core),
        functools.partial(pair_up, half_one),
    )
    todo[n.one_z2] = ((n.one_z1,), lambda v: last_sum(v, over_z(second_half(v), 2)))
    todo[n.attend_back] = (
        (*own, *other, n.mult, n.attend[4], n.attend[5], n.middle[8], n.dc1, n.dc2),
        attend_back,
    )
    todo[n.far] = ((n.attend_back[2],), over_core)
    todo[n.second_grad] = ((*firsts, *seconds), second_grad)
    todo[n.two_core] = ((n.second_grad[1],), over_core)
    todo[n.two_z1] = (
        (n.second_grad[0], n.two_core),
        functools.partial(pair_up, half_two),
    )
    todo[n.head_grad] = (
        (n.attend_back[0], n.attend_back[1], n.far, n.norm_near, n.norm_far),
        head_grad,
    )
    todo[n.head_core] = ((n.head_grad[2], n.head_grad[3]), lambda k, g: k + over_core(g).astype(F32))
    for k, name in enumerate((n.head_x, n.head_y, n.head_d)):
        todo[name] = (
            (n.head_core,),
            lambda v, k=k + 1: over_item(rows_of(v, k).astype(BF), k),
        )
    todo[n.head_sum] = ((n.head_core, n.head_x, n.head_y, n.head_d), head_sum)
    todo[n.two_z2] = ((n.two_z1,), lambda v: last_sum(v, over_z(second_half(v), 2)))
    todo[n.one_all] = ((n.one_z2, n.head_sum), below)
    pieces = []
    for name, total in ((n.one, n.one_all), (n.two, n.two_z2)):
        todo[name.near] = ((total,), lambda v: below(v, over_z(v, 2)))
        todo[name.far] = ((name.near,), lambda v: over_z(v, 1))
        todo[name.nx] = ((name.near,), lambda v: over_item(v, 1))
        todo[name.ny] = ((name.near,), lambda v: over_item(v, 2))
        todo[name.fx] = ((name.far,), lambda v: over_item(v, 1))
        todo[name.fy] = ((name.far,), lambda v: over_item(v, 2))
        todo[name.nd] = ((name.nx,), lambda v: over_item(v, 2))
        todo[name.fd] = ((name.fy,), lambda v: over_item(v, 1))
        nears, fars = (name.near, name.nx, name.ny, name.nd), (name.far, name.fx, name.fy, name.fd)
        flat, mirrored = [], []
        for k, halves in enumerate(zip(nears, fars)):
            for half, crossed in zip(halves, (name.cn(k), name.cf(k))):
                todo[crossed] = ((half,), over_core)
                flat.append(half)
                mirrored.append(crossed)
        pieces.append((flat, mirrored))
    own_one, mirrored_one = pieces[0]
    todo[n.put_own] = (tuple(own_one[:6]), put_own)
    todo[n.put_rest] = (
        (*own_one, *mirrored_one, n.put_own[2], free(n.put_own[0]), free(n.put_own[1])),
        put_rest,
    )
    todo[n.put_two] = (
        (*pieces[1][0], *pieces[1][1], n.put_rest[5], free(n.put_rest[1])),
        put_two,
    )
    todo[n.back_z1] = ((n.head_grad[1],), lambda v: over_z(v, 1))
    todo[n.back_z2] = (
        (n.head_grad[0], n.back_z1),
        lambda v, c: over_z(below(v[size:], c[size:]), 2),
    )
    todo[n.input_grad] = (
        (n.head_grad[0], n.back_z1, n.back_z2, n.middle[12]),
        input_grad,
    )
    todo[n.tiny_core] = (
        (n.middle[13], n.head_grad[4]),
        lambda u, v: below(u, v) + over_core(below(u, v)),
    )
    todo[n.tiny_x] = ((n.tiny_core,), lambda v: v + over_item(v, 1))
    todo[n.tiny_y] = ((n.tiny_x,), lambda v: v + over_item(v, 2))
    todo[n.tiny_z1] = ((n.tiny_y,), lambda v: v + over_z(v, 1))
    todo[n.tiny_z2] = ((n.tiny_z1,), lambda v: v + over_z(v, 2))
    def tiny_out(v):
        flat, cuts, at = v.reshape(-1), [], 0
        for length in (fan,) + (width,) * 8:
            cuts.append(flat[at : at + length])
            at += length
        return cuts

    todo[n.tiny_out] = ((n.tiny_z2,), tiny_out)
    made = run_steps(
        todo, {n.tokens: tokens[0], n.rand: rand_blocks, n.cot: cot}
    )
    layer_out, grad_tokens = made[n.layer_out], made[n.input_grad]
    grad_down, grad_qkv = made[n.put_rest][0], made[n.put_rest][2:5]
    grad_up, grad_out, _ = made[n.put_two]
    g_bu, g_fg, g_fs, g_bd, g_bo, g_ag, g_as, g_bq, g_bv = made[n.tiny_out]
    return (
        layer_out[None],
        grad_tokens[None],
        grad_qkv[0],
        grad_qkv[1],
        grad_qkv[2],
        grad_out,
        grad_up,
        grad_down,
        g_bq,
        g_bv,
        g_bo,
        g_bu,
        g_bd,
        g_ag,
        g_as,
        g_fg,
        g_fs,
    )


def per_device(tokens, rand_blocks, *rest):
    seqs, local_len, width = tokens.shape
    fan = rest[4].shape[1]
    fits = (
        seqs == 1
        and local_len == LANES
        and lax.axis_size("item") == GROUP
        and lax.axis_size("seq") == 2 * GROUP
        and HEADS % GROUP == 0
        and width == HEADS * HD
        and fan % (8 * LANES) == 0
        and width % (2 * LANES) == 0
    )
    chosen = split_device if fits else general_device
    return chosen(tokens, rand_blocks, *rest)


def solution(mesh):
    placed = (
        P("item", "seq", None),
        P(None, "item", None, None),
        P(),
        P(),
        P(),
        P(),
        P(),
        P(),
        P(),
        P(),
        P(),
        P(),
        P(),
        P(),
        P(),
        P(),
        P(),
        P("item", "seq", None),
    )
    return jax.shard_map(
        per_device,
        mesh=mesh,
        in_specs=placed,
        out_specs=(
            P("item", "seq", None),
            P("item", "seq", None),
            P(),
            P(),
            P(),
            P(),
            P(),
            P(),
            P(),
            P(),
            P(),
            P(),
            P(),
            P(),
            P(),
            P(),
            P(),
        ),
        check_vma=False,
    )
```
